32 devices in a mesh: mix: 4 (over z), fsdp: 4 (over y, x), tile: 2 (over core).
Axes of the slice: x: 2, y: 2, z: 4, core: 2. Of those that a mesh axis runs over, the one named last changes fastest.
Arguments:
- video: bfloat16 [16, 8, 8, 8, 256], P(('mix', 'fsdp'), 'tile'), parts along dimension 0
- conv_weight: bfloat16 [1024, 6912], P(('mix', 'fsdp')), parts along dimension 0, may hold values from -0.078125 to 0.078125
- down_weight: bfloat16 [1024, 2304], P(('mix', 'fsdp')), parts along dimension 0, may hold values from -0.125 to 0.125
- out_grad: bfloat16 [16, 8, 4, 4, 256], P(('mix', 'fsdp'), 'tile'), parts along dimension 0, may hold values from -6 to 6
- clip_bucket: int32 [16], P(('mix', 'fsdp')), parts along dimension 0, may hold values from 0 to 3
- start_frame: int32 [16], P(('mix', 'fsdp')), parts along dimension 0, may hold values from 0 to 4
- bucket_res: int32 [4, 2], replicated, may hold values from 4 to 8, as said below
Outputs:
- down: bfloat16 [16, 8, 4, 4, 256], P(('mix', 'fsdp'), 'tile'), parts along dimension 0
- video_grad: bfloat16 [16, 8, 8, 8, 256], P(('mix', 'fsdp'), 'tile'), parts along dimension 0
- conv_weight_grad: float32 [1024, 6912], P(('mix', 'fsdp')), parts along dimension 0
- down_weight_grad: float32 [1024, 2304], P(('mix', 'fsdp')), parts along dimension 0
The draws below stay inside these ranges and needn't reach their ends.
There are 4 independent parts, one for each index of `mix`. The reference program is written for one: setup_inputs(seed, part) draws one part's arguments, and reference() takes and returns one part's arrays. A program takes and returns all parts, laid end to end along the dimension named above; an argument that names none is the same for every part. Nothing has to cross between parts.
Inputs may be any that keep to these rules, and one draw needn't show every extreme that they name: `start_frame`: frames before it are padding. `bucket_res`: valid rows (column 0) and columns (column 1) per bucket; no two buckets have the same pair.
All inputs are finite; a program needn't handle non-finite values.
Results may differ from the reference program's by a relative error of at most 0.0051.
Values may be sent and summed in bfloat16 or wider, within the bound.
A program may use at most 128 MiB of HBM per device.

```python
import jax
import jax.numpy as jnp
from jax import lax

CHANNELS = 256
GROUPS = 32
SIDE = 8
BUCKETS = 4
CLIPS = 4
FRAMES = 8


def draw_video(key, part):
    noise_key = jax.random.fold_in(key, 11)
    channel_key = jax.random.fold_in(key, 12)
    full_shape = (CLIPS, FRAMES, SIDE, SIDE, CHANNELS)
    frame_pos = jnp.arange(FRAMES, dtype=jnp.float32) / max(FRAMES - 1, 1)
    channel_scale = jnp.exp(jax.random.uniform(channel_key, (CHANNELS,), jnp.float32, jnp.log(0.3), jnp.log(3.0)))
    noise = jnp.clip(jax.random.normal(noise_key, full_shape, jnp.float32), -5.0, 5.0)
    growth = 1.0 + 2.0 * frame_pos
    return (noise * growth[None, :, None, None, None] * channel_scale).astype(jnp.bfloat16)


def draw_bucket_res(key, part):
    order_key = jax.random.fold_in(key, 21)
    ranks = jax.random.permutation(order_key, jnp.arange(BUCKETS, dtype=jnp.int32))
    half_side = SIDE // 2
    rows = SIDE - ranks * half_side // (BUCKETS - 1)
    cols = SIDE - (BUCKETS - 1 - ranks) * half_side // (BUCKETS - 1)
    return jnp.stack([rows, cols], axis=1).astype(jnp.int32)


def plant(drawn, stream_key, smallest, high):
    shape = drawn.shape
    spot = [jax.random.randint(jax.random.fold_in(stream_key, axis), (), 0, shape[axis]) for axis in range(len(shape))]
    drawn = drawn.at[tuple(spot)].set(smallest)
    longest = shape.index(max(shape))
    spot[longest] = (spot[longest] + 1) % shape[longest]
    return drawn.at[tuple(spot)].set(high)


def with_spikes(array, key, source, target, blocks, factor):
    def block_of(dim):
        return (jnp.arange(array.shape[dim]) // (array.shape[dim] // blocks)).reshape((-1,) + (1,) * (array.ndim - 1 - dim))

    one_side = jax.random.permutation(key, blocks)[block_of(target)]
    far = (block_of(target) + blocks // 2) % blocks
    return jnp.where((block_of(source) == one_side) | (block_of(source) == far), factor * array, array)


def block_levels(stream_key, shape, cuts, least, high):
    factor_of = 1.0
    for dim, blocks in cuts:
        draws = jax.random.uniform(jax.random.fold_in(jax.random.fold_in(stream_key, 6), dim), (blocks,), jnp.float32, least / len(cuts), high / len(cuts))
        factor_of = factor_of * jnp.repeat(jnp.exp(draws), shape[dim] // blocks).reshape((-1,) + (1,) * (len(shape) - 1 - dim))
    return factor_of


def scatter_about(own_key, extent, width, reach, shards=(), held_as=jnp.bfloat16):
    drawn = width * jax.random.normal(own_key, extent, jnp.float32)
    if shards:
        drawn = drawn * block_levels(own_key, extent, shards, -0.22, 0.18)
    return jnp.clip(drawn, -reach, reach).astype(held_as)


def bell_draw_with(rng, dims, scale, reach, split, heavy, kind=jnp.bfloat16):
    array = scale * jax.random.normal(rng, dims, jnp.float32)
    if split:
        array = array * block_levels(rng, dims, split, -0.22, 0.18)
    return jnp.clip(with_spikes(array, jax.random.fold_in(rng, 3), *heavy), -reach, reach).astype(kind)


def setup_inputs(seed: int = 0, part: int = 0) -> dict:
    key_list = jax.random.split(jax.random.key(seed), 8)
    own_keys = jax.random.split(jax.random.fold_in(key_list[7], part), 8)
    video = draw_video(jax.random.fold_in(jax.random.fold_in(key_list[7], part), 71), part)
    conv_weight = scatter_about(own_keys[1], (CHANNELS, 27 * CHANNELS), (27 * CHANNELS) ** -0.5, 0.078125, ((0, 4),))
    down_weight = scatter_about(own_keys[2], (CHANNELS, 9 * CHANNELS), (9 * CHANNELS) ** -0.5, 0.125, ((0, 4),))
    out_grad = bell_draw_with(own_keys[3], (CLIPS, FRAMES, SIDE // 2, SIDE // 2, CHANNELS), 1.0, 6.0, ((0, 4), (1, 2)), (1, 4, 2, 2.0))
    clip_bucket = plant(jax.random.randint(own_keys[4], (CLIPS,), 0, BUCKETS), jax.random.fold_in(own_keys[4], 1), 0, BUCKETS - 1).astype(jnp.int32)
    start_frame = plant(jax.random.randint(own_keys[5], (CLIPS,), 0, FRAMES // 2 + 1), jax.random.fold_in(own_keys[5], 1), 0, (FRAMES // 2 + 1) - 1).astype(jnp.int32)
    bucket_res = draw_bucket_res(jax.random.fold_in(key_list[7], 71), part)
    return dict(video=video, conv_weight=conv_weight, down_weight=down_weight, out_grad=out_grad, clip_bucket=clip_bucket, start_frame=start_frame, bucket_res=bucket_res)


EPSILON = 1e-06

def tap_window(padded, tap_index, out_frames, side_cells, flipped):
    tap_time = tap_index // 9
    tap_row = tap_index // 3 % 3
    tap_col = tap_index % 3
    if flipped:
        tap_time, tap_row, tap_col = (2 - tap_time, 2 - tap_row, 2 - tap_col)
    window = padded[:, tap_time:tap_time + out_frames, tap_row:tap_row + side_cells, tap_col:tap_col + side_cells, :]
    return window.reshape(-1, padded.shape[-1])

def reference(video, conv_weight, down_weight, out_grad, clip_bucket, start_frame, bucket_res):
    channel_count = video.shape[-1]
    group_width = channel_count // GROUPS
    half_side = SIDE // 2
    limits = bucket_res[clip_bucket]
    frame_ids = jnp.arange(FRAMES, dtype=jnp.int32)
    positions = jnp.arange(SIDE, dtype=jnp.int32)
    in_time = frame_ids[None, :] >= start_frame[:, None]
    in_rows = positions[None, :] < limits[:, 0:1]
    in_cols = positions[None, :] < limits[:, 1:2]
    inside = in_time[:, :, None, None] & in_rows[:, None, :, None] & in_cols[:, None, None, :]
    mask = inside.astype(jnp.float32)[..., None]
    valid_count = lax.optimization_barrier(jnp.sum(mask, axis=(1, 2, 3, 4))) * group_width
    grouped_shape = (CLIPS, FRAMES, SIDE, SIDE, GROUPS, group_width)
    summed_axes = (1, 2, 3, 5)
    cell_weight = mask[..., None]
    grouped = video.astype(jnp.float32).reshape(grouped_shape)
    centre = lax.optimization_barrier(jnp.sum(grouped * cell_weight, axis=summed_axes)) / valid_count[:, None]
    offset = grouped - centre[:, None, None, None, :, None]
    spread = lax.optimization_barrier(jnp.sum(cell_weight * offset * offset, axis=summed_axes)) / valid_count[:, None]
    inverse = lax.rsqrt(spread + EPSILON)
    normed_grouped = offset * inverse[:, None, None, None, :, None]
    normed = normed_grouped.reshape(video.shape)
    hidden = (mask * jax.nn.silu(normed)).astype(jnp.bfloat16)
    padded = jnp.pad(hidden, ((0, 0), (2, 0), (1, 1), (1, 1), (0, 0)))
    conv_out = jnp.zeros((CLIPS * FRAMES * SIDE * SIDE, channel_count), jnp.float32)
    for tap_index in range(27):
        window = tap_window(padded, tap_index, FRAMES, SIDE, False)
        panel = conv_weight[:, tap_index * channel_count:(tap_index + 1) * channel_count]
        conv_out = conv_out + lax.dot_general(window, panel, (((1,), (1,)), ((), ())), preferred_element_type=jnp.float32)
    residual = (mask * (video.astype(jnp.float32) + conv_out.reshape(video.shape))).astype(jnp.bfloat16)
    down_padded = jnp.pad(residual, ((0, 0), (0, 0), (0, 1), (0, 1), (0, 0)))
    grad_flat = out_grad.reshape(-1, channel_count)
    down_out = jnp.zeros((CLIPS * FRAMES * half_side * half_side, channel_count), jnp.float32)
    spread_back = jnp.zeros((CLIPS, FRAMES, SIDE + 1, SIDE + 1, channel_count), jnp.float32)
    down_terms = []
    for tap_row in range(3):
        for tap_col in range(3):
            tap_index = tap_row * 3 + tap_col
            panel = down_weight[:, tap_index * channel_count:(tap_index + 1) * channel_count]
            window = down_padded[:, :, tap_row:tap_row + SIDE:2, tap_col:tap_col + SIDE:2, :].reshape(-1, channel_count)
            down_out = down_out + lax.dot_general(window, panel, (((1,), (1,)), ((), ())), preferred_element_type=jnp.float32)
            term = jnp.dot(grad_flat, panel, preferred_element_type=jnp.float32)
            spread_back = spread_back.at[:, :, tap_row:tap_row + SIDE:2, tap_col:tap_col + SIDE:2, :].add(term.reshape(CLIPS, FRAMES, half_side, half_side, channel_count))
            down_terms.append(lax.dot_general(grad_flat, window, (((0,), (0,)), ((), ())), preferred_element_type=jnp.float32))
    down = down_out.reshape(CLIPS, FRAMES, half_side, half_side, channel_count).astype(jnp.bfloat16)
    down_weight_grad = jnp.concatenate(down_terms, axis=1)
    res_grad = (mask * spread_back[:, :, :SIDE, :SIDE, :]).astype(jnp.bfloat16)
    res_flat = res_grad.reshape(-1, channel_count)
    grad_padded = jnp.pad(res_grad, ((0, 0), (0, 2), (1, 1), (1, 1), (0, 0)))
    back_hidden = jnp.zeros((CLIPS * FRAMES * SIDE * SIDE, channel_count), jnp.float32)
    conv_terms = []
    for tap_index in range(27):
        panel = conv_weight[:, tap_index * channel_count:(tap_index + 1) * channel_count]
        window = tap_window(padded, tap_index, FRAMES, SIDE, False)
        conv_terms.append(lax.dot_general(res_flat, window, (((0,), (0,)), ((), ())), preferred_element_type=jnp.float32))
        flipped_window = tap_window(grad_padded, tap_index, FRAMES, SIDE, True)
        back_hidden = back_hidden + jnp.dot(flipped_window, panel, preferred_element_type=jnp.float32)
    conv_weight_grad = jnp.concatenate(conv_terms, axis=1)
    gate_value = jax.nn.sigmoid(normed)
    pushed = mask * back_hidden.reshape(video.shape) * gate_value * (1.0 + normed * (1.0 - gate_value))
    pushed_grouped = pushed.reshape(grouped_shape)
    mean_push = lax.optimization_barrier(jnp.sum(pushed_grouped, axis=summed_axes)) / valid_count[:, None]
    mean_pair = lax.optimization_barrier(jnp.sum(pushed_grouped * normed_grouped, axis=summed_axes)) / valid_count[:, None]
    through_norm = inverse[:, None, None, None, :, None] * (pushed_grouped - mean_push[:, None, None, None, :, None] - normed_grouped * mean_pair[:, None, None, None, :, None])
    video_grad = (mask * through_norm.reshape(video.shape) + res_grad.astype(jnp.float32)).astype(jnp.bfloat16)
    return (down, video_grad, conv_weight_grad, down_weight_grad)
```

```python
import functools

import jax
import jax.numpy as jnp
import numpy as np
from jax import lax
from jax.experimental import pallas as pl
from jax.experimental.pallas import tpu as pltpu
from jax.sharding import PartitionSpec as P

GROUPS = 32


EPSILON = 1e-06


def shifted(block, axis, distance):
    devices = range(lax.axis_size(axis))
    route = [(i - distance, i) for i in devices if i - distance in devices]
    return lax.ppermute(block, axis, route)


def valid_mask(clip_bucket, start_frame, bucket_res, first_frame, frame_count, side_cells):
    bucket_ids = jnp.arange(bucket_res.shape[0], dtype=jnp.int32)
    picked = (clip_bucket[:, None] == bucket_ids[None, :]).astype(jnp.int32)
    limits = jnp.sum(picked[:, :, None] * bucket_res[None, :, :], axis=1)
    frame_ids = first_frame + jnp.arange(frame_count, dtype=jnp.int32)
    positions = jnp.arange(side_cells, dtype=jnp.int32)
    in_time = frame_ids[None, :] >= start_frame[:, None]
    in_rows = positions[None, :] < limits[:, 0:1]
    in_cols = positions[None, :] < limits[:, 1:2]
    inside = in_time[:, :, None, None] & in_rows[:, None, :, None] & in_cols[:, None, None, :]
    return (inside.astype(jnp.float32)[..., None], limits)


def time_group(padded, tap_time, out_frames, side_cells, flipped):
    channel_count = padded.shape[-1]
    time_start = 2 - tap_time if flipped else tap_time
    layers = []
    for tap_row in range(3):
        for tap_col in range(3):
            row_start = 2 - tap_row if flipped else tap_row
            col_start = 2 - tap_col if flipped else tap_col
            window = padded[
                :,
                time_start : time_start + out_frames,
                row_start : row_start + side_cells,
                col_start : col_start + side_cells,
                :,
            ]
            layers.append(window.reshape(-1, channel_count))
    return jnp.stack(layers)


def stride_taps(padded, side_cells):
    channel_count = padded.shape[-1]
    layers = []
    for tap_row in range(3):
        for tap_col in range(3):
            window = padded[
                :, :, tap_row : tap_row + side_cells : 2, tap_col : tap_col + side_cells : 2, :
            ]
            layers.append(window.reshape(-1, channel_count))
    return jnp.stack(layers)


def weight_terms(grad_rows, slabs, cot_rows, hidden_padded, frame_count, side_cells):
    out_rows = grad_rows.shape[1]
    down_term = lax.dot_general(
        grad_rows, slabs, (((0,), (1,)), ((), ())), preferred_element_type=jnp.float32
    ).reshape(out_rows, -1)
    conv_parts = []
    for tap_time in range(3):
        group = time_group(hidden_padded, tap_time, frame_count, side_cells, False)
        conv_parts.append(
            lax.dot_general(
                cot_rows, group, (((0,), (1,)), ((), ())), preferred_element_type=jnp.float32
            )
        )
    conv_term = jnp.concatenate(conv_parts, axis=1).reshape(out_rows, -1)
    return (conv_term, down_term)


def transpose_conv(grad_padded, conv_weight, out_frames, side_cells):
    channel_count = grad_padded.shape[-1]
    row_total = grad_padded.shape[0] * out_frames * side_cells * side_cells
    initial = jnp.zeros((row_total, channel_count), jnp.float32)
    running = initial
    weight_panel = lax.all_gather(conv_weight, "fsdp", axis=0, tiled=True)
    panel_rows = weight_panel.shape[0]
    panel = weight_panel.reshape(panel_rows, 27, channel_count)
    for tap_time in range(3):
        group = time_group(grad_padded, tap_time, out_frames, side_cells, True)
        running = running + lax.dot_general(
            group,
            panel[:, 9 * tap_time : 9 * tap_time + 9, :],
            (((0, 2), (1, 0)), ((), ())),
            preferred_element_type=jnp.float32,
        )
    return running


def shards(video, conv_weight, down_weight, out_grad, clip_bucket, start_frame, bucket_res):
    clip_count, frame_count, side_cells, side_again, channel_count = video.shape
    half_side = side_cells // 2
    group_width = channel_count // GROUPS
    tiles = lax.axis_size("tile")
    mask, limits = valid_mask(
        clip_bucket,
        start_frame,
        bucket_res,
        lax.axis_index("tile") * frame_count,
        frame_count,
        side_cells,
    )
    valid_count = (
        (frame_count * tiles - start_frame) * limits[:, 0] * limits[:, 1] * group_width
    ).astype(jnp.float32)
    grouped_shape = (clip_count, frame_count, side_cells, side_cells, GROUPS, group_width)
    summed_axes = (1, 2, 3, 5)
    cell_weight = mask[..., None]
    grouped = video.astype(jnp.float32).reshape(grouped_shape)
    first_sum = lax.psum(jnp.sum(grouped * cell_weight, axis=summed_axes), "tile")
    centre = first_sum / valid_count[:, None]
    offset = grouped - centre[:, None, None, None, :, None]
    second_sum = lax.psum(jnp.sum(cell_weight * offset * offset, axis=summed_axes), "tile")
    spread = second_sum / valid_count[:, None]
    inverse = lax.rsqrt(spread + EPSILON)
    normed_grouped = offset * inverse[:, None, None, None, :, None]
    normed = normed_grouped.reshape(video.shape)
    hidden = (mask * jax.nn.silu(normed)).astype(jnp.bfloat16)
    past = shifted(hidden[:, frame_count - 2 :], "tile", 1)
    hidden_padded = jnp.pad(
        jnp.concatenate([past, hidden], axis=1), ((0, 0), (0, 0), (1, 1), (1, 1), (0, 0))
    )

    def conv_columns(weight_panel):
        panel = weight_panel.reshape(weight_panel.shape[0], 27, channel_count)
        summed = None
        for tap_time in range(3):
            group = time_group(hidden_padded, tap_time, frame_count, side_cells, False)
            term = lax.dot_general(
                group,
                panel[:, 9 * tap_time : 9 * tap_time + 9, :],
                (((0, 2), (1, 2)), ((), ())),
                preferred_element_type=jnp.float32,
            )
            summed = term if summed is None else summed + term
        return summed

    conv_out = conv_columns(lax.all_gather(conv_weight, "fsdp", axis=0, tiled=True))
    residual = (mask * (video.astype(jnp.float32) + conv_out.reshape(video.shape))).astype(
        jnp.bfloat16
    )
    down_slabs = stride_taps(
        jnp.pad(residual, ((0, 0), (0, 0), (0, 1), (0, 1), (0, 0))), side_cells
    )
    weight_panel = lax.all_gather(down_weight, "fsdp", axis=0, tiled=True)
    panel = weight_panel.reshape(weight_panel.shape[0], 9, channel_count)
    down_out = lax.dot_general(
        down_slabs, panel, (((0, 2), (1, 2)), ((), ())), preferred_element_type=jnp.float32
    )
    down = down_out.astype(jnp.bfloat16).reshape(
        clip_count, frame_count, half_side, half_side, channel_count
    )
    grad_flat = out_grad.reshape(-1, channel_count)
    weight_panel = lax.all_gather(down_weight, "fsdp", axis=0, tiled=True)
    panel_rows = weight_panel.shape[0]
    panel = weight_panel.reshape(panel_rows, 9, channel_count)
    tap_grads = lax.dot_general(
        grad_flat, panel, (((1,), (0,)), ((), ())), preferred_element_type=jnp.float32
    )
    spread_back = jnp.zeros(
        (clip_count, frame_count, side_cells + 1, side_cells + 1, channel_count), jnp.float32
    )
    for tap_row in range(3):
        for tap_col in range(3):
            term = tap_grads[:, tap_row * 3 + tap_col, :].reshape(
                clip_count, frame_count, half_side, half_side, channel_count
            )
            spread_back = spread_back.at[
                :, :, tap_row : tap_row + side_cells : 2, tap_col : tap_col + side_cells : 2, :
            ].add(term)
    res_grad = (mask * spread_back[:, :, :side_cells, :side_cells, :]).astype(jnp.bfloat16)
    res_flat = res_grad.reshape(-1, channel_count)
    later = shifted(res_grad[:, :2], "tile", -1)
    grad_padded = jnp.pad(
        jnp.concatenate([res_grad, later], axis=1), ((0, 0), (0, 0), (1, 1), (1, 1), (0, 0))
    )
    back_hidden = transpose_conv(grad_padded, conv_weight, frame_count, side_cells).reshape(
        video.shape
    )
    gate_value = jax.nn.sigmoid(normed)
    pushed = mask * back_hidden * gate_value * (1.0 + normed * (1.0 - gate_value))
    pushed_grouped = pushed.reshape(grouped_shape)
    push_sum, pair_sum = lax.psum(
        (
            jnp.sum(pushed_grouped, axis=summed_axes),
            jnp.sum(pushed_grouped * normed_grouped, axis=summed_axes),
        ),
        "tile",
    )
    mean_push = push_sum / valid_count[:, None]
    mean_pair = pair_sum / valid_count[:, None]
    through_norm = inverse[:, None, None, None, :, None] * (
        pushed_grouped
        - mean_push[:, None, None, None, :, None]
        - normed_grouped * mean_pair[:, None, None, None, :, None]
    )
    video_grad = (mask * through_norm.reshape(video.shape) + res_grad.astype(jnp.float32)).astype(
        jnp.bfloat16
    )
    conv_term, down_term = weight_terms(
        grad_flat, down_slabs, res_flat, hidden_padded, frame_count, side_cells
    )
    conv_share, down_share = (
        lax.psum_scatter(conv_term, ("fsdp", "tile"), scatter_dimension=0, tiled=True),
        lax.psum_scatter(down_term, ("fsdp", "tile"), scatter_dimension=0, tiled=True),
    )
    conv_weight_grad, down_weight_grad = (
        lax.all_gather(conv_share, "tile", axis=0, tiled=True),
        lax.all_gather(down_share, "tile", axis=0, tiled=True),
    )
    return (down, video_grad, conv_weight_grad, down_weight_grad)


F32 = jnp.float32
BF16 = jnp.bfloat16
MESH = pl.DeviceIdType.MESH
WIDE = 256
OWN = 32


def lane_swap():
    lane = np.arange(512)
    outer, inner, channel = lane // 128, lane // 32 % 4, lane % 32
    table = np.zeros((512, 512), np.float32)
    table[lane, inner * 128 + outer * 32 + channel] = 1.0
    return jnp.asarray(table, BF16)


def lane_gather():
    lane = np.arange(1024)
    owner, part, channel = lane // 128, lane // 32 % 4, lane % 32
    table = np.zeros((4, 1024, 256), np.float32)
    table[part, lane, owner * 32 + channel] = 1.0
    return jnp.asarray(table, BF16)


def column_pick():
    table = np.zeros((2, 3, 256, 4, 4, 32), np.float32)
    for core in range(2):
        for tap in range(3):
            for chip in range(4):
                for channel in range(32):
                    table[core, tap, 64 * chip + 32 * core + channel, chip, tap, channel] = 1.0
    return jnp.asarray(table.reshape(2, 768, 512), BF16)


def dot(lhs, rhs):
    return jnp.dot(lhs, rhs, preferred_element_type=F32)


def dot_nt(lhs, rhs):
    return lax.dot_general(lhs, rhs, (((1,), (1,)), ((), ())), preferred_element_type=F32)


def move_cols(block, distance):
    if distance == 0:
        return block
    rows = block.shape[0]
    col = lax.broadcasted_iota(jnp.int32, block.shape, 0) % 8 + distance
    turned = pltpu.roll(block, (-distance) % rows, 0)
    return jnp.where((col >= 0) & (col < 8), turned, 0.0)


def fold_taps(result, outer, distances):
    parts = result.reshape(outer, 4, 8, 128)
    place = lax.broadcasted_iota(jnp.int32, (outer * 8, 128), 1) // OWN
    total = None
    for tap in range(3):
        layer = jnp.zeros((outer * 8, 128), F32)
        for clip in range(4):
            block = parts[:, clip].reshape(outer * 8, 128)
            turn = (OWN * (clip - tap)) % 128
            if turn:
                block = pltpu.roll(block, turn, 1)
            layer = jnp.where(place == clip, block, layer)
        layer = move_cols(layer, distances[tap])
        total = layer if total is None else total + layer
    return total


def group_total(row):
    first = lax.broadcasted_iota(jnp.int32, (128, 128), 0) // 8
    second = lax.broadcasted_iota(jnp.int32, (128, 128), 1) // 8
    same = (first == second).astype(F32)
    wide = jnp.broadcast_to(row, (8, 128))
    return jnp.dot(wide, same, preferred_element_type=F32, precision=lax.Precision.HIGHEST)[0:1]


def block_kernel(
    meta_ref, video_ref, cw_ref, dw_ref, og_ref, swap_ref, gather_ref, pick_ref,
    down_ref, vgrad_ref, cgrad_ref, dgrad_ref,
    meta_all, v_send, v_all, w_send, w_all, og_all, h_all, g_all, r_all, d_send, d_all,
    x_send, x_all, h_full, g_full, r_full, og_up, rows_fwd, cells, normed_ref, mask_ref,
    res_ref, stack_t, og_stack_t, back_ref, send_sems, recv_sems,
):
    chip = lax.axis_index("fsdp")
    core = lax.axis_index("tile")
    me = chip * 2 + core

    def peer(index):
        return {"fsdp": index // 2, "tile": index % 2}

    barrier = pltpu.get_barrier_semaphore()
    for step in range(1, 8):
        pl.semaphore_signal(barrier, inc=1, device_id=peer((me + step) % 8), device_id_type=MESH)
    pl.semaphore_wait(barrier, 7)

    def send(phase, step, src, dst, to):
        copy = pltpu.make_async_remote_copy(
            src_ref=src, dst_ref=dst, send_sem=send_sems.at[phase, step],
            recv_sem=recv_sems.at[phase, step], device_id=peer(to), device_id_type=MESH,
        )
        copy.start()
        return copy

    def send_all(phase, source, target):
        return [send(phase, s, source((me + s) % 8), target, (me + s) % 8) for s in range(1, 8)]

    def arrived(copies):
        for copy in copies:
            copy.wait_recv()

    meta_all[chip] = meta_ref[...]
    meta_copies = [
        send(3, s, meta_ref, meta_all.at[chip], ((chip + s) % 4) * 2 + core) for s in range(1, 4)
    ]
    halves = []
    for half in range(2):
        halves.append(
            jnp.concatenate(
                [video_ref[64 * t : 64 * t + 64, 128 * half : 128 * half + 128] for t in range(4)],
                axis=1,
            )
        )
    packed = dot(jnp.concatenate(halves, axis=0), swap_ref[...]).astype(BF16)
    for index in range(8):
        half, quarter = index // 4, index % 4
        v_send[index] = packed[64 * half : 64 * half + 64, 128 * quarter : 128 * quarter + 128]
    v_copies = send_all(0, lambda to: v_send.at[to], v_all.at[me])
    v_all[me] = v_send[me]
    og_all[me] = og_ref[...]
    og_copies = send_all(1, lambda to: og_ref, og_all.at[me])

    picks = None
    for tap in range(3):
        rows = [cw_ref[:, (3 * ab + tap) * WIDE : (3 * ab + tap + 1) * WIDE] for ab in range(9)]
        rows += [dw_ref[:, (3 * b + tap) * WIDE : (3 * b + tap + 1) * WIDE] for b in range(3)]
        term = dot(jnp.concatenate(rows, axis=0), pick_ref[core, 256 * tap : 256 * tap + 256, :])
        picks = term if picks is None else picks + term
    for other in range(4):
        w_send[other] = picks[:, 128 * other : 128 * other + 128].astype(BF16)
    w_all[chip] = w_send[chip]
    w_copies = []
    for s in range(1, 4):
        to = (chip + s) % 4
        w_copies.append(send(2, s, w_send.at[to], w_all.at[chip], to * 2 + core))

    mine = pl.ds(pl.multiple_of(core * OWN, OWN), OWN)
    for ab in range(9):
        for tap in range(3):
            at = (3 * ab + tap) * WIDE
            rows_fwd[ab, 32 * tap : 32 * tap + 32, :] = cw_ref[mine, at : at + WIDE]
        rows_fwd[ab, 96:128, :] = jnp.zeros((32, WIDE), BF16)
    for b in range(3):
        for tap in range(3):
            at = (3 * b + tap) * WIDE
            rows_fwd[9 + b, 32 * tap : 32 * tap + 32, :] = dw_ref[mine, at : at + WIDE]
        rows_fwd[9 + b, 96:128, :] = jnp.zeros((32, WIDE), BF16)

    edge = jnp.zeros((10, 32, WIDE), BF16)
    for t in range(2):
        h_full[t] = edge
        g_full[8 + t] = edge
    for t in range(8):
        for full, off in ((h_full, 2), (g_full, 0)):
            full[t + off, 0] = jnp.zeros((32, WIDE), BF16)
            full[t + off, 9] = jnp.zeros((32, WIDE), BF16)
        r_full[t, 4, 0] = jnp.zeros((32, WIDE), BF16)

    arrived(meta_copies)
    place1 = lax.broadcasted_iota(jnp.int32, (1, 128), 1) // OWN
    start = jnp.zeros((1, 128), F32)
    high = jnp.zeros((1, 128), F32)
    width = jnp.zeros((1, 128), F32)
    for clip in range(4):
        start = jnp.where(place1 == clip, meta_all[clip, 0:1, :], start)
        high = jnp.where(place1 == clip, meta_all[clip, 1:2, :], high)
        width = jnp.where(place1 == clip, meta_all[clip, 2:3, :], width)
    count = (8.0 - start) * high * width * 8.0
    row_id = lax.broadcasted_iota(jnp.int32, (512, 128), 0)
    in_time = (row_id // 64).astype(F32) >= start
    in_rows = (row_id // 8 % 8).astype(F32) < high
    in_cols = (row_id % 8).astype(F32) < width
    mask_ref[...] = jnp.where(in_time & in_rows & in_cols, 1.0, 0.0)

    arrived(v_copies)
    stacked = jnp.concatenate(
        [
            jnp.concatenate([v_all[2 * other + c] for other in range(4)], axis=1)
            for c in range(2)
        ],
        axis=0,
    )
    unpacked = dot(stacked, swap_ref[...])
    for t in range(8):
        c, q = t // 4, t % 4
        cells[64 * t : 64 * t + 64, :] = unpacked[64 * c : 64 * c + 64, 128 * q : 128 * q + 128]
    mask = mask_ref[...]
    centre = group_total(jnp.sum(mask * cells[...], axis=0, keepdims=True)) / count
    offset = cells[...] - centre
    spread = group_total(jnp.sum(mask * offset * offset, axis=0, keepdims=True)) / count
    inverse = lax.rsqrt(spread + EPSILON)
    normed = offset * inverse
    normed_ref[...] = normed
    h_all[me] = (mask * (normed / (1.0 + jnp.exp(-normed)))).astype(BF16)
    h_copies = send_all(4, lambda to: h_all.at[me], h_all.at[me])

    arrived(og_copies)
    up_row = lax.broadcasted_iota(jnp.int32, (128, 64), 0)
    up_col = lax.broadcasted_iota(jnp.int32, (128, 64), 1)
    lift = ((up_row // 8 == up_col // 4) & (up_row % 8 == 2 * (up_col % 4))).astype(F32).astype(BF16)
    for c in range(2):
        raised = [dot(lift, og_all[2 * clip + c]).reshape(16, 8, WIDE) for clip in range(4)]
        og_up[4 * c : 4 * c + 4] = (
            jnp.concatenate(raised, axis=1).astype(BF16).reshape(4, 4, 32, WIDE)
        )
    arrived(w_copies)

    def res_grad_frame(t, carry):
        lhs = og_up[t].reshape(128, WIDE)
        layers = []
        for b in range(3):
            panel = w_all[:, 64 * (9 + b) : 64 * (10 + b), :].reshape(256, 128)
            layers.append(fold_taps(dot(lhs, panel), 4, (0, -1, -2)).reshape(4, 8, 128))
        even = layers[0] + jnp.concatenate([jnp.zeros((1, 8, 128), F32), layers[2][:3]], axis=0)
        both = jnp.stack([even, layers[1]], axis=1).reshape(64, 128)
        at = pl.ds(pl.multiple_of(64 * t, 64), 64)
        value = (mask_ref[at, :] * both).astype(BF16)
        g_all[me, at, :] = value
        wide = value.astype(F32)
        res_ref[at, :] = wide
        shifts = [move_cols(wide, 1 - tap) for tap in range(3)]
        place = lax.broadcasted_iota(jnp.int32, (64, 128), 1) // OWN
        split = []
        for clip in range(4):
            block = jnp.zeros((64, 128), F32)
            for tap in range(3):
                turn = (OWN * (tap - clip)) % 128
                moved = pltpu.roll(shifts[tap], turn, 1) if turn else shifts[tap]
                block = jnp.where(place == tap, moved, block)
            split.append(block.reshape(8, 8, 128))
        rows = jnp.concatenate(split, axis=1).reshape(256, 128)
        stack_t[t] = rows.T.astype(BF16)
        return carry

    lax.fori_loop(0, 8, res_grad_frame, 0)
    g_copies = send_all(5, lambda to: g_all.at[me], g_all.at[me])

    def og_frame(t, carry):
        lhs = og_up[t].reshape(128, WIDE)
        from_row = lax.broadcasted_iota(jnp.int32, (WIDE, 128), 0)
        to_lane = lax.broadcasted_iota(jnp.int32, (WIDE, 128), 1)
        total = None
        for tap in range(3):
            chosen = (to_lane // OWN == tap) & (from_row == to_lane % OWN + OWN * me)
            term = move_cols(dot(lhs, chosen.astype(F32).astype(BF16)), -tap)
            total = term if total is None else total + term
        og_stack_t[t] = total.T.astype(BF16)
        return carry

    lax.fori_loop(0, 8, og_frame, 0)

    def assemble(source, t):
        at = pl.ds(pl.multiple_of(128 * t, 128), 128)
        lhs = jnp.concatenate([source[d, at, :] for d in range(8)], axis=1)
        blocks = [dot(lhs, gather_ref[clip]).reshape(16, 8, WIDE) for clip in range(4)]
        return jnp.concatenate(blocks, axis=1).astype(BF16).reshape(2, 8, 32, WIDE)

    arrived(h_copies)

    def fill_hidden(t, carry):
        h_full[pl.ds(2 * t + 2, 2), 1:9] = assemble(h_all, t)
        return carry

    lax.fori_loop(0, 4, fill_hidden, 0)

    def conv_frame(t, carry):
        total = None
        for a in range(3):
            for b in range(3):
                window = h_full[t + a, b : b + 8].reshape(256, WIDE)
                term = dot_nt(window, rows_fwd[3 * a + b])
                total = term if total is None else total + term
        folded = fold_taps(total, 8, (-1, 0, 1))
        at = pl.ds(pl.multiple_of(64 * t, 64), 64)
        r_all[me, at, :] = (mask_ref[at, :] * (cells[at, :] + folded)).astype(BF16)
        return carry

    lax.fori_loop(0, 8, conv_frame, 0)
    r_copies = send_all(6, lambda to: r_all.at[me], r_all.at[me])

    arrived(g_copies)

    def fill_grad(t, carry):
        g_full[pl.ds(2 * t, 2), 1:9] = assemble(g_all, t)
        return carry

    lax.fori_loop(0, 4, fill_grad, 0)

    def back_frame(t, carry):
        total = None
        for a in range(3):
            for b in range(3):
                window = g_full[t + 2 - a, 2 - b : 10 - b].reshape(256, WIDE)
                at = 64 * (3 * a + b)
                term = dot(window, w_all[:, at : at + 64, :].reshape(256, 128))
                total = term if total is None else total + term
        at = pl.ds(pl.multiple_of(64 * t, 64), 64)
        back_ref[at, :] = fold_taps(total, 8, (1, 0, -1))
        return carry

    lax.fori_loop(0, 8, back_frame, 0)
    mask = mask_ref[...]
    normed = normed_ref[...]
    gate = 1.0 / (1.0 + jnp.exp(-normed))
    pushed = mask * back_ref[...] * gate * (1.0 + normed * (1.0 - gate))
    mean_push = group_total(jnp.sum(pushed, axis=0, keepdims=True)) / count
    mean_pair = group_total(jnp.sum(pushed * normed, axis=0, keepdims=True)) / count
    through = inverse * (pushed - mean_push - normed * mean_pair)
    back_ref[...] = mask * through + res_ref[...]
    for c in range(2):
        quarter = [back_ref[64 * (4 * c + q) : 64 * (4 * c + q) + 64, :] for q in range(4)]
        swapped = dot(jnp.concatenate(quarter, axis=1).astype(BF16), swap_ref[...]).astype(BF16)
        for other in range(4):
            x_send[2 * other + c] = swapped[:, 128 * other : 128 * other + 128]
    x_all[me] = x_send[me]
    x_copies = send_all(8, lambda to: x_send.at[to], x_all.at[me])

    lhs = jnp.concatenate([stack_t[t] for t in range(8)], axis=1)
    for a in range(3):
        for b in range(3):
            rhs = h_full[a : a + 8, b : b + 8].reshape(2048, WIDE)
            grad = dot(lhs, rhs)
            for tap in range(3):
                at = (9 * a + 3 * b + tap) * WIDE
                cgrad_ref[mine, at : at + WIDE] = grad[32 * tap : 32 * tap + 32]
    sibling = chip * 2 + (1 - core)
    c_copy = send(9, 0, cgrad_ref.at[mine], cgrad_ref.at[mine], sibling)

    arrived(r_copies)

    def fill_residual(t, carry):
        r_full[pl.ds(2 * t, 2), 0:4] = assemble(r_all, t).reshape(2, 4, 2, 32, WIDE)
        return carry

    lax.fori_loop(0, 4, fill_residual, 0)

    def down_frame(t, carry):
        total = None
        for b in range(3):
            window = r_full[t, b // 2 : b // 2 + 4, b % 2].reshape(128, WIDE)
            term = dot_nt(window, rows_fwd[9 + b])
            total = term if total is None else total + term
        folded = fold_taps(total, 4, (0, 1, 2)).astype(BF16)
        to_row = lax.broadcasted_iota(jnp.int32, (16, 32), 0)
        from_row = lax.broadcasted_iota(jnp.int32, (16, 32), 1)
        even = (from_row == to_row * 2).astype(F32).astype(BF16)
        d_send[t] = dot(even, folded).astype(BF16)
        return carry

    lax.fori_loop(0, 8, down_frame, 0)

    def frames_of(to):
        return pl.ds(4 * (to % 2), 4)

    d_all[me] = d_send[frames_of(me)]
    d_copies = send_all(7, lambda to: d_send.at[frames_of(to)], d_all.at[me])
    lhs = jnp.concatenate([og_stack_t[t] for t in range(8)], axis=1)
    for b in range(3):
        rhs = r_full[:, b // 2 : b // 2 + 4, b % 2].reshape(1024, WIDE)
        grad = dot(lhs, rhs)
        for tap in range(3):
            at = (3 * b + tap) * WIDE
            dgrad_ref[mine, at : at + WIDE] = grad[32 * tap : 32 * tap + 32]
    g_copy = send(9, 1, dgrad_ref.at[mine], dgrad_ref.at[mine], sibling)

    arrived(x_copies)
    lhs = jnp.concatenate([x_all[d] for d in range(8)], axis=1)
    for t in range(4):
        vgrad_ref[64 * t : 64 * t + 64, :] = dot(lhs, gather_ref[t]).astype(BF16)
    arrived(d_copies)
    lhs = jnp.concatenate([d_all[d].reshape(64, 128) for d in range(8)], axis=1)
    down_ref[...] = dot(lhs, gather_ref[chip]).astype(BF16)
    arrived([c_copy, g_copy])
    for copies in (
        meta_copies, v_copies, og_copies, w_copies, h_copies, g_copies, r_copies, x_copies,
        d_copies, [c_copy, g_copy],
    ):
        for copy in copies:
            copy.wait_send()


def fused(video, conv_weight, down_weight, out_grad, clip_bucket, start_frame, bucket_res):
    bucket_ids = jnp.arange(bucket_res.shape[0], dtype=jnp.int32)
    picked = (clip_bucket[:, None] == bucket_ids[None, :]).astype(jnp.int32)
    limits = jnp.sum(picked[:, :, None] * bucket_res[None, :, :], axis=1)
    facts = jnp.concatenate([start_frame, limits[0], jnp.zeros((5,), jnp.int32)]).astype(F32)
    meta = jnp.broadcast_to(facts[:, None], (8, 128))
    vmem = pl.BlockSpec(memory_space=pltpu.VMEM)
    full = pltpu.VMEM((10, 10, 32, WIDE), BF16)
    gathered = pltpu.VMEM((8, 512, 128), BF16)
    wide = pltpu.VMEM((512, 128), F32)
    piece = pltpu.VMEM((8, 64, 128), BF16)
    down, video_grad, conv_grad, down_grad = pl.pallas_call(
        block_kernel,
        out_shape=(
            jax.ShapeDtypeStruct((64, WIDE), BF16),
            jax.ShapeDtypeStruct((256, WIDE), BF16),
            jax.ShapeDtypeStruct(conv_weight.shape, F32),
            jax.ShapeDtypeStruct(down_weight.shape, F32),
        ),
        in_specs=[vmem] * 8,
        out_specs=(vmem,) * 4,
        scratch_shapes=[
            pltpu.VMEM((4, 8, 128), F32),
            piece,
            piece,
            pltpu.VMEM((4, 768, 128), BF16),
            pltpu.VMEM((4, 768, 128), BF16),
            pltpu.VMEM((8, 64, WIDE), BF16),
            gathered,
            gathered,
            gathered,
            pltpu.VMEM((8, 16, 128), BF16),
            pltpu.VMEM((8, 4, 16, 128), BF16),
            piece,
            piece,
            full,
            full,
            pltpu.VMEM((8, 5, 2, 32, WIDE), BF16),
            pltpu.VMEM((8, 4, 32, WIDE), BF16),
            pltpu.VMEM((12, 128, WIDE), BF16),
            wide,
            wide,
            wide,
            wide,
            pltpu.VMEM((8, 128, 256), BF16),
            pltpu.VMEM((8, 128, 128), BF16),
            wide,
            pltpu.SemaphoreType.DMA((10, 8)),
            pltpu.SemaphoreType.DMA((10, 8)),
        ],
        compiler_params=pltpu.CompilerParams(
            collective_id=0, has_side_effects=True, vmem_limit_bytes=50 * 2**20
        ),
    )(
        meta,
        video.reshape(256, WIDE),
        conv_weight,
        down_weight,
        out_grad.reshape(64, WIDE),
        lane_swap(),
        lane_gather(),
        column_pick(),
    )
    return (down.reshape(out_grad.shape), video_grad.reshape(video.shape), conv_grad, down_grad)


def solution(mesh):
    placed = (
        P(("mix", "fsdp"), "tile", None, None, None),
        P(("mix", "fsdp"), None),
        P(("mix", "fsdp"), None),
        P(("mix", "fsdp"), "tile", None, None, None),
        P(("mix", "fsdp")),
        P(("mix", "fsdp")),
        P(),
    )
    return jax.shard_map(
        fused if mesh.shape["tile"] == 2 and mesh.shape["fsdp"] == 4 else shards,
        mesh=mesh,
        in_specs=placed,
        out_specs=(
            P(("mix", "fsdp"), "tile", None, None, None),
            P(("mix", "fsdp"), "tile", None, None, None),
            P(("mix", "fsdp"), None),
            P(("mix", "fsdp"), None),
        ),
        check_vma=False,
    )
```

```python
import functools

import jax
import jax.numpy as jnp
import numpy as np
from jax import lax
from jax.experimental import pallas as pl
from jax.experimental.pallas import tpu as pltpu
from jax.sharding import PartitionSpec as P

GROUPS = 32


EPSILON = 1e-06


def shifted(block, axis, distance):
    devices = range(lax.axis_size(axis))
    route = [(i - distance, i) for i in devices if i - distance in devices]
    return lax.ppermute(block, axis, route)


def valid_mask(clip_bucket, start_frame, bucket_res, first_frame, frame_count, side_cells):
    bucket_ids = jnp.arange(bucket_res.shape[0], dtype=jnp.int32)
    picked = (clip_bucket[:, None] == bucket_ids[None, :]).astype(jnp.int32)
    limits = jnp.sum(picked[:, :, None] * bucket_res[None, :, :], axis=1)
    frame_ids = first_frame + jnp.arange(frame_count, dtype=jnp.int32)
    positions = jnp.arange(side_cells, dtype=jnp.int32)
    in_time = frame_ids[None, :] >= start_frame[:, None]
    in_rows = positions[None, :] < limits[:, 0:1]
    in_cols = positions[None, :] < limits[:, 1:2]
    inside = in_time[:, :, None, None] & in_rows[:, None, :, None] & in_cols[:, None, None, :]
    return (inside.astype(jnp.float32)[..., None], limits)


def time_group(padded, tap_time, out_frames, side_cells, flipped):
    channel_count = padded.shape[-1]
    time_start = 2 - tap_time if flipped else tap_time
    layers = []
    for tap_row in range(3):
        for tap_col in range(3):
            row_start = 2 - tap_row if flipped else tap_row
            col_start = 2 - tap_col if flipped else tap_col
            window = padded[
                :,
                time_start : time_start + out_frames,
                row_start : row_start + side_cells,
                col_start : col_start + side_cells,
                :,
            ]
            layers.append(window.reshape(-1, channel_count))
    return jnp.stack(layers)


def stride_taps(padded, side_cells):
    channel_count = padded.shape[-1]
    layers = []
    for tap_row in range(3):
        for tap_col in range(3):
            window = padded[
                :, :, tap_row : tap_row + side_cells : 2, tap_col : tap_col + side_cells : 2, :
            ]
            layers.append(window.reshape(-1, channel_count))
    return jnp.stack(layers)


def weight_terms(grad_rows, slabs, cot_rows, hidden_padded, frame_count, side_cells):
    out_rows = grad_rows.shape[1]
    down_term = lax.dot_general(
        grad_rows, slabs, (((0,), (1,)), ((), ())), preferred_element_type=jnp.float32
    ).reshape(out_rows, -1)
    conv_parts = []
    for tap_time in range(3):
        group = time_group(hidden_padded, tap_time, frame_count, side_cells, False)
        conv_parts.append(
            lax.dot_general(
                cot_rows, group, (((0,), (1,)), ((), ())), preferred_element_type=jnp.float32
            )
        )
    conv_term = jnp.concatenate(conv_parts, axis=1).reshape(out_rows, -1)
    return (conv_term, down_term)


def transpose_conv(grad_padded, conv_weight, out_frames, side_cells):
    channel_count = grad_padded.shape[-1]
    row_total = grad_padded.shape[0] * out_frames * side_cells * side_cells
    initial = jnp.zeros((row_total, channel_count), jnp.float32)
    running = initial
    weight_panel = lax.all_gather(conv_weight, "fsdp", axis=0, tiled=True)
    panel_rows = weight_panel.shape[0]
    panel = weight_panel.reshape(panel_rows, 27, channel_count)
    for tap_time in range(3):
        group = time_group(grad_padded, tap_time, out_frames, side_cells, True)
        running = running + lax.dot_general(
            group,
            panel[:, 9 * tap_time : 9 * tap_time + 9, :],
            (((0, 2), (1, 0)), ((), ())),
            preferred_element_type=jnp.float32,
        )
    return running


def shards(video, conv_weight, down_weight, out_grad, clip_bucket, start_frame, bucket_res):
    clip_count, frame_count, side_cells, side_again, channel_count = video.shape
    half_side = side_cells // 2
    group_width = channel_count // GROUPS
    tiles = lax.axis_size("tile")
    mask, limits = valid_mask(
        clip_bucket,
        start_frame,
        bucket_res,
        lax.axis_index("tile") * frame_count,
        frame_count,
        side_cells,
    )
    valid_count = (
        (frame_count * tiles - start_frame) * limits[:, 0] * limits[:, 1] * group_width
    ).astype(jnp.float32)
    grouped_shape = (clip_count, frame_count, side_cells, side_cells, GROUPS, group_width)
    summed_axes = (1, 2, 3, 5)
    cell_weight = mask[..., None]
    grouped = video.astype(jnp.float32).reshape(grouped_shape)
    first_sum = lax.psum(jnp.sum(grouped * cell_weight, axis=summed_axes), "tile")
    centre = first_sum / valid_count[:, None]
    offset = grouped - centre[:, None, None, None, :, None]
    second_sum = lax.psum(jnp.sum(cell_weight * offset * offset, axis=summed_axes), "tile")
    spread = second_sum / valid_count[:, None]
    inverse = lax.rsqrt(spread + EPSILON)
    normed_grouped = offset * inverse[:, None, None, None, :, None]
    normed = normed_grouped.reshape(video.shape)
    hidden = (mask * jax.nn.silu(normed)).astype(jnp.bfloat16)
    past = shifted(hidden[:, frame_count - 2 :], "tile", 1)
    hidden_padded = jnp.pad(
        jnp.concatenate([past, hidden], axis=1), ((0, 0), (0, 0), (1, 1), (1, 1), (0, 0))
    )

    def conv_columns(weight_panel):
        panel = weight_panel.reshape(weight_panel.shape[0], 27, channel_count)
        summed = None
        for tap_time in range(3):
            group = time_group(hidden_padded, tap_time, frame_count, side_cells, False)
            term = lax.dot_general(
                group,
                panel[:, 9 * tap_time : 9 * tap_time + 9, :],
                (((0, 2), (1, 2)), ((), ())),
                preferred_element_type=jnp.float32,
            )
            summed = term if summed is None else summed + term
        return summed

    conv_out = conv_columns(lax.all_gather(conv_weight, "fsdp", axis=0, tiled=True))
    residual = (mask * (video.astype(jnp.float32) + conv_out.reshape(video.shape))).astype(
        jnp.bfloat16
    )
    down_slabs = stride_taps(
        jnp.pad(residual, ((0, 0), (0, 0), (0, 1), (0, 1), (0, 0))), side_cells
    )
    weight_panel = lax.all_gather(down_weight, "fsdp", axis=0, tiled=True)
    panel = weight_panel.reshape(weight_panel.shape[0], 9, channel_count)
    down_out = lax.dot_general(
        down_slabs, panel, (((0, 2), (1, 2)), ((), ())), preferred_element_type=jnp.float32
    )
    down = down_out.astype(jnp.bfloat16).reshape(
        clip_count, frame_count, half_side, half_side, channel_count
    )
    grad_flat = out_grad.reshape(-1, channel_count)
    weight_panel = lax.all_gather(down_weight, "fsdp", axis=0, tiled=True)
    panel_rows = weight_panel.shape[0]
    panel = weight_panel.reshape(panel_rows, 9, channel_count)
    tap_grads = lax.dot_general(
        grad_flat, panel, (((1,), (0,)), ((), ())), preferred_element_type=jnp.float32
    )
    spread_back = jnp.zeros(
        (clip_count, frame_count, side_cells + 1, side_cells + 1, channel_count), jnp.float32
    )
    for tap_row in range(3):
        for tap_col in range(3):
            term = tap_grads[:, tap_row * 3 + tap_col, :].reshape(
                clip_count, frame_count, half_side, half_side, channel_count
            )
            spread_back = spread_back.at[
                :, :, tap_row : tap_row + side_cells : 2, tap_col : tap_col + side_cells : 2, :
            ].add(term)
    res_grad = (mask * spread_back[:, :, :side_cells, :side_cells, :]).astype(jnp.bfloat16)
    res_flat = res_grad.reshape(-1, channel_count)
    later = shifted(res_grad[:, :2], "tile", -1)
    grad_padded = jnp.pad(
        jnp.concatenate([res_grad, later], axis=1), ((0, 0), (0, 0), (1, 1), (1, 1), (0, 0))
    )
    back_hidden = transpose_conv(grad_padded, conv_weight, frame_count, side_cells).reshape(
        video.shape
    )
    gate_value = jax.nn.sigmoid(normed)
    pushed = mask * back_hidden * gate_value * (1.0 + normed * (1.0 - gate_value))
    pushed_grouped = pushed.reshape(grouped_shape)
    push_sum, pair_sum = lax.psum(
        (
            jnp.sum(pushed_grouped, axis=summed_axes),
            jnp.sum(pushed_grouped * normed_grouped, axis=summed_axes),
        ),
        "tile",
    )
    mean_push = push_sum / valid_count[:, None]
    mean_pair = pair_sum / valid_count[:, None]
    through_norm = inverse[:, None, None, None, :, None] * (
        pushed_grouped
        - mean_push[:, None, None, None, :, None]
        - normed_grouped * mean_pair[:, None, None, None, :, None]
    )
    video_grad = (mask * through_norm.reshape(video.shape) + res_grad.astype(jnp.float32)).astype(
        jnp.bfloat16
    )
    conv_term, down_term = weight_terms(
        grad_flat, down_slabs, res_flat, hidden_padded, frame_count, side_cells
    )
    conv_share, down_share = (
        lax.psum_scatter(conv_term, ("fsdp", "tile"), scatter_dimension=0, tiled=True),
        lax.psum_scatter(down_term, ("fsdp", "tile"), scatter_dimension=0, tiled=True),
    )
    conv_weight_grad, down_weight_grad = (
        lax.all_gather(conv_share, "tile", axis=0, tiled=True),
        lax.all_gather(down_share, "tile", axis=0, tiled=True),
    )
    return (down, video_grad, conv_weight_grad, down_weight_grad)


F32 = jnp.float32
BF16 = jnp.bfloat16
MESH = pl.DeviceIdType.MESH
WIDE = 256
OWN = 32


def lane_swap():
    lane = np.arange(512)
    outer, inner, channel = lane // 128, lane // 32 % 4, lane % 32
    table = np.zeros((512, 512), np.float32)
    table[lane, inner * 128 + outer * 32 + channel] = 1.0
    return jnp.asarray(table, BF16)


def lane_gather():
    lane = np.arange(1024)
    owner, part, channel = lane // 128, lane // 32 % 4, lane % 32
    table = np.zeros((4, 1024, 256), np.float32)
    table[part, lane, owner * 32 + channel] = 1.0
    return jnp.asarray(table, BF16)


def column_pick():
    table = np.zeros((2, 3, 256, 4, 4, 32), np.float32)
    for core in range(2):
        for tap in range(3):
            for chip in range(4):
                for channel in range(32):
                    table[core, tap, 64 * chip + 32 * core + channel, chip, tap, channel] = 1.0
    return jnp.asarray(table.reshape(2, 768, 512), BF16)


def dot(lhs, rhs):
    return jnp.dot(lhs, rhs, preferred_element_type=F32)


def dot_nt(lhs, rhs):
    return lax.dot_general(lhs, rhs, (((1,), (1,)), ((), ())), preferred_element_type=F32)


def move_cols(block, distance):
    if distance == 0:
        return block
    rows = block.shape[0]
    col = lax.broadcasted_iota(jnp.int32, block.shape, 0) % 8 + distance
    turned = pltpu.roll(block, (-distance) % rows, 0)
    return jnp.where((col >= 0) & (col < 8), turned, 0.0)


def fold_taps(result, outer, distances):
    parts = result.reshape(outer, 4, 8, 128)
    place = lax.broadcasted_iota(jnp.int32, (outer * 8, 128), 1) // OWN
    total = None
    for tap in range(3):
        layer = jnp.zeros((outer * 8, 128), F32)
        for clip in range(4):
            block = parts[:, clip].reshape(outer * 8, 128)
            turn = (OWN * (clip - tap)) % 128
            if turn:
                block = pltpu.roll(block, turn, 1)
            layer = jnp.where(place == clip, block, layer)
        layer = move_cols(layer, distances[tap])
        total = layer if total is None else total + layer
    return total


def group_total(row):
    first = lax.broadcasted_iota(jnp.int32, (128, 128), 0) // 8
    second = lax.broadcasted_iota(jnp.int32, (128, 128), 1) // 8
    same = (first == second).astype(F32)
    wide = jnp.broadcast_to(row, (8, 128))
    return jnp.dot(wide, same, preferred_element_type=F32, precision=lax.Precision.HIGHEST)[0:1]


def block_kernel(
    bucket_ref, start_ref, res_table_ref, video_ref, cw_hbm, dw_hbm, og_ref, swap_hbm,
    gather_hbm, pick_hbm,
    down_ref, vgrad_ref, cgrad_ref, dgrad_ref,
    meta_ref, cw_ref, dw_ref, swap_ref, gather_ref, pick_ref,
    meta_all, v_send, v_all, w_send, w_all, og_all, h_all, g_all, r_all, d_send, d_all,
    x_send, x_all, h_full, g_full, r_full, og_up, rows_fwd, cells, normed_ref, mask_ref,
    res_ref, stack_t, og_stack_t, back_ref, load_sems, send_sems, recv_sems,
):
    chip = lax.axis_index("fsdp")
    core = lax.axis_index("tile")
    me = chip * 2 + core
    sibling = chip * 2 + (1 - core)

    def peer(index):
        return {"fsdp": index // 2, "tile": index % 2}

    loads = {}
    for index, (name, source, target) in enumerate(
        (
            ("swap", swap_hbm, swap_ref),
            ("dw", dw_hbm, dw_ref),
            ("pick", pick_hbm.at[core], pick_ref),
            ("cw", cw_hbm, cw_ref),
            ("gather", gather_hbm, gather_ref),
        )
    ):
        loads[name] = pltpu.make_async_copy(source, target, load_sems.at[index])
        loads[name].start()

    barrier = pltpu.get_barrier_semaphore()
    for step in range(1, 8):
        pl.semaphore_signal(barrier, inc=1, device_id=peer((me + step) % 8), device_id_type=MESH)
    pl.semaphore_wait(barrier, 7)

    def send(phase, step, src, dst, to):
        copy = pltpu.make_async_remote_copy(
            src_ref=src, dst_ref=dst, send_sem=send_sems.at[phase, step],
            recv_sem=recv_sems.at[phase, step], device_id=peer(to), device_id_type=MESH,
        )
        copy.start()
        return copy

    def send_all(phase, source, target):
        return [send(phase, s, source((me + s) % 8), target, (me + s) % 8) for s in range(1, 8)]

    def spread_out(phase, target):
        copies = [send(phase, 4, target.at[me], target.at[me], sibling)]
        for s in range(1, 4):
            copies.append(send(phase, s, target.at[me], target.at[me], ((chip + s) % 4) * 2 + core))
        return copies

    def relay(phase, target, copies):
        passed = []
        for s in range(1, 4):
            copies[s].wait_recv()
            slot = ((chip + 4 - s) % 4) * 2 + core
            passed.append(send(phase, 4 + s, target.at[slot], target.at[slot], sibling))
        copies.extend(passed)

    def complete(copies):
        copies[0].wait_recv()
        for copy in copies[4:]:
            copy.wait_recv()

    def arrived(copies):
        for copy in copies:
            copy.wait_recv()

    bucket = bucket_ref[0]
    high, width = jnp.int32(0), jnp.int32(0)
    for index in range(res_table_ref.shape[0]):
        high = high + jnp.where(bucket == index, res_table_ref[index, 0], 0)
        width = width + jnp.where(bucket == index, res_table_ref[index, 1], 0)
    line = lax.broadcasted_iota(jnp.int32, (8, 128), 0)
    facts = jnp.where(line == 0, start_ref[0], jnp.where(line == 1, high, width)).astype(F32)
    meta_ref[...] = facts
    meta_all[chip] = facts
    meta_copies = [
        send(3, s, meta_ref, meta_all.at[chip], ((chip + s) % 4) * 2 + core) for s in range(1, 4)
    ]
    loads["swap"].wait()
    halves = []
    for half in range(2):
        halves.append(
            jnp.concatenate(
                [video_ref[64 * t : 64 * t + 64, 128 * half : 128 * half + 128] for t in range(4)],
                axis=1,
            )
        )
    packed = dot(jnp.concatenate(halves, axis=0), swap_ref[...]).astype(BF16)
    for index in range(8):
        half, quarter = index // 4, index % 4
        v_send[index] = packed[64 * half : 64 * half + 64, 128 * quarter : 128 * quarter + 128]
    v_copies = send_all(0, lambda to: v_send.at[to], v_all.at[me])
    v_all[me] = v_send[me]
    og_all[me] = og_ref[0].astype(F32).reshape(64, WIDE).astype(BF16)
    og_copies = spread_out(1, og_all)

    loads["dw"].wait()
    loads["pick"].wait()

    def exchange_columns(phase, ref, blocks, first):
        picks = None
        for tap in range(3):
            at = [(3 * block + tap) * WIDE for block in range(blocks)]
            rows = jnp.concatenate([ref[:, low : low + WIDE] for low in at], axis=0)
            term = dot(rows, pick_ref[256 * tap : 256 * tap + 256, :])
            picks = term if picks is None else picks + term
        part = pl.ds(first, 64 * blocks)
        for other in range(4):
            w_send[other, part, :] = picks[:, 128 * other : 128 * other + 128].astype(BF16)
        w_all[chip, part, :] = w_send[chip, part, :]
        copies = []
        for s in range(1, 4):
            to = (chip + s) % 4
            copies.append(
                send(phase, s, w_send.at[to, part], w_all.at[chip, part], to * 2 + core)
            )
        return copies

    dw_copies = exchange_columns(2, dw_ref, 3, 576)

    arrived(meta_copies)
    place1 = lax.broadcasted_iota(jnp.int32, (1, 128), 1) // OWN
    start = jnp.zeros((1, 128), F32)
    high = jnp.zeros((1, 128), F32)
    width = jnp.zeros((1, 128), F32)
    for clip in range(4):
        start = jnp.where(place1 == clip, meta_all[clip, 0:1, :], start)
        high = jnp.where(place1 == clip, meta_all[clip, 1:2, :], high)
        width = jnp.where(place1 == clip, meta_all[clip, 2:3, :], width)
    count = (8.0 - start) * high * width * 8.0
    row_id = lax.broadcasted_iota(jnp.int32, (512, 128), 0)
    in_time = (row_id // 64).astype(F32) >= start
    in_rows = (row_id // 8 % 8).astype(F32) < high
    in_cols = (row_id % 8).astype(F32) < width
    mask_ref[...] = jnp.where(in_time & in_rows & in_cols, 1.0, 0.0)

    arrived(v_copies)
    stacked = jnp.concatenate(
        [
            jnp.concatenate([v_all[2 * other + c] for other in range(4)], axis=1)
            for c in range(2)
        ],
        axis=0,
    )
    unpacked = dot(stacked, swap_ref[...])
    for t in range(8):
        c, q = t // 4, t % 4
        cells[64 * t : 64 * t + 64, :] = unpacked[64 * c : 64 * c + 64, 128 * q : 128 * q + 128]
    mask = mask_ref[...]
    centre = group_total(jnp.sum(mask * cells[...], axis=0, keepdims=True)) / count
    offset = cells[...] - centre
    spread = group_total(jnp.sum(mask * offset * offset, axis=0, keepdims=True)) / count
    inverse = lax.rsqrt(spread + EPSILON)
    normed = offset * inverse
    normed_ref[...] = normed
    h_all[me] = (mask * (normed / (1.0 + jnp.exp(-normed)))).astype(BF16)
    h_copies = spread_out(4, h_all)

    relay(1, og_all, og_copies)
    complete(og_copies)
    up_row = lax.broadcasted_iota(jnp.int32, (128, 64), 0)
    up_col = lax.broadcasted_iota(jnp.int32, (128, 64), 1)
    lift = ((up_row // 8 == up_col // 4) & (up_row % 8 == 2 * (up_col % 4))).astype(F32).astype(BF16)
    for c in range(2):
        raised = [dot(lift, og_all[2 * clip + c]).reshape(16, 8, WIDE) for clip in range(4)]
        og_up[4 * c : 4 * c + 4] = (
            jnp.concatenate(raised, axis=1).astype(BF16).reshape(4, 4, 32, WIDE)
        )
    arrived(dw_copies)

    def res_grad_frame(t, carry):
        lhs = og_up[t].reshape(128, WIDE)
        layers = []
        for b in range(3):
            panel = w_all[:, 64 * (9 + b) : 64 * (10 + b), :].reshape(256, 128)
            layers.append(fold_taps(dot(lhs, panel), 4, (0, -1, -2)).reshape(4, 8, 128))
        even = layers[0] + jnp.concatenate([jnp.zeros((1, 8, 128), F32), layers[2][:3]], axis=0)
        both = jnp.stack([even, layers[1]], axis=1).reshape(64, 128)
        at = pl.ds(pl.multiple_of(64 * t, 64), 64)
        value = (mask_ref[at, :] * both).astype(BF16)
        g_all[me, at, :] = value
        wide = value.astype(F32)
        res_ref[at, :] = wide
        return carry

    lax.fori_loop(0, 8, res_grad_frame, 0)
    g_copies = spread_out(5, g_all)

    loads["cw"].wait()
    cw_copies = exchange_columns(10, cw_ref, 9, 0)

    mine = pl.ds(pl.multiple_of(core * OWN, OWN), OWN)
    for ab in range(9):
        for tap in range(3):
            at = (3 * ab + tap) * WIDE
            rows_fwd[ab, 32 * tap : 32 * tap + 32, :] = cw_ref[mine, at : at + WIDE]
        rows_fwd[ab, 96:128, :] = jnp.zeros((32, WIDE), BF16)
    for b in range(3):
        for tap in range(3):
            at = (3 * b + tap) * WIDE
            rows_fwd[9 + b, 32 * tap : 32 * tap + 32, :] = dw_ref[mine, at : at + WIDE]
        rows_fwd[9 + b, 96:128, :] = jnp.zeros((32, WIDE), BF16)

    edge = jnp.zeros((10, 32, WIDE), BF16)
    for t in range(2):
        h_full[t] = edge
        g_full[8 + t] = edge
    for t in range(8):
        for full, off in ((h_full, 2), (g_full, 0)):
            full[t + off, 0] = jnp.zeros((32, WIDE), BF16)
            full[t + off, 9] = jnp.zeros((32, WIDE), BF16)
        r_full[t, 4, 0] = jnp.zeros((32, WIDE), BF16)

    def stack_frame(t, carry):
        at = pl.ds(pl.multiple_of(64 * t, 64), 64)
        wide = res_ref[at, :]
        shifts = [move_cols(wide, 1 - tap) for tap in range(3)]
        place = lax.broadcasted_iota(jnp.int32, (64, 128), 1) // OWN
        split = []
        for clip in range(4):
            block = jnp.zeros((64, 128), F32)
            for tap in range(3):
                turn = (OWN * (tap - clip)) % 128
                moved = pltpu.roll(shifts[tap], turn, 1) if turn else shifts[tap]
                block = jnp.where(place == tap, moved, block)
            split.append(block.reshape(8, 8, 128))
        rows = jnp.concatenate(split, axis=1).reshape(256, 128)
        stack_t[t] = rows.T.astype(BF16)
        return carry

    lax.fori_loop(0, 8, stack_frame, 0)

    def og_frame(t, carry):
        lhs = og_up[t].reshape(128, WIDE)
        from_row = lax.broadcasted_iota(jnp.int32, (WIDE, 128), 0)
        to_lane = lax.broadcasted_iota(jnp.int32, (WIDE, 128), 1)
        total = None
        for tap in range(3):
            chosen = (to_lane // OWN == tap) & (from_row == to_lane % OWN + OWN * me)
            term = move_cols(dot(lhs, chosen.astype(F32).astype(BF16)), -tap)
            total = term if total is None else total + term
        og_stack_t[t] = total.T.astype(BF16)
        return carry

    lax.fori_loop(0, 8, og_frame, 0)

    def assemble(source, t):
        at = pl.ds(pl.multiple_of(128 * t, 128), 128)
        lhs = jnp.concatenate([source[d, at, :] for d in range(8)], axis=1)
        blocks = [dot(lhs, gather_ref[clip]).reshape(16, 8, WIDE) for clip in range(4)]
        return jnp.concatenate(blocks, axis=1).astype(BF16).reshape(2, 8, 32, WIDE)

    relay(4, h_all, h_copies)
    loads["gather"].wait()
    complete(h_copies)

    def fill_hidden(t, carry):
        h_full[pl.ds(2 * t + 2, 2), 1:9] = assemble(h_all, t)
        return carry

    lax.fori_loop(0, 4, fill_hidden, 0)

    def conv_frame(t, carry):
        total = None
        for a in range(3):
            for b in range(3):
                window = h_full[t + a, b : b + 8].reshape(256, WIDE)
                term = dot_nt(window, rows_fwd[3 * a + b])
                total = term if total is None else total + term
        folded = fold_taps(total, 8, (-1, 0, 1))
        at = pl.ds(pl.multiple_of(64 * t, 64), 64)
        r_all[me, at, :] = (mask_ref[at, :] * (cells[at, :] + folded)).astype(BF16)
        return carry

    lax.fori_loop(0, 4, conv_frame, 0)
    relay(5, g_all, g_copies)
    lax.fori_loop(4, 8, conv_frame, 0)
    r_copies = spread_out(6, r_all)

    complete(g_copies)

    def fill_grad(t, carry):
        g_full[pl.ds(2 * t, 2), 1:9] = assemble(g_all, t)
        return carry

    lax.fori_loop(0, 4, fill_grad, 0)

    arrived(cw_copies)

    def back_frame(t, carry):
        total = None
        for a in range(3):
            for b in range(3):
                window = g_full[t + 2 - a, 2 - b : 10 - b].reshape(256, WIDE)
                at = 64 * (3 * a + b)
                term = dot(window, w_all[:, at : at + 64, :].reshape(256, 128))
                total = term if total is None else total + term
        at = pl.ds(pl.multiple_of(64 * t, 64), 64)
        back_ref[at, :] = fold_taps(total, 8, (1, 0, -1))
        return carry

    lax.fori_loop(0, 8, back_frame, 0)
    mask = mask_ref[...]
    normed = normed_ref[...]
    gate = 1.0 / (1.0 + jnp.exp(-normed))
    pushed = mask * back_ref[...] * gate * (1.0 + normed * (1.0 - gate))
    mean_push = group_total(jnp.sum(pushed, axis=0, keepdims=True)) / count
    mean_pair = group_total(jnp.sum(pushed * normed, axis=0, keepdims=True)) / count
    through = inverse * (pushed - mean_push - normed * mean_pair)
    back_ref[...] = mask * through + res_ref[...]
    for c in range(2):
        quarter = [back_ref[64 * (4 * c + q) : 64 * (4 * c + q) + 64, :] for q in range(4)]
        swapped = dot(jnp.concatenate(quarter, axis=1).astype(BF16), swap_ref[...]).astype(BF16)
        for other in range(4):
            x_send[2 * other + c] = swapped[:, 128 * other : 128 * other + 128]
    x_all[me] = x_send[me]
    x_copies = send_all(8, lambda to: x_send.at[to], x_all.at[me])

    relay(6, r_all, r_copies)
    lhs = jnp.concatenate([stack_t[t] for t in range(8)], axis=1)
    for a in range(3):
        for b in range(3):
            rhs = h_full[a : a + 8, b : b + 8].reshape(2048, WIDE)
            grad = dot(lhs, rhs)
            for tap in range(3):
                at = (9 * a + 3 * b + tap) * WIDE
                cgrad_ref[mine, at : at + WIDE] = grad[32 * tap : 32 * tap + 32]
    c_copy = send(9, 0, cgrad_ref.at[mine], cgrad_ref.at[mine], sibling)

    complete(r_copies)

    def fill_residual(t, carry):
        r_full[pl.ds(2 * t, 2), 0:4] = assemble(r_all, t).reshape(2, 4, 2, 32, WIDE)
        return carry

    lax.fori_loop(0, 4, fill_residual, 0)

    def down_frame(t, carry):
        total = None
        for b in range(3):
            window = r_full[t, b // 2 : b // 2 + 4, b % 2].reshape(128, WIDE)
            term = dot_nt(window, rows_fwd[9 + b])
            total = term if total is None else total + term
        folded = fold_taps(total, 4, (0, 1, 2)).astype(BF16)
        to_row = lax.broadcasted_iota(jnp.int32, (16, 32), 0)
        from_row = lax.broadcasted_iota(jnp.int32, (16, 32), 1)
        even = (from_row == to_row * 2).astype(F32).astype(BF16)
        d_send[t] = dot(even, folded).astype(BF16)
        return carry

    lax.fori_loop(0, 8, down_frame, 0)

    def frames_of(to):
        return pl.ds(4 * (to % 2), 4)

    d_all[me] = d_send[frames_of(me)]
    d_copies = send_all(7, lambda to: d_send.at[frames_of(to)], d_all.at[me])
    lhs = jnp.concatenate([og_stack_t[t] for t in range(8)], axis=1)
    for b in range(3):
        rhs = r_full[:, b // 2 : b // 2 + 4, b % 2].reshape(1024, WIDE)
        grad = dot(lhs, rhs)
        for tap in range(3):
            at = (3 * b + tap) * WIDE
            dgrad_ref[mine, at : at + WIDE] = grad[32 * tap : 32 * tap + 32]
    g_copy = send(9, 1, dgrad_ref.at[mine], dgrad_ref.at[mine], sibling)

    arrived(x_copies)
    lhs = jnp.concatenate([x_all[d] for d in range(8)], axis=1)
    for t in range(4):
        vgrad_ref[64 * t : 64 * t + 64, :] = dot(lhs, gather_ref[t]).astype(BF16)
    arrived(d_copies)
    lhs = jnp.concatenate([d_all[d].reshape(64, 128) for d in range(8)], axis=1)
    down_ref[0] = dot(lhs, gather_ref[chip]).reshape(4, 4, 4, WIDE).astype(BF16)
    arrived([c_copy, g_copy])
    for copies in (
        meta_copies, v_copies, og_copies, dw_copies, cw_copies, h_copies, g_copies, r_copies, x_copies,
        d_copies, [c_copy, g_copy],
    ):
        for copy in copies:
            copy.wait_send()


def fused(video, conv_weight, down_weight, out_grad, clip_bucket, start_frame, bucket_res):
    vmem = pl.BlockSpec(memory_space=pltpu.VMEM)
    smem = pl.BlockSpec(memory_space=pltpu.SMEM)
    anywhere = pl.BlockSpec(memory_space=pl.ANY)
    full = pltpu.VMEM((10, 10, 32, WIDE), BF16)
    gathered = pltpu.VMEM((8, 512, 128), BF16)
    wide = pltpu.VMEM((512, 128), F32)
    piece = pltpu.VMEM((8, 64, 128), BF16)
    down, video_grad, conv_grad, down_grad = pl.pallas_call(
        block_kernel,
        out_shape=(
            jax.ShapeDtypeStruct(out_grad.shape, BF16),
            jax.ShapeDtypeStruct((256, WIDE), BF16),
            jax.ShapeDtypeStruct(conv_weight.shape, F32),
            jax.ShapeDtypeStruct(down_weight.shape, F32),
        ),
        in_specs=[smem] * 3 + [vmem, anywhere, anywhere, vmem] + [anywhere] * 3,
        out_specs=(vmem,) * 4,
        scratch_shapes=[
            pltpu.VMEM((8, 128), F32),
            pltpu.VMEM(conv_weight.shape, BF16),
            pltpu.VMEM(down_weight.shape, BF16),
            pltpu.VMEM((512, 512), BF16),
            pltpu.VMEM((4, 1024, 256), BF16),
            pltpu.VMEM((768, 512), BF16),
            pltpu.VMEM((4, 8, 128), F32),
            piece,
            piece,
            pltpu.VMEM((4, 768, 128), BF16),
            pltpu.VMEM((4, 768, 128), BF16),
            pltpu.VMEM((8, 64, WIDE), BF16),
            gathered,
            gathered,
            gathered,
            pltpu.VMEM((8, 16, 128), BF16),
            pltpu.VMEM((8, 4, 16, 128), BF16),
            piece,
            piece,
            full,
            full,
            pltpu.VMEM((8, 5, 2, 32, WIDE), BF16),
            pltpu.VMEM((8, 4, 32, WIDE), BF16),
            pltpu.VMEM((12, 128, WIDE), BF16),
            wide,
            wide,
            wide,
            wide,
            pltpu.VMEM((8, 128, 256), BF16),
            pltpu.VMEM((8, 128, 128), BF16),
            wide,
            pltpu.SemaphoreType.DMA((5,)),
            pltpu.SemaphoreType.DMA((11, 8)),
            pltpu.SemaphoreType.DMA((11, 8)),
        ],
        compiler_params=pltpu.CompilerParams(
            collective_id=0, has_side_effects=True, vmem_limit_bytes=60 * 2**20
        ),
    )(
        clip_bucket,
        start_frame,
        bucket_res,
        video.reshape(256, WIDE),
        conv_weight,
        down_weight,
        out_grad,
        lane_swap(),
        lane_gather(),
        column_pick(),
    )
    return (down, video_grad.reshape(video.shape), conv_grad, down_grad)


def solution(mesh):
    placed = (
        P(("mix", "fsdp"), "tile", None, None, None),
        P(("mix", "fsdp"), None),
        P(("mix", "fsdp"), None),
        P(("mix", "fsdp"), "tile", None, None, None),
        P(("mix", "fsdp")),
        P(("mix", "fsdp")),
        P(),
    )
    return jax.shard_map(
        fused if mesh.shape["tile"] == 2 and mesh.shape["fsdp"] == 4 else shards,
        mesh=mesh,
        in_specs=placed,
        out_specs=(
            P(("mix", "fsdp"), "tile", None, None, None),
            P(("mix", "fsdp"), "tile", None, None, None),
            P(("mix", "fsdp"), None),
            P(("mix", "fsdp"), None),
        ),
        check_vma=False,
    )
```

```python
import functools

import jax
import jax.numpy as jnp
import numpy as np
from jax import lax
from jax.experimental import pallas as pl
from jax.experimental.pallas import tpu as pltpu
from jax.sharding import PartitionSpec as P

GROUPS = 32


EPSILON = 1e-06


def shifted(block, axis, distance):
    devices = range(lax.axis_size(axis))
    route = [(i - distance, i) for i in devices if i - distance in devices]
    return lax.ppermute(block, axis, route)


def valid_mask(clip_bucket, start_frame, bucket_res, first_frame, frame_count, side_cells):
    bucket_ids = jnp.arange(bucket_res.shape[0], dtype=jnp.int32)
    picked = (clip_bucket[:, None] == bucket_ids[None, :]).astype(jnp.int32)
    limits = jnp.sum(picked[:, :, None] * bucket_res[None, :, :], axis=1)
    frame_ids = first_frame + jnp.arange(frame_count, dtype=jnp.int32)
    positions = jnp.arange(side_cells, dtype=jnp.int32)
    in_time = frame_ids[None, :] >= start_frame[:, None]
    in_rows = positions[None, :] < limits[:, 0:1]
    in_cols = positions[None, :] < limits[:, 1:2]
    inside = in_time[:, :, None, None] & in_rows[:, None, :, None] & in_cols[:, None, None, :]
    return (inside.astype(jnp.float32)[..., None], limits)


def time_group(padded, tap_time, out_frames, side_cells, flipped):
    channel_count = padded.shape[-1]
    time_start = 2 - tap_time if flipped else tap_time
    layers = []
    for tap_row in range(3):
        for tap_col in range(3):
            row_start = 2 - tap_row if flipped else tap_row
            col_start = 2 - tap_col if flipped else tap_col
            window = padded[
                :,
                time_start : time_start + out_frames,
                row_start : row_start + side_cells,
                col_start : col_start + side_cells,
                :,
            ]
            layers.append(window.reshape(-1, channel_count))
    return jnp.stack(layers)


def stride_taps(padded, side_cells):
    channel_count = padded.shape[-1]
    layers = []
    for tap_row in range(3):
        for tap_col in range(3):
            window = padded[
                :, :, tap_row : tap_row + side_cells : 2, tap_col : tap_col + side_cells : 2, :
            ]
            layers.append(window.reshape(-1, channel_count))
    return jnp.stack(layers)


def weight_terms(grad_rows, slabs, cot_rows, hidden_padded, frame_count, side_cells):
    out_rows = grad_rows.shape[1]
    down_term = lax.dot_general(
        grad_rows, slabs, (((0,), (1,)), ((), ())), preferred_element_type=jnp.float32
    ).reshape(out_rows, -1)
    conv_parts = []
    for tap_time in range(3):
        group = time_group(hidden_padded, tap_time, frame_count, side_cells, False)
        conv_parts.append(
            lax.dot_general(
                cot_rows, group, (((0,), (1,)), ((), ())), preferred_element_type=jnp.float32
            )
        )
    conv_term = jnp.concatenate(conv_parts, axis=1).reshape(out_rows, -1)
    return (conv_term, down_term)


def transpose_conv(grad_padded, conv_weight, out_frames, side_cells):
    channel_count = grad_padded.shape[-1]
    row_total = grad_padded.shape[0] * out_frames * side_cells * side_cells
    initial = jnp.zeros((row_total, channel_count), jnp.float32)
    running = initial
    weight_panel = lax.all_gather(conv_weight, "fsdp", axis=0, tiled=True)
    panel_rows = weight_panel.shape[0]
    panel = weight_panel.reshape(panel_rows, 27, channel_count)
    for tap_time in range(3):
        group = time_group(grad_padded, tap_time, out_frames, side_cells, True)
        running = running + lax.dot_general(
            group,
            panel[:, 9 * tap_time : 9 * tap_time + 9, :],
            (((0, 2), (1, 0)), ((), ())),
            preferred_element_type=jnp.float32,
        )
    return running


def shards(video, conv_weight, down_weight, out_grad, clip_bucket, start_frame, bucket_res):
    clip_count, frame_count, side_cells, side_again, channel_count = video.shape
    half_side = side_cells // 2
    group_width = channel_count // GROUPS
    tiles = lax.axis_size("tile")
    mask, limits = valid_mask(
        clip_bucket,
        start_frame,
        bucket_res,
        lax.axis_index("tile") * frame_count,
        frame_count,
        side_cells,
    )
    valid_count = (
        (frame_count * tiles - start_frame) * limits[:, 0] * limits[:, 1] * group_width
    ).astype(jnp.float32)
    grouped_shape = (clip_count, frame_count, side_cells, side_cells, GROUPS, group_width)
    summed_axes = (1, 2, 3, 5)
    cell_weight = mask[..., None]
    grouped = video.astype(jnp.float32).reshape(grouped_shape)
    first_sum = lax.psum(jnp.sum(grouped * cell_weight, axis=summed_axes), "tile")
    centre = first_sum / valid_count[:, None]
    offset = grouped - centre[:, None, None, None, :, None]
    second_sum = lax.psum(jnp.sum(cell_weight * offset * offset, axis=summed_axes), "tile")
    spread = second_sum / valid_count[:, None]
    inverse = lax.rsqrt(spread + EPSILON)
    normed_grouped = offset * inverse[:, None, None, None, :, None]
    normed = normed_grouped.reshape(video.shape)
    hidden = (mask * jax.nn.silu(normed)).astype(jnp.bfloat16)
    past = shifted(hidden[:, frame_count - 2 :], "tile", 1)
    hidden_padded = jnp.pad(
        jnp.concatenate([past, hidden], axis=1), ((0, 0), (0, 0), (1, 1), (1, 1), (0, 0))
    )

    def conv_columns(weight_panel):
        panel = weight_panel.reshape(weight_panel.shape[0], 27, channel_count)
        summed = None
        for tap_time in range(3):
            group = time_group(hidden_padded, tap_time, frame_count, side_cells, False)
            term = lax.dot_general(
                group,
                panel[:, 9 * tap_time : 9 * tap_time + 9, :],
                (((0, 2), (1, 2)), ((), ())),
                preferred_element_type=jnp.float32,
            )
            summed = term if summed is None else summed + term
        return summed

    conv_out = conv_columns(lax.all_gather(conv_weight, "fsdp", axis=0, tiled=True))
    residual = (mask * (video.astype(jnp.float32) + conv_out.reshape(video.shape))).astype(
        jnp.bfloat16
    )
    down_slabs = stride_taps(
        jnp.pad(residual, ((0, 0), (0, 0), (0, 1), (0, 1), (0, 0))), side_cells
    )
    weight_panel = lax.all_gather(down_weight, "fsdp", axis=0, tiled=True)
    panel = weight_panel.reshape(weight_panel.shape[0], 9, channel_count)
    down_out = lax.dot_general(
        down_slabs, panel, (((0, 2), (1, 2)), ((), ())), preferred_element_type=jnp.float32
    )
    down = down_out.astype(jnp.bfloat16).reshape(
        clip_count, frame_count, half_side, half_side, channel_count
    )
    grad_flat = out_grad.reshape(-1, channel_count)
    weight_panel = lax.all_gather(down_weight, "fsdp", axis=0, tiled=True)
    panel_rows = weight_panel.shape[0]
    panel = weight_panel.reshape(panel_rows, 9, channel_count)
    tap_grads = lax.dot_general(
        grad_flat, panel, (((1,), (0,)), ((), ())), preferred_element_type=jnp.float32
    )
    spread_back = jnp.zeros(
        (clip_count, frame_count, side_cells + 1, side_cells + 1, channel_count), jnp.float32
    )
    for tap_row in range(3):
        for tap_col in range(3):
            term = tap_grads[:, tap_row * 3 + tap_col, :].reshape(
                clip_count, frame_count, half_side, half_side, channel_count
            )
            spread_back = spread_back.at[
                :, :, tap_row : tap_row + side_cells : 2, tap_col : tap_col + side_cells : 2, :
            ].add(term)
    res_grad = (mask * spread_back[:, :, :side_cells, :side_cells, :]).astype(jnp.bfloat16)
    res_flat = res_grad.reshape(-1, channel_count)
    later = shifted(res_grad[:, :2], "tile", -1)
    grad_padded = jnp.pad(
        jnp.concatenate([res_grad, later], axis=1), ((0, 0), (0, 0), (1, 1), (1, 1), (0, 0))
    )
    back_hidden = transpose_conv(grad_padded, conv_weight, frame_count, side_cells).reshape(
        video.shape
    )
    gate_value = jax.nn.sigmoid(normed)
    pushed = mask * back_hidden * gate_value * (1.0 + normed * (1.0 - gate_value))
    pushed_grouped = pushed.reshape(grouped_shape)
    push_sum, pair_sum = lax.psum(
        (
            jnp.sum(pushed_grouped, axis=summed_axes),
            jnp.sum(pushed_grouped * normed_grouped, axis=summed_axes),
        ),
        "tile",
    )
    mean_push = push_sum / valid_count[:, None]
    mean_pair = pair_sum / valid_count[:, None]
    through_norm = inverse[:, None, None, None, :, None] * (
        pushed_grouped
        - mean_push[:, None, None, None, :, None]
        - normed_grouped * mean_pair[:, None, None, None, :, None]
    )
    video_grad = (mask * through_norm.reshape(video.shape) + res_grad.astype(jnp.float32)).astype(
        jnp.bfloat16
    )
    conv_term, down_term = weight_terms(
        grad_flat, down_slabs, res_flat, hidden_padded, frame_count, side_cells
    )
    conv_share, down_share = (
        lax.psum_scatter(conv_term, ("fsdp", "tile"), scatter_dimension=0, tiled=True),
        lax.psum_scatter(down_term, ("fsdp", "tile"), scatter_dimension=0, tiled=True),
    )
    conv_weight_grad, down_weight_grad = (
        lax.all_gather(conv_share, "tile", axis=0, tiled=True),
        lax.all_gather(down_share, "tile", axis=0, tiled=True),
    )
    return (down, video_grad, conv_weight_grad, down_weight_grad)


F32 = jnp.float32
BF16 = jnp.bfloat16
MESH = pl.DeviceIdType.MESH
WIDE = 256
OWN = 32


def lane_swap():
    lane = np.arange(512)
    outer, inner, channel = lane // 128, lane // 32 % 4, lane % 32
    table = np.zeros((512, 512), np.float32)
    table[lane, inner * 128 + outer * 32 + channel] = 1.0
    return jnp.asarray(table, BF16)


def column_pick():
    table = np.zeros((2, 3, 256, 4, 4, 32), np.float32)
    for core in range(2):
        for tap in range(3):
            for chip in range(4):
                for channel in range(32):
                    table[core, tap, 64 * chip + 32 * core + channel, chip, tap, channel] = 1.0
    return jnp.asarray(table.reshape(2, 768, 512), BF16)


def dot(lhs, rhs):
    return jnp.dot(lhs, rhs, preferred_element_type=F32)


def dot_nt(lhs, rhs):
    return lax.dot_general(lhs, rhs, (((1,), (1,)), ((), ())), preferred_element_type=F32)


def move_cols(block, distance):
    if distance == 0:
        return block
    rows = block.shape[0]
    col = lax.broadcasted_iota(jnp.int32, block.shape, 0) % 8 + distance
    turned = pltpu.roll(block, (-distance) % rows, 0)
    return jnp.where((col >= 0) & (col < 8), turned, 0.0)


def fold_taps(result, outer, distances):
    parts = result.reshape(outer, 4, 8, 128)
    place = lax.broadcasted_iota(jnp.int32, (outer * 8, 128), 1) // OWN
    total = None
    for tap in range(3):
        layer = jnp.zeros((outer * 8, 128), F32)
        for clip in range(4):
            block = parts[:, clip].reshape(outer * 8, 128)
            turn = (OWN * (clip - tap)) % 128
            if turn:
                block = pltpu.roll(block, turn, 1)
            layer = jnp.where(place == clip, block, layer)
        layer = move_cols(layer, distances[tap])
        total = layer if total is None else total + layer
    return total


def group_total(row):
    first = lax.broadcasted_iota(jnp.int32, (128, 128), 0) // 8
    second = lax.broadcasted_iota(jnp.int32, (128, 128), 1) // 8
    same = (first == second).astype(F32)
    wide = jnp.broadcast_to(row, (8, 128))
    return jnp.dot(wide, same, preferred_element_type=F32, precision=lax.Precision.HIGHEST)[0:1]


def gathered_lanes(pieces, swap):
    halves = [
        dot(jnp.concatenate(pieces[4 * half : 4 * half + 4], axis=1), swap) for half in range(2)
    ]
    return [
        jnp.concatenate([half[:, 128 * p : 128 * p + 128] for half in halves], axis=1)
        for p in range(4)
    ]


def block_kernel(
    bucket_ref, start_ref, res_table_ref, video_ref, cw_hbm, dw_hbm, og_ref, swap_hbm,
    pick_hbm,
    x_all, d_all, h_out, r_out, stack_out, og_stack_out,
    meta_ref, cw_ref, dw_ref, swap_ref, pick_ref,
    meta_all, v_send, v_all, w_send, w_all, og_all, h_all, g_all, r_all, d_send,
    x_send, h_full, g_full, r_full, og_up, rows_fwd, cells, normed_ref, mask_ref,
    res_ref, stack_t, og_stack_t, back_ref, load_sems, send_sems, recv_sems,
):
    chip = lax.axis_index("fsdp")
    core = lax.axis_index("tile")
    me = chip * 2 + core
    sibling = chip * 2 + (1 - core)

    def peer(index):
        return {"fsdp": index // 2, "tile": index % 2}

    loads = {}
    for index, (name, source, target) in enumerate(
        (
            ("swap", swap_hbm, swap_ref),
            ("dw", dw_hbm, dw_ref),
            ("pick", pick_hbm.at[core], pick_ref),
            ("cw", cw_hbm, cw_ref),
        )
    ):
        loads[name] = pltpu.make_async_copy(source, target, load_sems.at[index])
        loads[name].start()

    barrier = pltpu.get_barrier_semaphore()
    for step in range(1, 8):
        pl.semaphore_signal(barrier, inc=1, device_id=peer((me + step) % 8), device_id_type=MESH)
    pl.semaphore_wait(barrier, 7)

    def send(phase, step, src, dst, to):
        copy = pltpu.make_async_remote_copy(
            src_ref=src, dst_ref=dst, send_sem=send_sems.at[phase, step],
            recv_sem=recv_sems.at[phase, step], device_id=peer(to), device_id_type=MESH,
        )
        copy.start()
        return copy

    def send_all(phase, source, target):
        return [send(phase, s, source((me + s) % 8), target, (me + s) % 8) for s in range(1, 8)]

    def spread_out(phase, target):
        copies = [send(phase, 4, target.at[me], target.at[me], sibling)]
        for s in range(1, 4):
            copies.append(send(phase, s, target.at[me], target.at[me], ((chip + s) % 4) * 2 + core))
        return copies

    def relay(phase, target, copies):
        passed = []
        for s in range(1, 4):
            copies[s].wait_recv()
            slot = ((chip + 4 - s) % 4) * 2 + core
            passed.append(send(phase, 4 + s, target.at[slot], target.at[slot], sibling))
        copies.extend(passed)

    def complete(copies):
        copies[0].wait_recv()
        for copy in copies[4:]:
            copy.wait_recv()

    def arrived(copies):
        for copy in copies:
            copy.wait_recv()

    bucket = bucket_ref[0]
    high, width = jnp.int32(0), jnp.int32(0)
    for index in range(res_table_ref.shape[1]):
        high = high + jnp.where(bucket == index, res_table_ref[0, index], 0)
        width = width + jnp.where(bucket == index, res_table_ref[1, index], 0)
    line = lax.broadcasted_iota(jnp.int32, (8, 128), 0)
    facts = jnp.where(line == 0, start_ref[0], jnp.where(line == 1, high, width)).astype(F32)
    meta_ref[...] = facts
    meta_all[chip] = facts
    meta_copies = [
        send(3, s, meta_ref, meta_all.at[chip], ((chip + s) % 4) * 2 + core) for s in range(1, 4)
    ]
    loads["swap"].wait()
    halves = []
    for half in range(2):
        halves.append(
            jnp.concatenate(
                [video_ref[64 * t : 64 * t + 64, 128 * half : 128 * half + 128] for t in range(4)],
                axis=1,
            )
        )
    packed = dot(jnp.concatenate(halves, axis=0), swap_ref[...]).astype(BF16)
    for index in range(8):
        half, quarter = index // 4, index % 4
        v_send[index] = packed[64 * half : 64 * half + 64, 128 * quarter : 128 * quarter + 128]
    v_copies = send_all(0, lambda to: v_send.at[to], v_all.at[me])
    v_all[me] = v_send[me]
    og_all[me] = og_ref[0].astype(F32).reshape(64, WIDE).astype(BF16)
    og_copies = spread_out(1, og_all)

    loads["dw"].wait()
    loads["pick"].wait()

    def exchange_columns(phase, ref, blocks, first):
        picks = None
        for tap in range(3):
            at = [(3 * block + tap) * WIDE for block in range(blocks)]
            rows = jnp.concatenate([ref[:, low : low + WIDE] for low in at], axis=0)
            term = dot(rows, pick_ref[256 * tap : 256 * tap + 256, :])
            picks = term if picks is None else picks + term
        part = pl.ds(first, 64 * blocks)
        for other in range(4):
            w_send[other, part, :] = picks[:, 128 * other : 128 * other + 128].astype(BF16)
        w_all[chip, part, :] = w_send[chip, part, :]
        copies = []
        for s in range(1, 4):
            to = (chip + s) % 4
            copies.append(
                send(phase, s, w_send.at[to, part], w_all.at[chip, part], to * 2 + core)
            )
        return copies

    dw_copies = exchange_columns(2, dw_ref, 3, 576)

    arrived(meta_copies)
    place1 = lax.broadcasted_iota(jnp.int32, (1, 128), 1) // OWN
    start = jnp.zeros((1, 128), F32)
    high = jnp.zeros((1, 128), F32)
    width = jnp.zeros((1, 128), F32)
    for clip in range(4):
        start = jnp.where(place1 == clip, meta_all[clip, 0:1, :], start)
        high = jnp.where(place1 == clip, meta_all[clip, 1:2, :], high)
        width = jnp.where(place1 == clip, meta_all[clip, 2:3, :], width)
    count = (8.0 - start) * high * width * 8.0
    row_id = lax.broadcasted_iota(jnp.int32, (512, 128), 0)
    in_time = (row_id // 64).astype(F32) >= start
    in_rows = (row_id // 8 % 8).astype(F32) < high
    in_cols = (row_id % 8).astype(F32) < width
    mask_ref[...] = jnp.where(in_time & in_rows & in_cols, 1.0, 0.0)

    arrived(v_copies)
    stacked = jnp.concatenate(
        [
            jnp.concatenate([v_all[2 * other + c] for other in range(4)], axis=1)
            for c in range(2)
        ],
        axis=0,
    )
    unpacked = dot(stacked, swap_ref[...])
    for t in range(8):
        c, q = t // 4, t % 4
        cells[64 * t : 64 * t + 64, :] = unpacked[64 * c : 64 * c + 64, 128 * q : 128 * q + 128]
    mask = mask_ref[...]
    centre = group_total(jnp.sum(mask * cells[...], axis=0, keepdims=True)) / count
    offset = cells[...] - centre
    spread = group_total(jnp.sum(mask * offset * offset, axis=0, keepdims=True)) / count
    inverse = lax.rsqrt(spread + EPSILON)
    normed = offset * inverse
    normed_ref[...] = normed
    h_all[me] = (mask * (normed / (1.0 + jnp.exp(-normed)))).astype(BF16)
    h_copies = spread_out(4, h_all)

    relay(1, og_all, og_copies)
    complete(og_copies)
    up_row = lax.broadcasted_iota(jnp.int32, (128, 64), 0)
    up_col = lax.broadcasted_iota(jnp.int32, (128, 64), 1)
    lift = ((up_row // 8 == up_col // 4) & (up_row % 8 == 2 * (up_col % 4))).astype(F32).astype(BF16)
    for c in range(2):
        raised = [dot(lift, og_all[2 * clip + c]).reshape(16, 8, WIDE) for clip in range(4)]
        og_up[4 * c : 4 * c + 4] = (
            jnp.concatenate(raised, axis=1).astype(BF16).reshape(4, 4, 32, WIDE)
        )
    arrived(dw_copies)

    def res_grad_frame(t, carry):
        lhs = og_up[t].reshape(128, WIDE)
        layers = []
        for b in range(3):
            panel = w_all[:, 64 * (9 + b) : 64 * (10 + b), :].reshape(256, 128)
            layers.append(fold_taps(dot(lhs, panel), 4, (0, -1, -2)).reshape(4, 8, 128))
        even = layers[0] + jnp.concatenate([jnp.zeros((1, 8, 128), F32), layers[2][:3]], axis=0)
        both = jnp.stack([even, layers[1]], axis=1).reshape(64, 128)
        at = pl.ds(pl.multiple_of(64 * t, 64), 64)
        value = (mask_ref[at, :] * both).astype(BF16)
        g_all[me, at, :] = value
        wide = value.astype(F32)
        res_ref[at, :] = wide
        return carry

    lax.fori_loop(0, 8, res_grad_frame, 0)
    g_copies = spread_out(5, g_all)

    loads["cw"].wait()
    cw_copies = exchange_columns(10, cw_ref, 9, 0)

    mine = pl.ds(pl.multiple_of(core * OWN, OWN), OWN)
    for ab in range(9):
        for tap in range(3):
            at = (3 * ab + tap) * WIDE
            rows_fwd[ab, 32 * tap : 32 * tap + 32, :] = cw_ref[mine, at : at + WIDE]
        rows_fwd[ab, 96:128, :] = jnp.zeros((32, WIDE), BF16)
    for b in range(3):
        for tap in range(3):
            at = (3 * b + tap) * WIDE
            rows_fwd[9 + b, 32 * tap : 32 * tap + 32, :] = dw_ref[mine, at : at + WIDE]
        rows_fwd[9 + b, 96:128, :] = jnp.zeros((32, WIDE), BF16)

    edge = jnp.zeros((10, 32, WIDE), BF16)
    for t in range(2):
        h_full[t] = edge
        g_full[8 + t] = edge
    for t in range(8):
        for full, off in ((h_full, 2), (g_full, 0)):
            full[t + off, 0] = jnp.zeros((32, WIDE), BF16)
            full[t + off, 9] = jnp.zeros((32, WIDE), BF16)
        r_full[t, 4, 0] = jnp.zeros((32, WIDE), BF16)

    def og_frame(t, carry):
        from_row = lax.broadcasted_iota(jnp.int32, (WIDE, WIDE), 0)
        to_lane = lax.broadcasted_iota(jnp.int32, (WIDE, WIDE), 1)
        chosen = (from_row == to_lane % 64 + 64 * chip).astype(F32).astype(BF16)
        rows = dot(og_up[t].reshape(128, WIDE), chosen)
        tap = lax.broadcasted_iota(jnp.int32, (128, WIDE), 1) // 64
        once, twice = move_cols(rows, -1), move_cols(rows, -2)
        rows = jnp.where(tap == 0, rows, jnp.where(tap == 1, once, twice))
        og_stack_t[t] = rows.T.astype(BF16)
        return carry

    lax.fori_loop(0, 8, og_frame, 0)

    def keep(index, source, target):
        copy = pltpu.make_async_copy(source, target, load_sems.at[index])
        copy.start()
        return copy

    kept = [keep(4, og_stack_t, og_stack_out)]

    def assemble(source, t):
        at = pl.ds(pl.multiple_of(256 * t, 256), 256)
        clips = gathered_lanes([source[d, at, :] for d in range(8)], swap_ref[...])
        blocks = [clip.reshape(32, 8, WIDE) for clip in clips]
        return jnp.concatenate(blocks, axis=1).astype(BF16).reshape(4, 8, 32, WIDE)

    relay(4, h_all, h_copies)
    complete(h_copies)

    def fill_hidden(t, carry):
        h_full[pl.ds(4 * t + 2, 4), 1:9] = assemble(h_all, t)
        return carry

    lax.fori_loop(0, 2, fill_hidden, 0)
    kept.append(keep(5, h_full, h_out))

    def conv_frame(t, carry):
        total = None
        for a in range(3):
            for b in range(3):
                window = h_full[t + a, b : b + 8].reshape(256, WIDE)
                term = dot_nt(window, rows_fwd[3 * a + b])
                total = term if total is None else total + term
        folded = fold_taps(total, 8, (-1, 0, 1))
        at = pl.ds(pl.multiple_of(64 * t, 64), 64)
        r_all[me, at, :] = (mask_ref[at, :] * (cells[at, :] + folded)).astype(BF16)
        return carry

    lax.fori_loop(0, 4, conv_frame, 0)
    relay(5, g_all, g_copies)
    lax.fori_loop(4, 8, conv_frame, 0)
    r_copies = spread_out(6, r_all)

    complete(g_copies)

    def fill_grad(t, carry):
        g_full[pl.ds(4 * t, 4), 1:9] = assemble(g_all, t)
        return carry

    lax.fori_loop(0, 2, fill_grad, 0)

    arrived(cw_copies)

    def back_frame(t, carry):
        total = None
        for a in range(3):
            for b in range(3):
                window = g_full[t + 2 - a, 2 - b : 10 - b].reshape(256, WIDE)
                at = 64 * (3 * a + b)
                term = dot(window, w_all[:, at : at + 64, :].reshape(256, 128))
                total = term if total is None else total + term
        at = pl.ds(pl.multiple_of(64 * t, 64), 64)
        back_ref[at, :] = fold_taps(total, 8, (1, 0, -1))
        return carry

    lax.fori_loop(0, 8, back_frame, 0)
    mask = mask_ref[...]
    normed = normed_ref[...]
    gate = 1.0 / (1.0 + jnp.exp(-normed))
    pushed = mask * back_ref[...] * gate * (1.0 + normed * (1.0 - gate))
    mean_push = group_total(jnp.sum(pushed, axis=0, keepdims=True)) / count
    mean_pair = group_total(jnp.sum(pushed * normed, axis=0, keepdims=True)) / count
    through = inverse * (pushed - mean_push - normed * mean_pair)
    back_ref[...] = mask * through + res_ref[...]
    for c in range(2):
        quarter = [back_ref[64 * (4 * c + q) : 64 * (4 * c + q) + 64, :] for q in range(4)]
        swapped = dot(jnp.concatenate(quarter, axis=1).astype(BF16), swap_ref[...]).astype(BF16)
        for other in range(4):
            x_send[2 * other + c] = swapped[:, 128 * other : 128 * other + 128]
    x_all[me] = x_send[me]
    x_copies = send_all(8, lambda to: x_send.at[to], x_all.at[me])

    relay(6, r_all, r_copies)
    place = lax.broadcasted_iota(jnp.int32, (64, 128), 1) // OWN

    def stack_frame(t, carry):
        at = pl.ds(pl.multiple_of(64 * t, 64), 64)
        moved = []
        for c in range(2):
            block = g_all[2 * chip + c, at, :].astype(F32)
            moved.append([move_cols(block, 1 - tap) for tap in range(3)])
        split = []
        for clip in range(4):
            sides = [jnp.zeros((64, 128), F32)] * 2
            for tap in range(3):
                for c in range(2):
                    spot = 2 * (tap % 2) + c
                    turn = (OWN * (spot - clip)) % 128
                    block = moved[c][tap]
                    if turn:
                        block = pltpu.roll(block, turn, 1)
                    sides[tap // 2] = jnp.where(place == spot, block, sides[tap // 2])
            split.append(jnp.concatenate(sides, axis=1).reshape(8, 8, WIDE))
        rows = jnp.concatenate(split, axis=1).reshape(256, WIDE)
        stack_t[t] = rows.T.astype(BF16)
        return carry

    lax.fori_loop(0, 8, stack_frame, 0)
    kept.append(keep(6, stack_t, stack_out))

    complete(r_copies)

    def fill_residual(t, carry):
        r_full[pl.ds(4 * t, 4), 0:4] = assemble(r_all, t).reshape(4, 4, 2, 32, WIDE)
        return carry

    lax.fori_loop(0, 2, fill_residual, 0)
    kept.append(keep(7, r_full, r_out))

    def down_frame(t, carry):
        total = None
        for b in range(3):
            window = r_full[t, b // 2 : b // 2 + 4, b % 2].reshape(128, WIDE)
            term = dot_nt(window, rows_fwd[9 + b])
            total = term if total is None else total + term
        folded = fold_taps(total, 4, (0, 1, 2)).astype(BF16)
        to_row = lax.broadcasted_iota(jnp.int32, (16, 32), 0)
        from_row = lax.broadcasted_iota(jnp.int32, (16, 32), 1)
        even = (from_row == to_row * 2).astype(F32).astype(BF16)
        d_send[t] = dot(even, folded).astype(BF16)
        return carry

    lax.fori_loop(0, 8, down_frame, 0)

    def frames_of(to):
        return pl.ds(4 * (to % 2), 4)

    d_all[me] = d_send[frames_of(me)]
    d_copies = send_all(7, lambda to: d_send.at[frames_of(to)], d_all.at[me])
    arrived(x_copies)
    arrived(d_copies)
    for copy in kept:
        copy.wait()
    for copies in (
        meta_copies, v_copies, og_copies, dw_copies, cw_copies, h_copies, g_copies, r_copies, x_copies,
        d_copies,
    ):
        for copy in copies:
            copy.wait_send()


def finish_kernel(
    x_hbm, d_hbm, h_hbm, r_hbm, stack_hbm, og_stack_hbm, swap_hbm,
    down_ref, vgrad_ref, cgrad_hbm, dgrad_hbm,
    x_all, d_all, h_full, r_full, stack_t, og_stack_t, swap_ref, cgrad_ref, dgrad_ref,
    load_sems, store_sems,
):
    chip = lax.axis_index("fsdp")
    loads = []
    for index, (source, target) in enumerate(
        (
            (swap_hbm, swap_ref),
            (x_hbm, x_all),
            (d_hbm, d_all),
            (stack_hbm, stack_t),
            (h_hbm, h_full),
            (og_stack_hbm, og_stack_t),
            (r_hbm, r_full),
        )
    ):
        loads.append(pltpu.make_async_copy(source, target, load_sems.at[index]))
        loads[-1].start()
    for copy in loads[:3]:
        copy.wait()
    frames = gathered_lanes([x_all[d] for d in range(8)], swap_ref[...])
    for t, block in enumerate(frames):
        vgrad_ref[64 * t : 64 * t + 64, :] = block.astype(BF16)
    clips = gathered_lanes([d_all[d].reshape(64, 128) for d in range(8)], swap_ref[...])
    own = clips[0]
    for clip in range(1, 4):
        own = jnp.where(chip == clip, clips[clip], own)
    down_ref[0] = own.reshape(4, 4, 4, WIDE).astype(BF16)

    stores = []

    def put(grad, ref, hbm, block, index):
        for tap in range(3):
            at = (3 * block + tap) * WIDE
            ref[:, at : at + WIDE] = grad[64 * tap : 64 * tap + 64]
        part = pl.ds(3 * block * WIDE, 3 * WIDE)
        stores.append(pltpu.make_async_copy(ref.at[:, part], hbm.at[:, part], store_sems.at[index]))
        stores[-1].start()

    loads[3].wait()
    loads[4].wait()
    lhs = jnp.concatenate([stack_t[t, 0:192] for t in range(8)], axis=1)
    for a in range(3):
        for b in range(3):
            rhs = h_full[a : a + 8, b : b + 8].reshape(2048, WIDE)
            put(dot(lhs, rhs), cgrad_ref, cgrad_hbm, 3 * a + b, 3 * a + b)
    loads[5].wait()
    loads[6].wait()
    lhs = jnp.concatenate([og_stack_t[t, 0:192] for t in range(8)], axis=1)
    for b in range(3):
        rhs = r_full[:, b // 2 : b // 2 + 4, b % 2].reshape(1024, WIDE)
        put(dot(lhs, rhs), dgrad_ref, dgrad_hbm, b, 9 + b)
    for copy in stores:
        copy.wait()


def fused(video, conv_weight, down_weight, out_grad, clip_bucket, start_frame, bucket_res):
    vmem = pl.BlockSpec(memory_space=pltpu.VMEM)
    smem = pl.BlockSpec(memory_space=pltpu.SMEM)
    anywhere = pl.BlockSpec(memory_space=pl.ANY)
    full = pltpu.VMEM((10, 10, 32, WIDE), BF16)
    gathered = pltpu.VMEM((8, 512, 128), BF16)
    wide = pltpu.VMEM((512, 128), F32)
    piece = pltpu.VMEM((8, 64, 128), BF16)
    sent = jax.ShapeDtypeStruct((8, 64, 128), BF16)
    sent_down = jax.ShapeDtypeStruct((8, 4, 16, 128), BF16)
    full_cells = jax.ShapeDtypeStruct((10, 10, 32, WIDE), BF16)
    even_cells = jax.ShapeDtypeStruct((8, 5, 2, 32, WIDE), BF16)
    stack = jax.ShapeDtypeStruct((8, 256, 256), BF16)
    og_stack = jax.ShapeDtypeStruct((8, 256, 128), BF16)
    swap = lane_swap()
    parts = pl.pallas_call(
        block_kernel,
        out_shape=(sent, sent_down, full_cells, even_cells, stack, og_stack),
        in_specs=[smem] * 3 + [vmem, anywhere, anywhere, vmem] + [anywhere] * 2,
        out_specs=(vmem,) * 2 + (anywhere,) * 4,
        scratch_shapes=[
            pltpu.VMEM((8, 128), F32),
            pltpu.VMEM(conv_weight.shape, BF16),
            pltpu.VMEM(down_weight.shape, BF16),
            pltpu.VMEM((512, 512), BF16),
            pltpu.VMEM((768, 512), BF16),
            pltpu.VMEM((4, 8, 128), F32),
            piece,
            piece,
            pltpu.VMEM((4, 768, 128), BF16),
            pltpu.VMEM((4, 768, 128), BF16),
            pltpu.VMEM((8, 64, WIDE), BF16),
            gathered,
            gathered,
            gathered,
            pltpu.VMEM((8, 16, 128), BF16),
            piece,
            full,
            full,
            pltpu.VMEM((8, 5, 2, 32, WIDE), BF16),
            pltpu.VMEM((8, 4, 32, WIDE), BF16),
            pltpu.VMEM((12, 128, WIDE), BF16),
            wide,
            wide,
            wide,
            wide,
            pltpu.VMEM((8, 256, 256), BF16),
            pltpu.VMEM((8, 256, 128), BF16),
            wide,
            pltpu.SemaphoreType.DMA((8,)),
            pltpu.SemaphoreType.DMA((11, 8)),
            pltpu.SemaphoreType.DMA((11, 8)),
        ],
        compiler_params=pltpu.CompilerParams(
            collective_id=0, has_side_effects=True, vmem_limit_bytes=60 * 2**20
        ),
    )(
        clip_bucket,
        start_frame,
        bucket_res.T,
        video.reshape(256, WIDE),
        conv_weight,
        down_weight,
        out_grad,
        swap,
        column_pick(),
    )
    kinds = (sent, sent_down, full_cells, even_cells, stack, og_stack, swap)
    down, video_grad, conv_grad, down_grad = pl.pallas_call(
        finish_kernel,
        out_shape=(
            jax.ShapeDtypeStruct(out_grad.shape, BF16),
            jax.ShapeDtypeStruct((256, WIDE), BF16),
            jax.ShapeDtypeStruct(conv_weight.shape, F32),
            jax.ShapeDtypeStruct(down_weight.shape, F32),
        ),
        in_specs=[anywhere] * 7,
        out_specs=(vmem, vmem, anywhere, anywhere),
        scratch_shapes=[pltpu.VMEM(kind.shape, BF16) for kind in kinds]
        + [
            pltpu.VMEM(conv_weight.shape, F32),
            pltpu.VMEM(down_weight.shape, F32),
            pltpu.SemaphoreType.DMA((7,)),
            pltpu.SemaphoreType.DMA((12,)),
        ],
        compiler_params=pltpu.CompilerParams(vmem_limit_bytes=60 * 2**20),
    )(*parts, swap)
    return (down, video_grad.reshape(video.shape), conv_grad, down_grad)


def solution(mesh):
    placed = (
        P(("mix", "fsdp"), "tile", None, None, None),
        P(("mix", "fsdp"), None),
        P(("mix", "fsdp"), None),
        P(("mix", "fsdp"), "tile", None, None, None),
        P(("mix", "fsdp")),
        P(("mix", "fsdp")),
        P(),
    )
    return jax.shard_map(
        fused if mesh.shape["tile"] == 2 and mesh.shape["fsdp"] == 4 else shards,
        mesh=mesh,
        in_specs=placed,
        out_specs=(
            P(("mix", "fsdp"), "tile", None, None, None),
            P(("mix", "fsdp"), "tile", None, None, None),
            P(("mix", "fsdp"), None),
            P(("mix", "fsdp"), None),
        ),
        check_vma=False,
    )
```

```python
import functools

import jax
import jax.numpy as jnp
import numpy as np
from jax import lax
from jax.experimental import pallas as pl
from jax.experimental.pallas import tpu as pltpu
from jax.sharding import PartitionSpec as P

GROUPS = 32


EPSILON = 1e-06


def shifted(block, axis, distance):
    devices = range(lax.axis_size(axis))
    route = [(i - distance, i) for i in devices if i - distance in devices]
    return lax.ppermute(block, axis, route)


def valid_mask(clip_bucket, start_frame, bucket_res, first_frame, frame_count, side_cells):
    bucket_ids = jnp.arange(bucket_res.shape[0], dtype=jnp.int32)
    picked = (clip_bucket[:, None] == bucket_ids[None, :]).astype(jnp.int32)
    limits = jnp.sum(picked[:, :, None] * bucket_res[None, :, :], axis=1)
    frame_ids = first_frame + jnp.arange(frame_count, dtype=jnp.int32)
    positions = jnp.arange(side_cells, dtype=jnp.int32)
    in_time = frame_ids[None, :] >= start_frame[:, None]
    in_rows = positions[None, :] < limits[:, 0:1]
    in_cols = positions[None, :] < limits[:, 1:2]
    inside = in_time[:, :, None, None] & in_rows[:, None, :, None] & in_cols[:, None, None, :]
    return (inside.astype(jnp.float32)[..., None], limits)


def time_group(padded, tap_time, out_frames, side_cells, flipped):
    channel_count = padded.shape[-1]
    time_start = 2 - tap_time if flipped else tap_time
    layers = []
    for tap_row in range(3):
        for tap_col in range(3):
            row_start = 2 - tap_row if flipped else tap_row
            col_start = 2 - tap_col if flipped else tap_col
            window = padded[
                :,
                time_start : time_start + out_frames,
                row_start : row_start + side_cells,
                col_start : col_start + side_cells,
                :,
            ]
            layers.append(window.reshape(-1, channel_count))
    return jnp.stack(layers)


def stride_taps(padded, side_cells):
    channel_count = padded.shape[-1]
    layers = []
    for tap_row in range(3):
        for tap_col in range(3):
            window = padded[
                :, :, tap_row : tap_row + side_cells : 2, tap_col : tap_col + side_cells : 2, :
            ]
            layers.append(window.reshape(-1, channel_count))
    return jnp.stack(layers)


def weight_terms(grad_rows, slabs, cot_rows, hidden_padded, frame_count, side_cells):
    out_rows = grad_rows.shape[1]
    down_term = lax.dot_general(
        grad_rows, slabs, (((0,), (1,)), ((), ())), preferred_element_type=jnp.float32
    ).reshape(out_rows, -1)
    conv_parts = []
    for tap_time in range(3):
        group = time_group(hidden_padded, tap_time, frame_count, side_cells, False)
        conv_parts.append(
            lax.dot_general(
                cot_rows, group, (((0,), (1,)), ((), ())), preferred_element_type=jnp.float32
            )
        )
    conv_term = jnp.concatenate(conv_parts, axis=1).reshape(out_rows, -1)
    return (conv_term, down_term)


def transpose_conv(grad_padded, conv_weight, out_frames, side_cells):
    channel_count = grad_padded.shape[-1]
    row_total = grad_padded.shape[0] * out_frames * side_cells * side_cells
    initial = jnp.zeros((row_total, channel_count), jnp.float32)
    running = initial
    weight_panel = lax.all_gather(conv_weight, "fsdp", axis=0, tiled=True)
    panel_rows = weight_panel.shape[0]
    panel = weight_panel.reshape(panel_rows, 27, channel_count)
    for tap_time in range(3):
        group = time_group(grad_padded, tap_time, out_frames, side_cells, True)
        running = running + lax.dot_general(
            group,
            panel[:, 9 * tap_time : 9 * tap_time + 9, :],
            (((0, 2), (1, 0)), ((), ())),
            preferred_element_type=jnp.float32,
        )
    return running


def shards(video, conv_weight, down_weight, out_grad, clip_bucket, start_frame, bucket_res):
    clip_count, frame_count, side_cells, side_again, channel_count = video.shape
    half_side = side_cells // 2
    group_width = channel_count // GROUPS
    tiles = lax.axis_size("tile")
    mask, limits = valid_mask(
        clip_bucket,
        start_frame,
        bucket_res,
        lax.axis_index("tile") * frame_count,
        frame_count,
        side_cells,
    )
    valid_count = (
        (frame_count * tiles - start_frame) * limits[:, 0] * limits[:, 1] * group_width
    ).astype(jnp.float32)
    grouped_shape = (clip_count, frame_count, side_cells, side_cells, GROUPS, group_width)
    summed_axes = (1, 2, 3, 5)
    cell_weight = mask[..., None]
    grouped = video.astype(jnp.float32).reshape(grouped_shape)
    first_sum = lax.psum(jnp.sum(grouped * cell_weight, axis=summed_axes), "tile")
    centre = first_sum / valid_count[:, None]
    offset = grouped - centre[:, None, None, None, :, None]
    second_sum = lax.psum(jnp.sum(cell_weight * offset * offset, axis=summed_axes), "tile")
    spread = second_sum / valid_count[:, None]
    inverse = lax.rsqrt(spread + EPSILON)
    normed_grouped = offset * inverse[:, None, None, None, :, None]
    normed = normed_grouped.reshape(video.shape)
    hidden = (mask * jax.nn.silu(normed)).astype(jnp.bfloat16)
    past = shifted(hidden[:, frame_count - 2 :], "tile", 1)
    hidden_padded = jnp.pad(
        jnp.concatenate([past, hidden], axis=1), ((0, 0), (0, 0), (1, 1), (1, 1), (0, 0))
    )

    def conv_columns(weight_panel):
        panel = weight_panel.reshape(weight_panel.shape[0], 27, channel_count)
        summed = None
        for tap_time in range(3):
            group = time_group(hidden_padded, tap_time, frame_count, side_cells, False)
            term = lax.dot_general(
                group,
                panel[:, 9 * tap_time : 9 * tap_time + 9, :],
                (((0, 2), (1, 2)), ((), ())),
                preferred_element_type=jnp.float32,
            )
            summed = term if summed is None else summed + term
        return summed

    conv_out = conv_columns(lax.all_gather(conv_weight, "fsdp", axis=0, tiled=True))
    residual = (mask * (video.astype(jnp.float32) + conv_out.reshape(video.shape))).astype(
        jnp.bfloat16
    )
    down_slabs = stride_taps(
        jnp.pad(residual, ((0, 0), (0, 0), (0, 1), (0, 1), (0, 0))), side_cells
    )
    weight_panel = lax.all_gather(down_weight, "fsdp", axis=0, tiled=True)
    panel = weight_panel.reshape(weight_panel.shape[0], 9, channel_count)
    down_out = lax.dot_general(
        down_slabs, panel, (((0, 2), (1, 2)), ((), ())), preferred_element_type=jnp.float32
    )
    down = down_out.astype(jnp.bfloat16).reshape(
        clip_count, frame_count, half_side, half_side, channel_count
    )
    grad_flat = out_grad.reshape(-1, channel_count)
    weight_panel = lax.all_gather(down_weight, "fsdp", axis=0, tiled=True)
    panel_rows = weight_panel.shape[0]
    panel = weight_panel.reshape(panel_rows, 9, channel_count)
    tap_grads = lax.dot_general(
        grad_flat, panel, (((1,), (0,)), ((), ())), preferred_element_type=jnp.float32
    )
    spread_back = jnp.zeros(
        (clip_count, frame_count, side_cells + 1, side_cells + 1, channel_count), jnp.float32
    )
    for tap_row in range(3):
        for tap_col in range(3):
            term = tap_grads[:, tap_row * 3 + tap_col, :].reshape(
                clip_count, frame_count, half_side, half_side, channel_count
            )
            spread_back = spread_back.at[
                :, :, tap_row : tap_row + side_cells : 2, tap_col : tap_col + side_cells : 2, :
            ].add(term)
    res_grad = (mask * spread_back[:, :, :side_cells, :side_cells, :]).astype(jnp.bfloat16)
    res_flat = res_grad.reshape(-1, channel_count)
    later = shifted(res_grad[:, :2], "tile", -1)
    grad_padded = jnp.pad(
        jnp.concatenate([res_grad, later], axis=1), ((0, 0), (0, 0), (1, 1), (1, 1), (0, 0))
    )
    back_hidden = transpose_conv(grad_padded, conv_weight, frame_count, side_cells).reshape(
        video.shape
    )
    gate_value = jax.nn.sigmoid(normed)
    pushed = mask * back_hidden * gate_value * (1.0 + normed * (1.0 - gate_value))
    pushed_grouped = pushed.reshape(grouped_shape)
    push_sum, pair_sum = lax.psum(
        (
            jnp.sum(pushed_grouped, axis=summed_axes),
            jnp.sum(pushed_grouped * normed_grouped, axis=summed_axes),
        ),
        "tile",
    )
    mean_push = push_sum / valid_count[:, None]
    mean_pair = pair_sum / valid_count[:, None]
    through_norm = inverse[:, None, None, None, :, None] * (
        pushed_grouped
        - mean_push[:, None, None, None, :, None]
        - normed_grouped * mean_pair[:, None, None, None, :, None]
    )
    video_grad = (mask * through_norm.reshape(video.shape) + res_grad.astype(jnp.float32)).astype(
        jnp.bfloat16
    )
    conv_term, down_term = weight_terms(
        grad_flat, down_slabs, res_flat, hidden_padded, frame_count, side_cells
    )
    conv_share, down_share = (
        lax.psum_scatter(conv_term, ("fsdp", "tile"), scatter_dimension=0, tiled=True),
        lax.psum_scatter(down_term, ("fsdp", "tile"), scatter_dimension=0, tiled=True),
    )
    conv_weight_grad, down_weight_grad = (
        lax.all_gather(conv_share, "tile", axis=0, tiled=True),
        lax.all_gather(down_share, "tile", axis=0, tiled=True),
    )
    return (down, video_grad, conv_weight_grad, down_weight_grad)


F32 = jnp.float32
BF16 = jnp.bfloat16
MESH = pl.DeviceIdType.MESH
WIDE = 256
OWN = 32


def lane_swap():
    lane = np.arange(512)
    outer, inner, channel = lane // 128, lane // 32 % 4, lane % 32
    table = np.zeros((512, 512), np.float32)
    table[lane, inner * 128 + outer * 32 + channel] = 1.0
    return jnp.asarray(table, BF16)


def column_pick():
    table = np.zeros((2, 3, 256, 4, 4, 32), np.float32)
    for core in range(2):
        for tap in range(3):
            for chip in range(4):
                for channel in range(32):
                    table[core, tap, 64 * chip + 32 * core + channel, chip, tap, channel] = 1.0
    return jnp.asarray(table.reshape(2, 768, 512), BF16)


def dot(lhs, rhs):
    return jnp.dot(lhs, rhs, preferred_element_type=F32)


def dot_nt(lhs, rhs):
    return lax.dot_general(lhs, rhs, (((1,), (1,)), ((), ())), preferred_element_type=F32)


def move_cols(block, distance):
    if distance == 0:
        return block
    rows = block.shape[0]
    col = lax.broadcasted_iota(jnp.int32, block.shape, 0) % 8 + distance
    turned = pltpu.roll(block, (-distance) % rows, 0)
    return jnp.where((col >= 0) & (col < 8), turned, 0.0)


def fold_taps(result, outer, distances):
    parts = result.reshape(outer, 4, 8, 128)
    place = lax.broadcasted_iota(jnp.int32, (outer * 8, 128), 1) // OWN
    total = None
    for tap in range(3):
        layer = jnp.zeros((outer * 8, 128), F32)
        for clip in range(4):
            block = parts[:, clip].reshape(outer * 8, 128)
            turn = (OWN * (clip - tap)) % 128
            if turn:
                block = pltpu.roll(block, turn, 1)
            layer = jnp.where(place == clip, block, layer)
        layer = move_cols(layer, distances[tap])
        total = layer if total is None else total + layer
    return total


def group_total(row):
    first = lax.broadcasted_iota(jnp.int32, (128, 128), 0) // 8
    second = lax.broadcasted_iota(jnp.int32, (128, 128), 1) // 8
    same = (first == second).astype(F32)
    wide = jnp.broadcast_to(row, (8, 128))
    return jnp.dot(wide, same, preferred_element_type=F32, precision=lax.Precision.HIGHEST)[0:1]


def gathered_lanes(pieces, swap):
    halves = [
        dot(jnp.concatenate(pieces[4 * half : 4 * half + 4], axis=1), swap) for half in range(2)
    ]
    return [
        jnp.concatenate([half[:, 128 * p : 128 * p + 128] for half in halves], axis=1)
        for p in range(4)
    ]


def block_kernel(
    bucket_ref, start_ref, res_table_ref, video_ref, cw_hbm, dw_hbm, og_ref, swap_hbm,
    pick_hbm,
    x_all, d_all, h_out, r_out, stack_out, og_stack_out,
    meta_ref, cw_ref, dw_ref, swap_ref, pick_ref,
    meta_all, v_send, v_all, w_send, w_all, og_all, h_all, g_all, r_all, d_send,
    x_send, p_send, p_all, h_full, g_full, r_full, rows_back, og_up, rows_fwd, cells, normed_ref, mask_ref,
    res_ref, stack_t, og_stack_t, back_ref, load_sems, send_sems, recv_sems,
):
    chip = lax.axis_index("fsdp")
    core = lax.axis_index("tile")
    me = chip * 2 + core
    sibling = chip * 2 + (1 - core)

    def peer(index):
        return {"fsdp": index // 2, "tile": index % 2}

    loads = {}
    for index, (name, source, target) in enumerate(
        (
            ("swap", swap_hbm, swap_ref),
            ("dw", dw_hbm, dw_ref),
            ("pick", pick_hbm.at[core], pick_ref),
            ("cw", cw_hbm, cw_ref),
        )
    ):
        loads[name] = pltpu.make_async_copy(source, target, load_sems.at[index])
        loads[name].start()

    barrier = pltpu.get_barrier_semaphore()
    for step in range(1, 8):
        pl.semaphore_signal(barrier, inc=1, device_id=peer((me + step) % 8), device_id_type=MESH)
    pl.semaphore_wait(barrier, 7)

    def send(phase, step, src, dst, to):
        copy = pltpu.make_async_remote_copy(
            src_ref=src, dst_ref=dst, send_sem=send_sems.at[phase, step],
            recv_sem=recv_sems.at[phase, step], device_id=peer(to), device_id_type=MESH,
        )
        copy.start()
        return copy

    def send_all(phase, source, target):
        return [send(phase, s, source((me + s) % 8), target, (me + s) % 8) for s in range(1, 8)]

    def spread_out(phase, target):
        copies = [send(phase, 4, target.at[me], target.at[me], sibling)]
        for s in range(1, 4):
            copies.append(send(phase, s, target.at[me], target.at[me], ((chip + s) % 4) * 2 + core))
        return copies

    def relay(phase, target, copies):
        passed = []
        for s in range(1, 4):
            copies[s].wait_recv()
            slot = ((chip + 4 - s) % 4) * 2 + core
            passed.append(send(phase, 4 + s, target.at[slot], target.at[slot], sibling))
        copies.extend(passed)

    def complete(copies):
        copies[0].wait_recv()
        for copy in copies[4:]:
            copy.wait_recv()

    def arrived(copies):
        for copy in copies:
            copy.wait_recv()

    bucket = bucket_ref[0]
    high, width = jnp.int32(0), jnp.int32(0)
    for index in range(res_table_ref.shape[1]):
        high = high + jnp.where(bucket == index, res_table_ref[0, index], 0)
        width = width + jnp.where(bucket == index, res_table_ref[1, index], 0)
    line = lax.broadcasted_iota(jnp.int32, (8, 128), 0)
    facts = jnp.where(line == 0, start_ref[0], jnp.where(line == 1, high, width)).astype(F32)
    meta_ref[...] = facts
    meta_all[chip] = facts
    meta_copies = [
        send(3, s, meta_ref, meta_all.at[chip], ((chip + s) % 4) * 2 + core) for s in range(1, 4)
    ]
    loads["swap"].wait()
    halves = []
    for half in range(2):
        halves.append(
            jnp.concatenate(
                [video_ref[64 * t : 64 * t + 64, 128 * half : 128 * half + 128] for t in range(4)],
                axis=1,
            )
        )
    packed = dot(jnp.concatenate(halves, axis=0), swap_ref[...]).astype(BF16)
    for index in range(8):
        half, quarter = index // 4, index % 4
        v_send[index] = packed[64 * half : 64 * half + 64, 128 * quarter : 128 * quarter + 128]
    v_copies = send_all(0, lambda to: v_send.at[to], v_all.at[me])
    v_all[me] = v_send[me]
    og_all[me] = og_ref[0].astype(F32).reshape(64, WIDE).astype(BF16)
    og_copies = spread_out(1, og_all)

    loads["dw"].wait()
    loads["pick"].wait()

    picks = None
    for tap in range(3):
        at = [(3 * b + tap) * WIDE for b in range(3)]
        rows = jnp.concatenate([dw_ref[:, low : low + WIDE] for low in at], axis=0)
        term = dot(rows, pick_ref[256 * tap : 256 * tap + 256, :])
        picks = term if picks is None else picks + term
    for other in range(4):
        w_send[other] = picks[:, 128 * other : 128 * other + 128].astype(BF16)
    w_all[chip] = w_send[chip]
    dw_copies = []
    for s in range(1, 4):
        to = (chip + s) % 4
        dw_copies.append(send(2, s, w_send.at[to], w_all.at[chip], to * 2 + core))

    arrived(meta_copies)
    place1 = lax.broadcasted_iota(jnp.int32, (1, 128), 1) // OWN
    start = jnp.zeros((1, 128), F32)
    high = jnp.zeros((1, 128), F32)
    width = jnp.zeros((1, 128), F32)
    for clip in range(4):
        start = jnp.where(place1 == clip, meta_all[clip, 0:1, :], start)
        high = jnp.where(place1 == clip, meta_all[clip, 1:2, :], high)
        width = jnp.where(place1 == clip, meta_all[clip, 2:3, :], width)
    count = (8.0 - start) * high * width * 8.0
    row_id = lax.broadcasted_iota(jnp.int32, (512, 128), 0)
    in_time = (row_id // 64).astype(F32) >= start
    in_rows = (row_id // 8 % 8).astype(F32) < high
    in_cols = (row_id % 8).astype(F32) < width
    mask_ref[...] = jnp.where(in_time & in_rows & in_cols, 1.0, 0.0)

    arrived(v_copies)
    stacked = jnp.concatenate(
        [
            jnp.concatenate([v_all[2 * other + c] for other in range(4)], axis=1)
            for c in range(2)
        ],
        axis=0,
    )
    unpacked = dot(stacked, swap_ref[...])
    for t in range(8):
        c, q = t // 4, t % 4
        cells[64 * t : 64 * t + 64, :] = unpacked[64 * c : 64 * c + 64, 128 * q : 128 * q + 128]
    mask = mask_ref[...]
    centre = group_total(jnp.sum(mask * cells[...], axis=0, keepdims=True)) / count
    offset = cells[...] - centre
    spread = group_total(jnp.sum(mask * offset * offset, axis=0, keepdims=True)) / count
    inverse = lax.rsqrt(spread + EPSILON)
    normed = offset * inverse
    normed_ref[...] = normed
    h_all[me] = (mask * (normed / (1.0 + jnp.exp(-normed)))).astype(BF16)
    h_copies = spread_out(4, h_all)

    relay(1, og_all, og_copies)
    complete(og_copies)
    up_row = lax.broadcasted_iota(jnp.int32, (128, 64), 0)
    up_col = lax.broadcasted_iota(jnp.int32, (128, 64), 1)
    lift = ((up_row // 8 == up_col // 4) & (up_row % 8 == 2 * (up_col % 4))).astype(F32).astype(BF16)
    for c in range(2):
        raised = [dot(lift, og_all[2 * clip + c]).reshape(16, 8, WIDE) for clip in range(4)]
        og_up[4 * c : 4 * c + 4] = (
            jnp.concatenate(raised, axis=1).astype(BF16).reshape(4, 4, 32, WIDE)
        )
    arrived(dw_copies)

    def res_grad_frame(t, carry):
        lhs = og_up[t].reshape(128, WIDE)
        layers = []
        for b in range(3):
            panel = w_all[:, 64 * b : 64 * b + 64, :].reshape(256, 128)
            layers.append(fold_taps(dot(lhs, panel), 4, (0, -1, -2)).reshape(4, 8, 128))
        even = layers[0] + jnp.concatenate([jnp.zeros((1, 8, 128), F32), layers[2][:3]], axis=0)
        both = jnp.stack([even, layers[1]], axis=1).reshape(64, 128)
        at = pl.ds(pl.multiple_of(64 * t, 64), 64)
        value = (mask_ref[at, :] * both).astype(BF16)
        g_all[me, at, :] = value
        wide = value.astype(F32)
        res_ref[at, :] = wide
        return carry

    lax.fori_loop(0, 8, res_grad_frame, 0)
    g_copies = [send(5, 0, g_all.at[me], g_all.at[me], sibling)]

    loads["cw"].wait()
    from_row = lax.broadcasted_iota(jnp.int32, (WIDE, 128), 0)
    to_lane = lax.broadcasted_iota(jnp.int32, (WIDE, 128), 1)
    chosen = from_row == to_lane // OWN * 64 + OWN * core + to_lane % OWN
    chosen = chosen.astype(F32).astype(BF16)
    for ab in range(9):
        at = [(3 * ab + tap) * WIDE for tap in range(3)]
        rows = jnp.concatenate([cw_ref[:, low : low + WIDE] for low in at], axis=0)
        rows_back[ab, 0:192, :] = dot(rows, chosen).astype(BF16)
        rows_back[ab, 192:256, :] = jnp.zeros((64, 128), BF16)

    mine = pl.ds(pl.multiple_of(core * OWN, OWN), OWN)
    for ab in range(9):
        for tap in range(3):
            at = (3 * ab + tap) * WIDE
            rows_fwd[ab, 32 * tap : 32 * tap + 32, :] = cw_ref[mine, at : at + WIDE]
        rows_fwd[ab, 96:128, :] = jnp.zeros((32, WIDE), BF16)
    for b in range(3):
        for tap in range(3):
            at = (3 * b + tap) * WIDE
            rows_fwd[9 + b, 32 * tap : 32 * tap + 32, :] = dw_ref[mine, at : at + WIDE]
        rows_fwd[9 + b, 96:128, :] = jnp.zeros((32, WIDE), BF16)

    edge = jnp.zeros((10, 32, WIDE), BF16)
    for t in range(2):
        h_full[t] = edge
        g_full[8 + t] = edge
    for t in range(8):
        for full, off in ((h_full, 2), (g_full, 0)):
            full[t + off, 0] = jnp.zeros((32, WIDE), BF16)
            full[t + off, 9] = jnp.zeros((32, WIDE), BF16)
        r_full[t, 4, 0] = jnp.zeros((32, WIDE), BF16)

    arrived(g_copies)
    place = lax.broadcasted_iota(jnp.int32, (64, 128), 1) // OWN

    def stack_frame(t, carry):
        at = pl.ds(pl.multiple_of(64 * t, 64), 64)
        moved = []
        for c in range(2):
            block = g_all[2 * chip + c, at, :].astype(F32)
            moved.append([move_cols(block, 1 - tap) for tap in range(3)])
        split = []
        for clip in range(4):
            sides = [jnp.zeros((64, 128), F32)] * 2
            for tap in range(3):
                for c in range(2):
                    spot = 2 * (tap % 2) + c
                    turn = (OWN * (spot - clip)) % 128
                    block = moved[c][tap]
                    if turn:
                        block = pltpu.roll(block, turn, 1)
                    sides[tap // 2] = jnp.where(place == spot, block, sides[tap // 2])
            split.append(jnp.concatenate(sides, axis=1).reshape(8, 8, WIDE))
        rows = jnp.concatenate(split, axis=1).reshape(256, WIDE)
        g_full[t, 1:9] = rows.astype(BF16).reshape(8, 32, WIDE)
        return carry

    lax.fori_loop(0, 8, stack_frame, 0)

    def back_frame(t, carry):
        total = None
        for a in range(3):
            for b in range(3):
                window = g_full[t + 2 - a, 2 - b : 10 - b].reshape(256, WIDE)
                term = dot(window, rows_back[3 * a + b])
                total = term if total is None else total + term
        parts = total.reshape(8, 4, 8, 128)
        at = pl.ds(pl.multiple_of(64 * t, 64), 64)
        own = jnp.zeros((64, 128), F32)
        for other in range(4):
            piece = jnp.zeros((64, 128), F32)
            for clip in range(4):
                block = parts[:, clip].reshape(64, 128)
                turn = (OWN * (clip - other)) % 128
                if turn:
                    block = pltpu.roll(block, turn, 1)
                piece = jnp.where(place == clip, block, piece)
            p_send[other, at, :] = piece.astype(BF16)
            own = jnp.where(chip == other, piece, own)
        back_ref[at, :] = own
        return carry

    lax.fori_loop(0, 5, back_frame, 0)
    relay(4, h_all, h_copies)
    lax.fori_loop(5, 8, back_frame, 0)
    p_copies = []
    for s in range(1, 4):
        to = (chip + s) % 4
        p_copies.append(send(10, s, p_send.at[to], p_all.at[s], to * 2 + core))

    def assemble(source, t):
        at = pl.ds(pl.multiple_of(256 * t, 256), 256)
        clips = gathered_lanes([source[d, at, :] for d in range(8)], swap_ref[...])
        blocks = [clip.reshape(32, 8, WIDE) for clip in clips]
        return jnp.concatenate(blocks, axis=1).astype(BF16).reshape(4, 8, 32, WIDE)

    def keep(index, source, target):
        copy = pltpu.make_async_copy(source, target, load_sems.at[index])
        copy.start()
        return copy

    kept = []

    complete(h_copies)

    def fill_hidden(t, carry):
        h_full[pl.ds(4 * t + 2, 4), 1:9] = assemble(h_all, t)
        return carry

    lax.fori_loop(0, 2, fill_hidden, 0)
    kept.append(keep(5, h_full, h_out))

    def conv_frame(t, carry):
        total = None
        for a in range(3):
            for b in range(3):
                window = h_full[t + a, b : b + 8].reshape(256, WIDE)
                term = dot_nt(window, rows_fwd[3 * a + b])
                total = term if total is None else total + term
        folded = fold_taps(total, 8, (-1, 0, 1))
        at = pl.ds(pl.multiple_of(64 * t, 64), 64)
        r_all[me, at, :] = (mask_ref[at, :] * (cells[at, :] + folded)).astype(BF16)
        return carry

    lax.fori_loop(0, 8, conv_frame, 0)
    r_copies = spread_out(6, r_all)

    arrived(p_copies)
    mask = mask_ref[...]
    normed = normed_ref[...]
    gate = 1.0 / (1.0 + jnp.exp(-normed))
    back = back_ref[...]
    for s in range(1, 4):
        back = back + p_all[s].astype(F32)
    pushed = mask * back * gate * (1.0 + normed * (1.0 - gate))
    mean_push = group_total(jnp.sum(pushed, axis=0, keepdims=True)) / count
    mean_pair = group_total(jnp.sum(pushed * normed, axis=0, keepdims=True)) / count
    through = inverse * (pushed - mean_push - normed * mean_pair)
    back_ref[...] = mask * through + res_ref[...]
    for c in range(2):
        quarter = [back_ref[64 * (4 * c + q) : 64 * (4 * c + q) + 64, :] for q in range(4)]
        swapped = dot(jnp.concatenate(quarter, axis=1).astype(BF16), swap_ref[...]).astype(BF16)
        for other in range(4):
            x_send[2 * other + c] = swapped[:, 128 * other : 128 * other + 128]
    x_all[me] = x_send[me]
    x_copies = send_all(8, lambda to: x_send.at[to], x_all.at[me])

    def og_frame(t, carry):
        from_row = lax.broadcasted_iota(jnp.int32, (WIDE, WIDE), 0)
        to_lane = lax.broadcasted_iota(jnp.int32, (WIDE, WIDE), 1)
        chosen = (from_row == to_lane % 64 + 64 * chip).astype(F32).astype(BF16)
        rows = dot(og_up[t].reshape(128, WIDE), chosen)
        tap = lax.broadcasted_iota(jnp.int32, (128, WIDE), 1) // 64
        once, twice = move_cols(rows, -1), move_cols(rows, -2)
        rows = jnp.where(tap == 0, rows, jnp.where(tap == 1, once, twice))
        og_stack_t[t] = rows.T.astype(BF16)
        return carry

    lax.fori_loop(0, 8, og_frame, 0)

    kept.append(keep(4, og_stack_t, og_stack_out))
    relay(6, r_all, r_copies)
    def turn_frame(t, carry):
        rows = g_full[t, 1:9].reshape(256, WIDE).astype(F32)
        stack_t[t] = rows.T.astype(BF16)
        return carry

    lax.fori_loop(0, 8, turn_frame, 0)
    kept.append(keep(6, stack_t, stack_out))

    complete(r_copies)

    def fill_residual(t, carry):
        r_full[pl.ds(4 * t, 4), 0:4] = assemble(r_all, t).reshape(4, 4, 2, 32, WIDE)
        return carry

    lax.fori_loop(0, 2, fill_residual, 0)
    kept.append(keep(7, r_full, r_out))

    def down_frame(t, carry):
        total = None
        for b in range(3):
            window = r_full[t, b // 2 : b // 2 + 4, b % 2].reshape(128, WIDE)
            term = dot_nt(window, rows_fwd[9 + b])
            total = term if total is None else total + term
        folded = fold_taps(total, 4, (0, 1, 2)).astype(BF16)
        to_row = lax.broadcasted_iota(jnp.int32, (16, 32), 0)
        from_row = lax.broadcasted_iota(jnp.int32, (16, 32), 1)
        even = (from_row == to_row * 2).astype(F32).astype(BF16)
        d_send[t] = dot(even, folded).astype(BF16)
        return carry

    lax.fori_loop(0, 8, down_frame, 0)

    def frames_of(to):
        return pl.ds(4 * (to % 2), 4)

    d_all[me] = d_send[frames_of(me)]
    d_copies = send_all(7, lambda to: d_send.at[frames_of(to)], d_all.at[me])
    arrived(x_copies)
    arrived(d_copies)
    for copy in kept:
        copy.wait()
    for copies in (
        meta_copies, v_copies, og_copies, dw_copies, p_copies, h_copies, g_copies, r_copies, x_copies,
        d_copies,
    ):
        for copy in copies:
            copy.wait_send()


def finish_kernel(
    x_hbm, d_hbm, h_hbm, r_hbm, stack_hbm, og_stack_hbm, swap_hbm,
    down_ref, vgrad_ref, cgrad_hbm, dgrad_hbm,
    x_all, d_all, h_full, r_full, stack_t, og_stack_t, swap_ref, cgrad_ref, dgrad_ref,
    load_sems, store_sems,
):
    chip = lax.axis_index("fsdp")
    loads = []
    for index, (source, target) in enumerate(
        (
            (swap_hbm, swap_ref),
            (x_hbm, x_all),
            (d_hbm, d_all),
            (stack_hbm, stack_t),
            (h_hbm, h_full),
            (og_stack_hbm, og_stack_t),
            (r_hbm, r_full),
        )
    ):
        loads.append(pltpu.make_async_copy(source, target, load_sems.at[index]))
        loads[-1].start()
    for copy in loads[:3]:
        copy.wait()
    frames = gathered_lanes([x_all[d] for d in range(8)], swap_ref[...])
    for t, block in enumerate(frames):
        vgrad_ref[64 * t : 64 * t + 64, :] = block.astype(BF16)
    clips = gathered_lanes([d_all[d].reshape(64, 128) for d in range(8)], swap_ref[...])
    own = clips[0]
    for clip in range(1, 4):
        own = jnp.where(chip == clip, clips[clip], own)
    down_ref[0] = own.reshape(4, 4, 4, WIDE).astype(BF16)

    stores = []

    def put(grad, ref, hbm, block, index):
        for tap in range(3):
            at = (3 * block + tap) * WIDE
            ref[:, at : at + WIDE] = grad[64 * tap : 64 * tap + 64]
        part = pl.ds(3 * block * WIDE, 3 * WIDE)
        stores.append(pltpu.make_async_copy(ref.at[:, part], hbm.at[:, part], store_sems.at[index]))
        stores[-1].start()

    loads[3].wait()
    loads[4].wait()
    lhs = jnp.concatenate([stack_t[t, 0:192] for t in range(8)], axis=1)
    for a in range(3):
        for b in range(3):
            rhs = h_full[a : a + 8, b : b + 8].reshape(2048, WIDE)
            put(dot(lhs, rhs), cgrad_ref, cgrad_hbm, 3 * a + b, 3 * a + b)
    loads[5].wait()
    loads[6].wait()
    lhs = jnp.concatenate([og_stack_t[t, 0:192] for t in range(8)], axis=1)
    for b in range(3):
        rhs = r_full[:, b // 2 : b // 2 + 4, b % 2].reshape(1024, WIDE)
        put(dot(lhs, rhs), dgrad_ref, dgrad_hbm, b, 9 + b)
    for copy in stores:
        copy.wait()


def fused(video, conv_weight, down_weight, out_grad, clip_bucket, start_frame, bucket_res):
    vmem = pl.BlockSpec(memory_space=pltpu.VMEM)
    smem = pl.BlockSpec(memory_space=pltpu.SMEM)
    anywhere = pl.BlockSpec(memory_space=pl.ANY)
    full = pltpu.VMEM((10, 10, 32, WIDE), BF16)
    gathered = pltpu.VMEM((8, 512, 128), BF16)
    wide = pltpu.VMEM((512, 128), F32)
    piece = pltpu.VMEM((8, 64, 128), BF16)
    sent = jax.ShapeDtypeStruct((8, 64, 128), BF16)
    sent_down = jax.ShapeDtypeStruct((8, 4, 16, 128), BF16)
    full_cells = jax.ShapeDtypeStruct((10, 10, 32, WIDE), BF16)
    even_cells = jax.ShapeDtypeStruct((8, 5, 2, 32, WIDE), BF16)
    stack = jax.ShapeDtypeStruct((8, 256, 256), BF16)
    og_stack = jax.ShapeDtypeStruct((8, 256, 128), BF16)
    swap = lane_swap()
    parts = pl.pallas_call(
        block_kernel,
        out_shape=(sent, sent_down, full_cells, even_cells, stack, og_stack),
        in_specs=[smem] * 3 + [vmem, anywhere, anywhere, vmem] + [anywhere] * 2,
        out_specs=(vmem,) * 2 + (anywhere,) * 4,
        scratch_shapes=[
            pltpu.VMEM((8, 128), F32),
            pltpu.VMEM(conv_weight.shape, BF16),
            pltpu.VMEM(down_weight.shape, BF16),
            pltpu.VMEM((512, 512), BF16),
            pltpu.VMEM((768, 512), BF16),
            pltpu.VMEM((4, 8, 128), F32),
            piece,
            piece,
            pltpu.VMEM((4, 192, 128), BF16),
            pltpu.VMEM((4, 192, 128), BF16),
            pltpu.VMEM((8, 64, WIDE), BF16),
            gathered,
            gathered,
            gathered,
            pltpu.VMEM((8, 16, 128), BF16),
            piece,
            pltpu.VMEM((4, 512, 128), BF16),
            pltpu.VMEM((4, 512, 128), BF16),
            full,
            full,
            pltpu.VMEM((8, 5, 2, 32, WIDE), BF16),
            pltpu.VMEM((9, 256, 128), BF16),
            pltpu.VMEM((8, 4, 32, WIDE), BF16),
            pltpu.VMEM((12, 128, WIDE), BF16),
            wide,
            wide,
            wide,
            wide,
            pltpu.VMEM((8, 256, 256), BF16),
            pltpu.VMEM((8, 256, 128), BF16),
            wide,
            pltpu.SemaphoreType.DMA((8,)),
            pltpu.SemaphoreType.DMA((11, 8)),
            pltpu.SemaphoreType.DMA((11, 8)),
        ],
        compiler_params=pltpu.CompilerParams(
            collective_id=0, has_side_effects=True, vmem_limit_bytes=60 * 2**20
        ),
    )(
        clip_bucket,
        start_frame,
        bucket_res.T,
        video.reshape(256, WIDE),
        conv_weight,
        down_weight,
        out_grad,
        swap,
        column_pick(),
    )
    kinds = (sent, sent_down, full_cells, even_cells, stack, og_stack, swap)
    down, video_grad, conv_grad, down_grad = pl.pallas_call(
        finish_kernel,
        out_shape=(
            jax.ShapeDtypeStruct(out_grad.shape, BF16),
            jax.ShapeDtypeStruct((256, WIDE), BF16),
            jax.ShapeDtypeStruct(conv_weight.shape, F32),
            jax.ShapeDtypeStruct(down_weight.shape, F32),
        ),
        in_specs=[anywhere] * 7,
        out_specs=(vmem, vmem, anywhere, anywhere),
        scratch_shapes=[pltpu.VMEM(kind.shape, BF16) for kind in kinds]
        + [
            pltpu.VMEM(conv_weight.shape, F32),
            pltpu.VMEM(down_weight.shape, F32),
            pltpu.SemaphoreType.DMA((7,)),
            pltpu.SemaphoreType.DMA((12,)),
        ],
        compiler_params=pltpu.CompilerParams(vmem_limit_bytes=60 * 2**20),
    )(*parts, swap)
    return (down, video_grad.reshape(video.shape), conv_grad, down_grad)


def solution(mesh):
    placed = (
        P(("mix", "fsdp"), "tile", None, None, None),
        P(("mix", "fsdp"), None),
        P(("mix", "fsdp"), None),
        P(("mix", "fsdp"), "tile", None, None, None),
        P(("mix", "fsdp")),
        P(("mix", "fsdp")),
        P(),
    )
    return jax.shard_map(
        fused if mesh.shape["tile"] == 2 and mesh.shape["fsdp"] == 4 else shards,
        mesh=mesh,
        in_specs=placed,
        out_specs=(
            P(("mix", "fsdp"), "tile", None, None, None),
            P(("mix", "fsdp"), "tile", None, None, None),
            P(("mix", "fsdp"), None),
            P(("mix", "fsdp"), None),
        ),
        check_vma=False,
    )
```

```python
import functools

import jax
import jax.numpy as jnp
import numpy as np
from jax import lax
from jax.experimental import pallas as pl
from jax.experimental.pallas import tpu as pltpu
from jax.sharding import PartitionSpec as P

GROUPS = 32


EPSILON = 1e-06


def shifted(block, axis, distance):
    devices = range(lax.axis_size(axis))
    route = [(i - distance, i) for i in devices if i - distance in devices]
    return lax.ppermute(block, axis, route)


def valid_mask(clip_bucket, start_frame, bucket_res, first_frame, frame_count, side_cells):
    bucket_ids = jnp.arange(bucket_res.shape[0], dtype=jnp.int32)
    picked = (clip_bucket[:, None] == bucket_ids[None, :]).astype(jnp.int32)
    limits = jnp.sum(picked[:, :, None] * bucket_res[None, :, :], axis=1)
    frame_ids = first_frame + jnp.arange(frame_count, dtype=jnp.int32)
    positions = jnp.arange(side_cells, dtype=jnp.int32)
    in_time = frame_ids[None, :] >= start_frame[:, None]
    in_rows = positions[None, :] < limits[:, 0:1]
    in_cols = positions[None, :] < limits[:, 1:2]
    inside = in_time[:, :, None, None] & in_rows[:, None, :, None] & in_cols[:, None, None, :]
    return (inside.astype(jnp.float32)[..., None], limits)


def time_group(padded, tap_time, out_frames, side_cells, flipped):
    channel_count = padded.shape[-1]
    time_start = 2 - tap_time if flipped else tap_time
    layers = []
    for tap_row in range(3):
        for tap_col in range(3):
            row_start = 2 - tap_row if flipped else tap_row
            col_start = 2 - tap_col if flipped else tap_col
            window = padded[
                :,
                time_start : time_start + out_frames,
                row_start : row_start + side_cells,
                col_start : col_start + side_cells,
                :,
            ]
            layers.append(window.reshape(-1, channel_count))
    return jnp.stack(layers)


def stride_taps(padded, side_cells):
    channel_count = padded.shape[-1]
    layers = []
    for tap_row in range(3):
        for tap_col in range(3):
            window = padded[
                :, :, tap_row : tap_row + side_cells : 2, tap_col : tap_col + side_cells : 2, :
            ]
            layers.append(window.reshape(-1, channel_count))
    return jnp.stack(layers)


def weight_terms(grad_rows, slabs, cot_rows, hidden_padded, frame_count, side_cells):
    out_rows = grad_rows.shape[1]
    down_term = lax.dot_general(
        grad_rows, slabs, (((0,), (1,)), ((), ())), preferred_element_type=jnp.float32
    ).reshape(out_rows, -1)
    conv_parts = []
    for tap_time in range(3):
        group = time_group(hidden_padded, tap_time, frame_count, side_cells, False)
        conv_parts.append(
            lax.dot_general(
                cot_rows, group, (((0,), (1,)), ((), ())), preferred_element_type=jnp.float32
            )
        )
    conv_term = jnp.concatenate(conv_parts, axis=1).reshape(out_rows, -1)
    return (conv_term, down_term)


def transpose_conv(grad_padded, conv_weight, out_frames, side_cells):
    channel_count = grad_padded.shape[-1]
    row_total = grad_padded.shape[0] * out_frames * side_cells * side_cells
    initial = jnp.zeros((row_total, channel_count), jnp.float32)
    running = initial
    weight_panel = lax.all_gather(conv_weight, "fsdp", axis=0, tiled=True)
    panel_rows = weight_panel.shape[0]
    panel = weight_panel.reshape(panel_rows, 27, channel_count)
    for tap_time in range(3):
        group = time_group(grad_padded, tap_time, out_frames, side_cells, True)
        running = running + lax.dot_general(
            group,
            panel[:, 9 * tap_time : 9 * tap_time + 9, :],
            (((0, 2), (1, 0)), ((), ())),
            preferred_element_type=jnp.float32,
        )
    return running


def shards(video, conv_weight, down_weight, out_grad, clip_bucket, start_frame, bucket_res):
    clip_count, frame_count, side_cells, side_again, channel_count = video.shape
    half_side = side_cells // 2
    group_width = channel_count // GROUPS
    tiles = lax.axis_size("tile")
    mask, limits = valid_mask(
        clip_bucket,
        start_frame,
        bucket_res,
        lax.axis_index("tile") * frame_count,
        frame_count,
        side_cells,
    )
    valid_count = (
        (frame_count * tiles - start_frame) * limits[:, 0] * limits[:, 1] * group_width
    ).astype(jnp.float32)
    grouped_shape = (clip_count, frame_count, side_cells, side_cells, GROUPS, group_width)
    summed_axes = (1, 2, 3, 5)
    cell_weight = mask[..., None]
    grouped = video.astype(jnp.float32).reshape(grouped_shape)
    first_sum = lax.psum(jnp.sum(grouped * cell_weight, axis=summed_axes), "tile")
    centre = first_sum / valid_count[:, None]
    offset = grouped - centre[:, None, None, None, :, None]
    second_sum = lax.psum(jnp.sum(cell_weight * offset * offset, axis=summed_axes), "tile")
    spread = second_sum / valid_count[:, None]
    inverse = lax.rsqrt(spread + EPSILON)
    normed_grouped = offset * inverse[:, None, None, None, :, None]
    normed = normed_grouped.reshape(video.shape)
    hidden = (mask * jax.nn.silu(normed)).astype(jnp.bfloat16)
    past = shifted(hidden[:, frame_count - 2 :], "tile", 1)
    hidden_padded = jnp.pad(
        jnp.concatenate([past, hidden], axis=1), ((0, 0), (0, 0), (1, 1), (1, 1), (0, 0))
    )

    def conv_columns(weight_panel):
        panel = weight_panel.reshape(weight_panel.shape[0], 27, channel_count)
        summed = None
        for tap_time in range(3):
            group = time_group(hidden_padded, tap_time, frame_count, side_cells, False)
            term = lax.dot_general(
                group,
                panel[:, 9 * tap_time : 9 * tap_time + 9, :],
                (((0, 2), (1, 2)), ((), ())),
                preferred_element_type=jnp.float32,
            )
            summed = term if summed is None else summed + term
        return summed

    conv_out = conv_columns(lax.all_gather(conv_weight, "fsdp", axis=0, tiled=True))
    residual = (mask * (video.astype(jnp.float32) + conv_out.reshape(video.shape))).astype(
        jnp.bfloat16
    )
    down_slabs = stride_taps(
        jnp.pad(residual, ((0, 0), (0, 0), (0, 1), (0, 1), (0, 0))), side_cells
    )
    weight_panel = lax.all_gather(down_weight, "fsdp", axis=0, tiled=True)
    panel = weight_panel.reshape(weight_panel.shape[0], 9, channel_count)
    down_out = lax.dot_general(
        down_slabs, panel, (((0, 2), (1, 2)), ((), ())), preferred_element_type=jnp.float32
    )
    down = down_out.astype(jnp.bfloat16).reshape(
        clip_count, frame_count, half_side, half_side, channel_count
    )
    grad_flat = out_grad.reshape(-1, channel_count)
    weight_panel = lax.all_gather(down_weight, "fsdp", axis=0, tiled=True)
    panel_rows = weight_panel.shape[0]
    panel = weight_panel.reshape(panel_rows, 9, channel_count)
    tap_grads = lax.dot_general(
        grad_flat, panel, (((1,), (0,)), ((), ())), preferred_element_type=jnp.float32
    )
    spread_back = jnp.zeros(
        (clip_count, frame_count, side_cells + 1, side_cells + 1, channel_count), jnp.float32
    )
    for tap_row in range(3):
        for tap_col in range(3):
            term = tap_grads[:, tap_row * 3 + tap_col, :].reshape(
                clip_count, frame_count, half_side, half_side, channel_count
            )
            spread_back = spread_back.at[
                :, :, tap_row : tap_row + side_cells : 2, tap_col : tap_col + side_cells : 2, :
            ].add(term)
    res_grad = (mask * spread_back[:, :, :side_cells, :side_cells, :]).astype(jnp.bfloat16)
    res_flat = res_grad.reshape(-1, channel_count)
    later = shifted(res_grad[:, :2], "tile", -1)
    grad_padded = jnp.pad(
        jnp.concatenate([res_grad, later], axis=1), ((0, 0), (0, 0), (1, 1), (1, 1), (0, 0))
    )
    back_hidden = transpose_conv(grad_padded, conv_weight, frame_count, side_cells).reshape(
        video.shape
    )
    gate_value = jax.nn.sigmoid(normed)
    pushed = mask * back_hidden * gate_value * (1.0 + normed * (1.0 - gate_value))
    pushed_grouped = pushed.reshape(grouped_shape)
    push_sum, pair_sum = lax.psum(
        (
            jnp.sum(pushed_grouped, axis=summed_axes),
            jnp.sum(pushed_grouped * normed_grouped, axis=summed_axes),
        ),
        "tile",
    )
    mean_push = push_sum / valid_count[:, None]
    mean_pair = pair_sum / valid_count[:, None]
    through_norm = inverse[:, None, None, None, :, None] * (
        pushed_grouped
        - mean_push[:, None, None, None, :, None]
        - normed_grouped * mean_pair[:, None, None, None, :, None]
    )
    video_grad = (mask * through_norm.reshape(video.shape) + res_grad.astype(jnp.float32)).astype(
        jnp.bfloat16
    )
    conv_term, down_term = weight_terms(
        grad_flat, down_slabs, res_flat, hidden_padded, frame_count, side_cells
    )
    conv_share, down_share = (
        lax.psum_scatter(conv_term, ("fsdp", "tile"), scatter_dimension=0, tiled=True),
        lax.psum_scatter(down_term, ("fsdp", "tile"), scatter_dimension=0, tiled=True),
    )
    conv_weight_grad, down_weight_grad = (
        lax.all_gather(conv_share, "tile", axis=0, tiled=True),
        lax.all_gather(down_share, "tile", axis=0, tiled=True),
    )
    return (down, video_grad, conv_weight_grad, down_weight_grad)


F32 = jnp.float32
BF16 = jnp.bfloat16
MESH = pl.DeviceIdType.MESH
WIDE = 256
OWN = 32


def lane_swap():
    lane = np.arange(512)
    outer, inner, channel = lane // 128, lane // 32 % 4, lane % 32
    table = np.zeros((512, 512), np.float32)
    table[lane, inner * 128 + outer * 32 + channel] = 1.0
    return jnp.asarray(table, BF16)


def column_pick():
    table = np.zeros((2, 3, 256, 4, 4, 32), np.float32)
    for core in range(2):
        for tap in range(3):
            for chip in range(4):
                for channel in range(32):
                    table[core, tap, 64 * chip + 32 * core + channel, chip, tap, channel] = 1.0
    return jnp.asarray(table.reshape(2, 768, 512), BF16)


def dot(lhs, rhs):
    return jnp.dot(lhs, rhs, preferred_element_type=F32)


def move_cols(block, distance):
    if distance == 0:
        return block
    rows = block.shape[0]
    col = lax.broadcasted_iota(jnp.int32, block.shape, 0) % 8 + distance
    turned = pltpu.roll(block, (-distance) % rows, 0)
    return jnp.where((col >= 0) & (col < 8), turned, 0.0)


def fold_taps(result, outer, distances):
    parts = result.reshape(outer, 4, 8, 128)
    place = lax.broadcasted_iota(jnp.int32, (outer * 8, 128), 1) // OWN
    total = None
    for tap in range(3):
        layer = jnp.zeros((outer * 8, 128), F32)
        for clip in range(4):
            block = parts[:, clip].reshape(outer * 8, 128)
            turn = (OWN * (clip - tap)) % 128
            if turn:
                block = pltpu.roll(block, turn, 1)
            layer = jnp.where(place == clip, block, layer)
        layer = move_cols(layer, distances[tap])
        total = layer if total is None else total + layer
    return total


def group_total(row):
    first = lax.broadcasted_iota(jnp.int32, (128, 128), 0) // 8
    second = lax.broadcasted_iota(jnp.int32, (128, 128), 1) // 8
    same = (first == second).astype(F32)
    wide = jnp.broadcast_to(row, (8, 128))
    return jnp.dot(wide, same, preferred_element_type=F32, precision=lax.Precision.HIGHEST)[0:1]


def gathered_lanes(pieces, swap):
    halves = [
        dot(jnp.concatenate(pieces[4 * half : 4 * half + 4], axis=1), swap) for half in range(2)
    ]
    return [
        jnp.concatenate([half[:, 128 * p : 128 * p + 128] for half in halves], axis=1)
        for p in range(4)
    ]


def block_kernel(
    bucket_ref, start_ref, res_table_ref, video_ref, cw_hbm, dw_hbm, og_ref, swap_hbm,
    pick_hbm,
    x_all, d_all, h_out, r_out, stack_out, og_stack_out,
    meta_ref, cw_ref, dw_ref, swap_ref, pick_ref,
    meta_all, v_send, v_all, w_send, w_all, og_all, h_all, g_all, r_all, d_send,
    x_send, p_send, p_all, h_full, g_full, r_full, rows_back, rows_down, sums, og_up, rows_fwd, cells, normed_ref, mask_ref,
    res_ref, stack_t, og_stack_t, back_ref, load_sems, send_sems, recv_sems,
):
    chip = lax.axis_index("fsdp")
    core = lax.axis_index("tile")
    me = chip * 2 + core
    sibling = chip * 2 + (1 - core)

    def peer(index):
        return {"fsdp": index // 2, "tile": index % 2}

    loads = {}
    for index, (name, source, target) in enumerate(
        (
            ("swap", swap_hbm, swap_ref),
            ("dw", dw_hbm, dw_ref),
            ("pick", pick_hbm.at[core], pick_ref),
            ("cw", cw_hbm, cw_ref),
        )
    ):
        loads[name] = pltpu.make_async_copy(source, target, load_sems.at[index])
        loads[name].start()

    barrier = pltpu.get_barrier_semaphore()
    for step in range(1, 8):
        pl.semaphore_signal(barrier, inc=1, device_id=peer((me + step) % 8), device_id_type=MESH)
    pl.semaphore_wait(barrier, 7)

    def send(phase, step, src, dst, to):
        copy = pltpu.make_async_remote_copy(
            src_ref=src, dst_ref=dst, send_sem=send_sems.at[phase, step],
            recv_sem=recv_sems.at[phase, step], device_id=peer(to), device_id_type=MESH,
        )
        copy.start()
        return copy

    def send_all(phase, source, target):
        return [send(phase, s, source((me + s) % 8), target, (me + s) % 8) for s in range(1, 8)]

    def spread_out(phase, target):
        copies = [send(phase, 4, target.at[me], target.at[me], sibling)]
        for s in range(1, 4):
            copies.append(send(phase, s, target.at[me], target.at[me], ((chip + s) % 4) * 2 + core))
        return copies

    def relay(phase, target, copies):
        passed = []
        for s in range(1, 4):
            copies[s].wait_recv()
            slot = ((chip + 4 - s) % 4) * 2 + core
            passed.append(send(phase, 4 + s, target.at[slot], target.at[slot], sibling))
        copies.extend(passed)

    def complete(copies):
        copies[0].wait_recv()
        for copy in copies[4:]:
            copy.wait_recv()

    def arrived(copies):
        for copy in copies:
            copy.wait_recv()

    bucket = bucket_ref[0]
    high, width = jnp.int32(0), jnp.int32(0)
    for index in range(res_table_ref.shape[1]):
        high = high + jnp.where(bucket == index, res_table_ref[0, index], 0)
        width = width + jnp.where(bucket == index, res_table_ref[1, index], 0)
    line = lax.broadcasted_iota(jnp.int32, (8, 128), 0)
    facts = jnp.where(line == 0, start_ref[0], jnp.where(line == 1, high, width)).astype(F32)
    meta_ref[...] = facts
    meta_all[chip] = facts
    meta_copies = [
        send(3, s, meta_ref, meta_all.at[chip], ((chip + s) % 4) * 2 + core) for s in range(1, 4)
    ]
    loads["swap"].wait()
    halves = []
    for half in range(2):
        halves.append(
            jnp.concatenate(
                [video_ref[64 * t : 64 * t + 64, 128 * half : 128 * half + 128] for t in range(4)],
                axis=1,
            )
        )
    packed = dot(jnp.concatenate(halves, axis=0), swap_ref[...]).astype(BF16)
    for index in range(8):
        half, quarter = index // 4, index % 4
        v_send[index] = packed[64 * half : 64 * half + 64, 128 * quarter : 128 * quarter + 128]
    v_copies = send_all(0, lambda to: v_send.at[to], v_all.at[me])
    v_all[me] = v_send[me]
    og_all[me] = og_ref[0].astype(F32).reshape(64, WIDE).astype(BF16)
    og_copies = spread_out(1, og_all)

    loads["dw"].wait()
    loads["pick"].wait()

    picks = None
    for tap in range(3):
        at = [(3 * b + tap) * WIDE for b in range(3)]
        rows = jnp.concatenate([dw_ref[:, low : low + WIDE] for low in at], axis=0)
        term = dot(rows, pick_ref[256 * tap : 256 * tap + 256, :])
        picks = term if picks is None else picks + term
    for other in range(4):
        w_send[other] = picks[:, 128 * other : 128 * other + 128].astype(BF16)
    w_all[chip] = w_send[chip]
    dw_copies = []
    for s in range(1, 4):
        to = (chip + s) % 4
        dw_copies.append(send(2, s, w_send.at[to], w_all.at[chip], to * 2 + core))

    arrived(meta_copies)
    place1 = lax.broadcasted_iota(jnp.int32, (1, 128), 1) // OWN
    start = jnp.zeros((1, 128), F32)
    high = jnp.zeros((1, 128), F32)
    width = jnp.zeros((1, 128), F32)
    for clip in range(4):
        start = jnp.where(place1 == clip, meta_all[clip, 0:1, :], start)
        high = jnp.where(place1 == clip, meta_all[clip, 1:2, :], high)
        width = jnp.where(place1 == clip, meta_all[clip, 2:3, :], width)
    count = (8.0 - start) * high * width * 8.0
    row_id = lax.broadcasted_iota(jnp.int32, (512, 128), 0)
    in_time = (row_id // 64).astype(F32) >= start
    in_rows = (row_id // 8 % 8).astype(F32) < high
    in_cols = (row_id % 8).astype(F32) < width
    mask_ref[...] = jnp.where(in_time & in_rows & in_cols, 1.0, 0.0)

    arrived(v_copies)
    stacked = jnp.concatenate(
        [
            jnp.concatenate([v_all[2 * other + c] for other in range(4)], axis=1)
            for c in range(2)
        ],
        axis=0,
    )
    unpacked = dot(stacked, swap_ref[...])
    for t in range(8):
        c, q = t // 4, t % 4
        cells[64 * t : 64 * t + 64, :] = unpacked[64 * c : 64 * c + 64, 128 * q : 128 * q + 128]
    mask = mask_ref[...]
    centre = group_total(jnp.sum(mask * cells[...], axis=0, keepdims=True)) / count
    offset = cells[...] - centre
    spread = group_total(jnp.sum(mask * offset * offset, axis=0, keepdims=True)) / count
    inverse = lax.rsqrt(spread + EPSILON)
    normed = offset * inverse
    normed_ref[...] = normed
    h_all[me] = (mask * (normed / (1.0 + jnp.exp(-normed)))).astype(BF16)
    h_copies = spread_out(4, h_all)

    relay(1, og_all, og_copies)
    complete(og_copies)
    up_row = lax.broadcasted_iota(jnp.int32, (128, 64), 0)
    up_col = lax.broadcasted_iota(jnp.int32, (128, 64), 1)
    lift = ((up_row // 8 == up_col // 4) & (up_row % 8 == 2 * (up_col % 4))).astype(F32).astype(BF16)
    for c in range(2):
        raised = [dot(lift, og_all[2 * clip + c]).reshape(16, 8, WIDE) for clip in range(4)]
        og_up[4 * c : 4 * c + 4] = (
            jnp.concatenate(raised, axis=1).astype(BF16).reshape(4, 4, 32, WIDE)
        )
    arrived(dw_copies)

    def res_grad_frame(t, carry):
        lhs = og_up[t].reshape(128, WIDE)
        layers = []
        for b in range(3):
            panel = w_all[:, 64 * b : 64 * b + 64, :].reshape(256, 128)
            layers.append(fold_taps(dot(lhs, panel), 4, (0, -1, -2)).reshape(4, 8, 128))
        even = layers[0] + jnp.concatenate([jnp.zeros((1, 8, 128), F32), layers[2][:3]], axis=0)
        both = jnp.stack([even, layers[1]], axis=1).reshape(64, 128)
        at = pl.ds(pl.multiple_of(64 * t, 64), 64)
        value = (mask_ref[at, :] * both).astype(BF16)
        g_all[me, at, :] = value
        wide = value.astype(F32)
        res_ref[at, :] = wide
        return carry

    lax.fori_loop(0, 8, res_grad_frame, 0)
    g_copies = [send(5, 0, g_all.at[me], g_all.at[me], sibling)]

    loads["cw"].wait()
    from_row = lax.broadcasted_iota(jnp.int32, (WIDE, 128), 0)
    to_lane = lax.broadcasted_iota(jnp.int32, (WIDE, 128), 1)
    chosen = from_row == to_lane // OWN * 64 + OWN * core + to_lane % OWN
    chosen = chosen.astype(F32).astype(BF16)
    for ab in range(9):
        at = [(3 * ab + tap) * WIDE for tap in range(3)]
        rows = jnp.concatenate([cw_ref[:, low : low + WIDE] for low in at], axis=0)
        low = 128 * (ab // 3)
        rows_back[ab % 3, 0:192, low : low + 128] = dot(rows, chosen).astype(BF16)
        rows_back[ab % 3, 192:256, low : low + 128] = jnp.zeros((64, 128), BF16)

    mine = pl.ds(pl.multiple_of(core * OWN, OWN), OWN)
    blank = jnp.zeros((32, WIDE), BF16)

    def turned(ref, block):
        rows = [ref[mine, (3 * block + c) * WIDE : (3 * block + c + 1) * WIDE] for c in range(3)]
        return jnp.concatenate(rows + [blank], axis=0).T

    for ab in range(9):
        low = 128 * (ab // 3)
        rows_fwd[ab % 3, :, low : low + 128] = turned(cw_ref, ab)
    for b in range(3):
        rows_down[b] = turned(dw_ref, b)

    edge = jnp.zeros((10, 32, WIDE), BF16)
    for t in range(2):
        h_full[t] = edge
        g_full[8 + t] = edge
    for t in range(8):
        for full, off in ((h_full, 2), (g_full, 0)):
            full[t + off, 0] = jnp.zeros((32, WIDE), BF16)
            full[t + off, 9] = jnp.zeros((32, WIDE), BF16)
        r_full[t, 4, 0] = jnp.zeros((32, WIDE), BF16)

    arrived(g_copies)
    place = lax.broadcasted_iota(jnp.int32, (64, 128), 1) // OWN

    def stack_frame(t, carry):
        at = pl.ds(pl.multiple_of(64 * t, 64), 64)
        moved = []
        for c in range(2):
            block = g_all[2 * chip + c, at, :].astype(F32)
            moved.append([move_cols(block, 1 - tap) for tap in range(3)])
        split = []
        for clip in range(4):
            sides = [jnp.zeros((64, 128), F32)] * 2
            for tap in range(3):
                for c in range(2):
                    spot = 2 * (tap % 2) + c
                    turn = (OWN * (spot - clip)) % 128
                    block = moved[c][tap]
                    if turn:
                        block = pltpu.roll(block, turn, 1)
                    sides[tap // 2] = jnp.where(place == spot, block, sides[tap // 2])
            split.append(jnp.concatenate(sides, axis=1).reshape(8, 8, WIDE))
        rows = jnp.concatenate(split, axis=1).reshape(256, WIDE)
        g_full[t, 1:9] = rows.astype(BF16).reshape(8, 32, WIDE)
        return carry

    lax.fori_loop(0, 8, stack_frame, 0)

    def three_taps(u, full, weights, shift, row_of):
        total = None
        for b in range(3):
            low = row_of(b)
            window = full[pl.ds(2 * u + shift, 2), low : low + 8].reshape(512, WIDE)
            term = dot(window, weights[b])
            total = term if total is None else total + term
        return [
            total[:, 128 * a : 128 * a + 128].reshape(2, 256, 128) for a in range(3)
        ]

    def back_pair(u, carry):
        parts = three_taps(u, g_full, rows_back, 0, lambda b: 2 - b)
        for a in range(3):
            at = pl.ds(2 * u + a, 2)
            sums[at] = sums[at] + parts[a]
        return carry

    def back_frame(t, carry):
        total = sums[t + 2]
        parts = total.reshape(8, 4, 8, 128)
        at = pl.ds(pl.multiple_of(64 * t, 64), 64)
        own = jnp.zeros((64, 128), F32)
        for other in range(4):
            piece = jnp.zeros((64, 128), F32)
            for clip in range(4):
                block = parts[:, clip].reshape(64, 128)
                turn = (OWN * (clip - other)) % 128
                if turn:
                    block = pltpu.roll(block, turn, 1)
                piece = jnp.where(place == clip, block, piece)
            p_send[other, at, :] = piece.astype(BF16)
            own = jnp.where(chip == other, piece, own)
        back_ref[at, :] = own
        return carry

    sums[...] = jnp.zeros((10, 256, 128), F32)
    lax.fori_loop(0, 4, back_pair, 0)
    lax.fori_loop(0, 4, back_frame, 0)
    relay(4, h_all, h_copies)
    lax.fori_loop(4, 8, back_frame, 0)
    p_copies = []
    for s in range(1, 4):
        to = (chip + s) % 4
        p_copies.append(send(10, s, p_send.at[to], p_all.at[s], to * 2 + core))

    def assemble(source, t):
        at = pl.ds(pl.multiple_of(256 * t, 256), 256)
        clips = gathered_lanes([source[d, at, :] for d in range(8)], swap_ref[...])
        blocks = [clip.reshape(32, 8, WIDE) for clip in clips]
        return jnp.concatenate(blocks, axis=1).astype(BF16).reshape(4, 8, 32, WIDE)

    def keep(index, source, target):
        copy = pltpu.make_async_copy(source, target, load_sems.at[index])
        copy.start()
        return copy

    kept = []

    complete(h_copies)

    def fill_hidden(t, carry):
        h_full[pl.ds(4 * t + 2, 4), 1:9] = assemble(h_all, t)
        return carry

    lax.fori_loop(0, 2, fill_hidden, 0)
    kept.append(keep(5, h_full, h_out))

    def conv_pair(u, carry):
        parts = three_taps(u, h_full, rows_fwd, 2, lambda b: b)
        for a in range(3):
            at = pl.ds(2 * u + 2 - a, 2)
            sums[at] = sums[at] + parts[a]
        return carry

    def conv_frame(t, carry):
        total = sums[t]
        folded = fold_taps(total, 8, (-1, 0, 1))
        at = pl.ds(pl.multiple_of(64 * t, 64), 64)
        r_all[me, at, :] = (mask_ref[at, :] * (cells[at, :] + folded)).astype(BF16)
        return carry

    sums[...] = jnp.zeros((10, 256, 128), F32)
    lax.fori_loop(0, 4, conv_pair, 0)
    lax.fori_loop(0, 8, conv_frame, 0)
    r_copies = spread_out(6, r_all)

    arrived(p_copies)
    mask = mask_ref[...]
    normed = normed_ref[...]
    gate = 1.0 / (1.0 + jnp.exp(-normed))
    back = back_ref[...]
    for s in range(1, 4):
        back = back + p_all[s].astype(F32)
    pushed = mask * back * gate * (1.0 + normed * (1.0 - gate))
    mean_push = group_total(jnp.sum(pushed, axis=0, keepdims=True)) / count
    mean_pair = group_total(jnp.sum(pushed * normed, axis=0, keepdims=True)) / count
    through = inverse * (pushed - mean_push - normed * mean_pair)
    back_ref[...] = mask * through + res_ref[...]
    for c in range(2):
        quarter = [back_ref[64 * (4 * c + q) : 64 * (4 * c + q) + 64, :] for q in range(4)]
        swapped = dot(jnp.concatenate(quarter, axis=1).astype(BF16), swap_ref[...]).astype(BF16)
        for other in range(4):
            x_send[2 * other + c] = swapped[:, 128 * other : 128 * other + 128]
    x_all[me] = x_send[me]
    x_copies = send_all(8, lambda to: x_send.at[to], x_all.at[me])

    relay(6, r_all, r_copies)

    def turn_frame(t, carry):
        stack_t[t] = g_full[t, 1:9].reshape(256, WIDE).T
        return carry

    lax.fori_loop(0, 8, turn_frame, 0)
    kept.append(keep(6, stack_t, stack_out))

    complete(r_copies)

    def fill_residual(t, carry):
        r_full[pl.ds(4 * t, 4), 0:4] = assemble(r_all, t).reshape(4, 4, 2, 32, WIDE)
        return carry

    lax.fori_loop(0, 2, fill_residual, 0)
    kept.append(keep(7, r_full, r_out))

    def down_frame(t, carry):
        total = None
        for b in range(3):
            window = r_full[t, b // 2 : b // 2 + 4, b % 2].reshape(128, WIDE)
            term = dot(window, rows_down[b])
            total = term if total is None else total + term
        folded = fold_taps(total, 4, (0, 1, 2)).astype(BF16)
        to_row = lax.broadcasted_iota(jnp.int32, (16, 32), 0)
        from_row = lax.broadcasted_iota(jnp.int32, (16, 32), 1)
        even = (from_row == to_row * 2).astype(F32).astype(BF16)
        d_send[t] = dot(even, folded).astype(BF16)
        return carry

    lax.fori_loop(0, 8, down_frame, 0)

    def frames_of(to):
        return pl.ds(4 * (to % 2), 4)

    d_all[me] = d_send[frames_of(me)]
    d_copies = send_all(7, lambda to: d_send.at[frames_of(to)], d_all.at[me])
    def og_frame(t, carry):
        from_row = lax.broadcasted_iota(jnp.int32, (WIDE, WIDE), 0)
        to_lane = lax.broadcasted_iota(jnp.int32, (WIDE, WIDE), 1)
        chosen = (from_row == to_lane % 64 + 64 * chip).astype(F32).astype(BF16)
        rows = dot(og_up[t].reshape(128, WIDE), chosen)
        tap = lax.broadcasted_iota(jnp.int32, (128, WIDE), 1) // 64
        once, twice = move_cols(rows, -1), move_cols(rows, -2)
        rows = jnp.where(tap == 0, rows, jnp.where(tap == 1, once, twice))
        og_stack_t[t] = rows.T.astype(BF16)
        return carry

    lax.fori_loop(0, 8, og_frame, 0)

    kept.append(keep(4, og_stack_t, og_stack_out))
    arrived(x_copies)
    arrived(d_copies)
    for copy in kept:
        copy.wait()
    for copies in (
        meta_copies, v_copies, og_copies, dw_copies, p_copies, h_copies, g_copies, r_copies, x_copies,
        d_copies,
    ):
        for copy in copies:
            copy.wait_send()


def finish_kernel(
    x_hbm, d_hbm, h_hbm, r_hbm, stack_hbm, og_stack_hbm, swap_hbm,
    down_ref, vgrad_ref, cgrad_hbm, dgrad_hbm,
    x_all, d_all, h_full, r_full, stack_t, og_stack_t, swap_ref, cgrad_ref, dgrad_ref,
    load_sems, store_sems,
):
    chip = lax.axis_index("fsdp")
    loads = []
    for index, (source, target) in enumerate(
        (
            (swap_hbm, swap_ref),
            (x_hbm, x_all),
            (d_hbm, d_all),
            (stack_hbm, stack_t),
            (h_hbm, h_full),
            (og_stack_hbm, og_stack_t),
            (r_hbm, r_full),
        )
    ):
        loads.append(pltpu.make_async_copy(source, target, load_sems.at[index]))
        loads[-1].start()
    for copy in loads[:3]:
        copy.wait()
    frames = gathered_lanes([x_all[d] for d in range(8)], swap_ref[...])
    for t, block in enumerate(frames):
        vgrad_ref[64 * t : 64 * t + 64, :] = block.astype(BF16)
    clips = gathered_lanes([d_all[d].reshape(64, 128) for d in range(8)], swap_ref[...])
    own = clips[0]
    for clip in range(1, 4):
        own = jnp.where(chip == clip, clips[clip], own)
    down_ref[0] = own.reshape(4, 4, 4, WIDE).astype(BF16)

    stores = []

    def put(grad, ref, hbm, block, index):
        for tap in range(3):
            at = (3 * block + tap) * WIDE
            ref[:, at : at + WIDE] = grad[64 * tap : 64 * tap + 64]
        part = pl.ds(3 * block * WIDE, 3 * WIDE)
        stores.append(pltpu.make_async_copy(ref.at[:, part], hbm.at[:, part], store_sems.at[index]))
        stores[-1].start()

    loads[3].wait()
    loads[4].wait()
    lhs = jnp.concatenate([stack_t[t, 0:192] for t in range(8)], axis=1)
    for a in range(3):
        for b in range(3):
            rhs = h_full[a : a + 8, b : b + 8].reshape(2048, WIDE)
            put(dot(lhs, rhs), cgrad_ref, cgrad_hbm, 3 * a + b, 3 * a + b)
    loads[5].wait()
    loads[6].wait()
    lhs = jnp.concatenate([og_stack_t[t, 0:192] for t in range(8)], axis=1)
    for b in range(3):
        rhs = r_full[:, b // 2 : b // 2 + 4, b % 2].reshape(1024, WIDE)
        put(dot(lhs, rhs), dgrad_ref, dgrad_hbm, b, 9 + b)
    for copy in stores:
        copy.wait()


def fused(video, conv_weight, down_weight, out_grad, clip_bucket, start_frame, bucket_res):
    vmem = pl.BlockSpec(memory_space=pltpu.VMEM)
    smem = pl.BlockSpec(memory_space=pltpu.SMEM)
    anywhere = pl.BlockSpec(memory_space=pl.ANY)
    full = pltpu.VMEM((10, 10, 32, WIDE), BF16)
    gathered = pltpu.VMEM((8, 512, 128), BF16)
    wide = pltpu.VMEM((512, 128), F32)
    piece = pltpu.VMEM((8, 64, 128), BF16)
    sent = jax.ShapeDtypeStruct((8, 64, 128), BF16)
    sent_down = jax.ShapeDtypeStruct((8, 4, 16, 128), BF16)
    full_cells = jax.ShapeDtypeStruct((10, 10, 32, WIDE), BF16)
    even_cells = jax.ShapeDtypeStruct((8, 5, 2, 32, WIDE), BF16)
    stack = jax.ShapeDtypeStruct((8, 256, 256), BF16)
    og_stack = jax.ShapeDtypeStruct((8, 256, 128), BF16)
    swap = lane_swap()
    parts = pl.pallas_call(
        block_kernel,
        out_shape=(sent, sent_down, full_cells, even_cells, stack, og_stack),
        in_specs=[smem] * 3 + [vmem, anywhere, anywhere, vmem] + [anywhere] * 2,
        out_specs=(vmem,) * 2 + (anywhere,) * 4,
        scratch_shapes=[
            pltpu.VMEM((8, 128), F32),
            pltpu.VMEM(conv_weight.shape, BF16),
            pltpu.VMEM(down_weight.shape, BF16),
            pltpu.VMEM((512, 512), BF16),
            pltpu.VMEM((768, 512), BF16),
            pltpu.VMEM((4, 8, 128), F32),
            piece,
            piece,
            pltpu.VMEM((4, 192, 128), BF16),
            pltpu.VMEM((4, 192, 128), BF16),
            pltpu.VMEM((8, 64, WIDE), BF16),
            gathered,
            gathered,
            gathered,
            pltpu.VMEM((8, 16, 128), BF16),
            piece,
            pltpu.VMEM((4, 512, 128), BF16),
            pltpu.VMEM((4, 512, 128), BF16),
            full,
            full,
            pltpu.VMEM((8, 5, 2, 32, WIDE), BF16),
            pltpu.VMEM((3, 256, 384), BF16),
            pltpu.VMEM((3, 256, 128), BF16),
            pltpu.VMEM((10, 256, 128), F32),
            pltpu.VMEM((8, 4, 32, WIDE), BF16),
            pltpu.VMEM((3, 256, 384), BF16),
            wide,
            wide,
            wide,
            wide,
            pltpu.VMEM((8, 256, 256), BF16),
            pltpu.VMEM((8, 256, 128), BF16),
            wide,
            pltpu.SemaphoreType.DMA((8,)),
            pltpu.SemaphoreType.DMA((11, 8)),
            pltpu.SemaphoreType.DMA((11, 8)),
        ],
        compiler_params=pltpu.CompilerParams(
            collective_id=0, has_side_effects=True, vmem_limit_bytes=60 * 2**20
        ),
    )(
        clip_bucket,
        start_frame,
        bucket_res.T,
        video.reshape(256, WIDE),
        conv_weight,
        down_weight,
        out_grad,
        swap,
        column_pick(),
    )
    kinds = (sent, sent_down, full_cells, even_cells, stack, og_stack, swap)
    down, video_grad, conv_grad, down_grad = pl.pallas_call(
        finish_kernel,
        out_shape=(
            jax.ShapeDtypeStruct(out_grad.shape, BF16),
            jax.ShapeDtypeStruct((256, WIDE), BF16),
            jax.ShapeDtypeStruct(conv_weight.shape, F32),
            jax.ShapeDtypeStruct(down_weight.shape, F32),
        ),
        in_specs=[anywhere] * 7,
        out_specs=(vmem, vmem, anywhere, anywhere),
        scratch_shapes=[pltpu.VMEM(kind.shape, BF16) for kind in kinds]
        + [
            pltpu.VMEM(conv_weight.shape, F32),
            pltpu.VMEM(down_weight.shape, F32),
            pltpu.SemaphoreType.DMA((7,)),
            pltpu.SemaphoreType.DMA((12,)),
        ],
        compiler_params=pltpu.CompilerParams(vmem_limit_bytes=60 * 2**20),
    )(*parts, swap)
    return (down, video_grad.reshape(video.shape), conv_grad, down_grad)


def solution(mesh):
    placed = (
        P(("mix", "fsdp"), "tile", None, None, None),
        P(("mix", "fsdp"), None),
        P(("mix", "fsdp"), None),
        P(("mix", "fsdp"), "tile", None, None, None),
        P(("mix", "fsdp")),
        P(("mix", "fsdp")),
        P(),
    )
    return jax.shard_map(
        fused if mesh.shape["tile"] == 2 and mesh.shape["fsdp"] == 4 else shards,
        mesh=mesh,
        in_specs=placed,
        out_specs=(
            P(("mix", "fsdp"), "tile", None, None, None),
            P(("mix", "fsdp"), "tile", None, None, None),
            P(("mix", "fsdp"), None),
            P(("mix", "fsdp"), None),
        ),
        check_vma=False,
    )
```

```python
import functools

import jax
import jax.numpy as jnp
import numpy as np
from jax import lax
from jax.experimental import pallas as pl
from jax.experimental.pallas import tpu as pltpu
from jax.sharding import PartitionSpec as P

GROUPS = 32


EPSILON = 1e-06


def shifted(block, axis, distance):
    devices = range(lax.axis_size(axis))
    route = [(i - distance, i) for i in devices if i - distance in devices]
    return lax.ppermute(block, axis, route)


def valid_mask(clip_bucket, start_frame, bucket_res, first_frame, frame_count, side_cells):
    bucket_ids = jnp.arange(bucket_res.shape[0], dtype=jnp.int32)
    picked = (clip_bucket[:, None] == bucket_ids[None, :]).astype(jnp.int32)
    limits = jnp.sum(picked[:, :, None] * bucket_res[None, :, :], axis=1)
    frame_ids = first_frame + jnp.arange(frame_count, dtype=jnp.int32)
    positions = jnp.arange(side_cells, dtype=jnp.int32)
    in_time = frame_ids[None, :] >= start_frame[:, None]
    in_rows = positions[None, :] < limits[:, 0:1]
    in_cols = positions[None, :] < limits[:, 1:2]
    inside = in_time[:, :, None, None] & in_rows[:, None, :, None] & in_cols[:, None, None, :]
    return (inside.astype(jnp.float32)[..., None], limits)


def time_group(padded, tap_time, out_frames, side_cells, flipped):
    channel_count = padded.shape[-1]
    time_start = 2 - tap_time if flipped else tap_time
    layers = []
    for tap_row in range(3):
        for tap_col in range(3):
            row_start = 2 - tap_row if flipped else tap_row
            col_start = 2 - tap_col if flipped else tap_col
            window = padded[
                :,
                time_start : time_start + out_frames,
                row_start : row_start + side_cells,
                col_start : col_start + side_cells,
                :,
            ]
            layers.append(window.reshape(-1, channel_count))
    return jnp.stack(layers)


def stride_taps(padded, side_cells):
    channel_count = padded.shape[-1]
    layers = []
    for tap_row in range(3):
        for tap_col in range(3):
            window = padded[
                :, :, tap_row : tap_row + side_cells : 2, tap_col : tap_col + side_cells : 2, :
            ]
            layers.append(window.reshape(-1, channel_count))
    return jnp.stack(layers)


def weight_terms(grad_rows, slabs, cot_rows, hidden_padded, frame_count, side_cells):
    out_rows = grad_rows.shape[1]
    down_term = lax.dot_general(
        grad_rows, slabs, (((0,), (1,)), ((), ())), preferred_element_type=jnp.float32
    ).reshape(out_rows, -1)
    conv_parts = []
    for tap_time in range(3):
        group = time_group(hidden_padded, tap_time, frame_count, side_cells, False)
        conv_parts.append(
            lax.dot_general(
                cot_rows, group, (((0,), (1,)), ((), ())), preferred_element_type=jnp.float32
            )
        )
    conv_term = jnp.concatenate(conv_parts, axis=1).reshape(out_rows, -1)
    return (conv_term, down_term)


def transpose_conv(grad_padded, conv_weight, out_frames, side_cells):
    channel_count = grad_padded.shape[-1]
    row_total = grad_padded.shape[0] * out_frames * side_cells * side_cells
    initial = jnp.zeros((row_total, channel_count), jnp.float32)
    running = initial
    weight_panel = lax.all_gather(conv_weight, "fsdp", axis=0, tiled=True)
    panel_rows = weight_panel.shape[0]
    panel = weight_panel.reshape(panel_rows, 27, channel_count)
    for tap_time in range(3):
        group = time_group(grad_padded, tap_time, out_frames, side_cells, True)
        running = running + lax.dot_general(
            group,
            panel[:, 9 * tap_time : 9 * tap_time + 9, :],
            (((0, 2), (1, 0)), ((), ())),
            preferred_element_type=jnp.float32,
        )
    return running


def shards(video, conv_weight, down_weight, out_grad, clip_bucket, start_frame, bucket_res):
    clip_count, frame_count, side_cells, side_again, channel_count = video.shape
    half_side = side_cells // 2
    group_width = channel_count // GROUPS
    tiles = lax.axis_size("tile")
    mask, limits = valid_mask(
        clip_bucket,
        start_frame,
        bucket_res,
        lax.axis_index("tile") * frame_count,
        frame_count,
        side_cells,
    )
    valid_count = (
        (frame_count * tiles - start_frame) * limits[:, 0] * limits[:, 1] * group_width
    ).astype(jnp.float32)
    grouped_shape = (clip_count, frame_count, side_cells, side_cells, GROUPS, group_width)
    summed_axes = (1, 2, 3, 5)
    cell_weight = mask[..., None]
    grouped = video.astype(jnp.float32).reshape(grouped_shape)
    first_sum = lax.psum(jnp.sum(grouped * cell_weight, axis=summed_axes), "tile")
    centre = first_sum / valid_count[:, None]
    offset = grouped - centre[:, None, None, None, :, None]
    second_sum = lax.psum(jnp.sum(cell_weight * offset * offset, axis=summed_axes), "tile")
    spread = second_sum / valid_count[:, None]
    inverse = lax.rsqrt(spread + EPSILON)
    normed_grouped = offset * inverse[:, None, None, None, :, None]
    normed = normed_grouped.reshape(video.shape)
    hidden = (mask * jax.nn.silu(normed)).astype(jnp.bfloat16)
    past = shifted(hidden[:, frame_count - 2 :], "tile", 1)
    hidden_padded = jnp.pad(
        jnp.concatenate([past, hidden], axis=1), ((0, 0), (0, 0), (1, 1), (1, 1), (0, 0))
    )

    def conv_columns(weight_panel):
        panel = weight_panel.reshape(weight_panel.shape[0], 27, channel_count)
        summed = None
        for tap_time in range(3):
            group = time_group(hidden_padded, tap_time, frame_count, side_cells, False)
            term = lax.dot_general(
                group,
                panel[:, 9 * tap_time : 9 * tap_time + 9, :],
                (((0, 2), (1, 2)), ((), ())),
                preferred_element_type=jnp.float32,
            )
            summed = term if summed is None else summed + term
        return summed

    conv_out = conv_columns(lax.all_gather(conv_weight, "fsdp", axis=0, tiled=True))
    residual = (mask * (video.astype(jnp.float32) + conv_out.reshape(video.shape))).astype(
        jnp.bfloat16
    )
    down_slabs = stride_taps(
        jnp.pad(residual, ((0, 0), (0, 0), (0, 1), (0, 1), (0, 0))), side_cells
    )
    weight_panel = lax.all_gather(down_weight, "fsdp", axis=0, tiled=True)
    panel = weight_panel.reshape(weight_panel.shape[0], 9, channel_count)
    down_out = lax.dot_general(
        down_slabs, panel, (((0, 2), (1, 2)), ((), ())), preferred_element_type=jnp.float32
    )
    down = down_out.astype(jnp.bfloat16).reshape(
        clip_count, frame_count, half_side, half_side, channel_count
    )
    grad_flat = out_grad.reshape(-1, channel_count)
    weight_panel = lax.all_gather(down_weight, "fsdp", axis=0, tiled=True)
    panel_rows = weight_panel.shape[0]
    panel = weight_panel.reshape(panel_rows, 9, channel_count)
    tap_grads = lax.dot_general(
        grad_flat, panel, (((1,), (0,)), ((), ())), preferred_element_type=jnp.float32
    )
    spread_back = jnp.zeros(
        (clip_count, frame_count, side_cells + 1, side_cells + 1, channel_count), jnp.float32
    )
    for tap_row in range(3):
        for tap_col in range(3):
            term = tap_grads[:, tap_row * 3 + tap_col, :].reshape(
                clip_count, frame_count, half_side, half_side, channel_count
            )
            spread_back = spread_back.at[
                :, :, tap_row : tap_row + side_cells : 2, tap_col : tap_col + side_cells : 2, :
            ].add(term)
    res_grad = (mask * spread_back[:, :, :side_cells, :side_cells, :]).astype(jnp.bfloat16)
    res_flat = res_grad.reshape(-1, channel_count)
    later = shifted(res_grad[:, :2], "tile", -1)
    grad_padded = jnp.pad(
        jnp.concatenate([res_grad, later], axis=1), ((0, 0), (0, 0), (1, 1), (1, 1), (0, 0))
    )
    back_hidden = transpose_conv(grad_padded, conv_weight, frame_count, side_cells).reshape(
        video.shape
    )
    gate_value = jax.nn.sigmoid(normed)
    pushed = mask * back_hidden * gate_value * (1.0 + normed * (1.0 - gate_value))
    pushed_grouped = pushed.reshape(grouped_shape)
    push_sum, pair_sum = lax.psum(
        (
            jnp.sum(pushed_grouped, axis=summed_axes),
            jnp.sum(pushed_grouped * normed_grouped, axis=summed_axes),
        ),
        "tile",
    )
    mean_push = push_sum / valid_count[:, None]
    mean_pair = pair_sum / valid_count[:, None]
    through_norm = inverse[:, None, None, None, :, None] * (
        pushed_grouped
        - mean_push[:, None, None, None, :, None]
        - normed_grouped * mean_pair[:, None, None, None, :, None]
    )
    video_grad = (mask * through_norm.reshape(video.shape) + res_grad.astype(jnp.float32)).astype(
        jnp.bfloat16
    )
    conv_term, down_term = weight_terms(
        grad_flat, down_slabs, res_flat, hidden_padded, frame_count, side_cells
    )
    conv_share, down_share = (
        lax.psum_scatter(conv_term, ("fsdp", "tile"), scatter_dimension=0, tiled=True),
        lax.psum_scatter(down_term, ("fsdp", "tile"), scatter_dimension=0, tiled=True),
    )
    conv_weight_grad, down_weight_grad = (
        lax.all_gather(conv_share, "tile", axis=0, tiled=True),
        lax.all_gather(down_share, "tile", axis=0, tiled=True),
    )
    return (down, video_grad, conv_weight_grad, down_weight_grad)


F32 = jnp.float32
BF16 = jnp.bfloat16
MESH = pl.DeviceIdType.MESH
WIDE = 256
OWN = 32


def lane_swap():
    lane = np.arange(512)
    outer, inner, channel = lane // 128, lane // 32 % 4, lane % 32
    table = np.zeros((512, 512), np.float32)
    table[lane, inner * 128 + outer * 32 + channel] = 1.0
    return jnp.asarray(table, BF16)


def column_pick():
    table = np.zeros((2, 3, 256, 4, 4, 32), np.float32)
    for core in range(2):
        for tap in range(3):
            for chip in range(4):
                for channel in range(32):
                    table[core, tap, 64 * chip + 32 * core + channel, chip, tap, channel] = 1.0
    return jnp.asarray(table.reshape(2, 768, 512), BF16)


def dot(lhs, rhs):
    return jnp.dot(lhs, rhs, preferred_element_type=F32)


def move_cols(block, distance):
    if distance == 0:
        return block
    rows = block.shape[0]
    col = (lax.broadcasted_iota(jnp.int32, block.shape, 0) & 7) + distance
    turned = pltpu.roll(block, (-distance) % rows, 0)
    return jnp.where((col >= 0) & (col < 8), turned, 0.0)


def fold_taps(result, outer, distances):
    parts = result.reshape(outer, 4, 8, 128)
    place = lax.broadcasted_iota(jnp.int32, (outer * 8, 128), 1) >> 5
    total = None
    for tap in range(3):
        layer = jnp.zeros((outer * 8, 128), F32)
        for clip in range(4):
            block = parts[:, clip].reshape(outer * 8, 128)
            turn = (OWN * (clip - tap)) % 128
            if turn:
                block = pltpu.roll(block, turn, 1)
            layer = jnp.where(place == clip, block, layer)
        layer = move_cols(layer, distances[tap])
        total = layer if total is None else total + layer
    return total


def group_total(row):
    first = lax.broadcasted_iota(jnp.int32, (128, 128), 0) >> 3
    second = lax.broadcasted_iota(jnp.int32, (128, 128), 1) >> 3
    same = (first == second).astype(F32)
    wide = jnp.broadcast_to(row, (8, 128))
    return jnp.dot(wide, same, preferred_element_type=F32, precision=lax.Precision.HIGHEST)[0:1]


def gathered_lanes(pieces, swap):
    halves = [
        dot(jnp.concatenate(pieces[4 * half : 4 * half + 4], axis=1), swap) for half in range(2)
    ]
    return [
        jnp.concatenate([half[:, 128 * p : 128 * p + 128] for half in halves], axis=1)
        for p in range(4)
    ]


def block_kernel(
    bucket_ref, start_ref, res_table_ref, video_ref, cw_hbm, dw_hbm, og_ref, swap_hbm,
    pick_hbm,
    x_all, d_all, h_out, r_out, stack_out, og_stack_out,
    meta_ref, cw_ref, dw_ref, swap_ref, pick_ref,
    meta_all, v_send, v_all, w_send, w_all, og_all, h_all, g_all, r_all, d_send,
    x_send, p_send, p_all, h_full, g_full, r_full, rows_back, rows_down, sums, og_up, rows_fwd, cells, normed_ref, mask_ref,
    res_ref, stack_t, og_stack_t, back_ref, load_sems, send_sems, recv_sems,
):
    chip = lax.axis_index("fsdp")
    core = lax.axis_index("tile")
    me = chip * 2 + core
    sibling = chip * 2 + (1 - core)

    def peer(index):
        return {"fsdp": index // 2, "tile": index % 2}

    loads = {}
    for index, (name, source, target) in enumerate(
        (
            ("swap", swap_hbm, swap_ref),
            ("dw", dw_hbm, dw_ref),
            ("pick", pick_hbm.at[core], pick_ref),
            ("cw", cw_hbm, cw_ref),
        )
    ):
        loads[name] = pltpu.make_async_copy(source, target, load_sems.at[index])
        loads[name].start()

    barrier = pltpu.get_barrier_semaphore()
    for step in range(1, 8):
        pl.semaphore_signal(barrier, inc=1, device_id=peer((me + step) % 8), device_id_type=MESH)
    pl.semaphore_wait(barrier, 7)

    def send(phase, step, src, dst, to):
        copy = pltpu.make_async_remote_copy(
            src_ref=src, dst_ref=dst, send_sem=send_sems.at[phase, step],
            recv_sem=recv_sems.at[phase, step], device_id=peer(to), device_id_type=MESH,
        )
        copy.start()
        return copy

    def send_all(phase, source, target):
        return [send(phase, s, source((me + s) % 8), target, (me + s) % 8) for s in range(1, 8)]

    def spread_out(phase, target):
        copies = [send(phase, 4, target.at[me], target.at[me], sibling)]
        for s in range(1, 4):
            copies.append(send(phase, s, target.at[me], target.at[me], ((chip + s) % 4) * 2 + core))
        return copies

    def relay(phase, target, copies):
        passed = []
        for s in range(1, 4):
            copies[s].wait_recv()
            slot = ((chip + 4 - s) % 4) * 2 + core
            passed.append(send(phase, 4 + s, target.at[slot], target.at[slot], sibling))
        copies.extend(passed)

    def complete(copies):
        copies[0].wait_recv()
        for copy in copies[4:]:
            copy.wait_recv()

    def arrived(copies):
        for copy in copies:
            copy.wait_recv()

    bucket = bucket_ref[0]
    high, width = jnp.int32(0), jnp.int32(0)
    for index in range(res_table_ref.shape[1]):
        high = high + jnp.where(bucket == index, res_table_ref[0, index], 0)
        width = width + jnp.where(bucket == index, res_table_ref[1, index], 0)
    line = lax.broadcasted_iota(jnp.int32, (8, 128), 0)
    facts = jnp.where(line == 0, start_ref[0], jnp.where(line == 1, high, width)).astype(F32)
    meta_ref[...] = facts
    meta_all[chip] = facts
    meta_copies = [
        send(3, s, meta_ref, meta_all.at[chip], ((chip + s) % 4) * 2 + core) for s in range(1, 4)
    ]
    loads["swap"].wait()
    halves = []
    for half in range(2):
        halves.append(
            jnp.concatenate(
                [video_ref[64 * t : 64 * t + 64, 128 * half : 128 * half + 128] for t in range(4)],
                axis=1,
            )
        )
    packed = dot(jnp.concatenate(halves, axis=0), swap_ref[...]).astype(BF16)
    for index in range(8):
        half, quarter = index // 4, index % 4
        v_send[index] = packed[64 * half : 64 * half + 64, 128 * quarter : 128 * quarter + 128]
    v_copies = send_all(0, lambda to: v_send.at[to], v_all.at[me])
    v_all[me] = v_send[me]
    og_all[me] = og_ref[0].astype(F32).reshape(64, WIDE).astype(BF16)
    og_copies = spread_out(1, og_all)

    loads["dw"].wait()
    loads["pick"].wait()

    picks = None
    for tap in range(3):
        at = [(3 * b + tap) * WIDE for b in range(3)]
        rows = jnp.concatenate([dw_ref[:, low : low + WIDE] for low in at], axis=0)
        term = dot(rows, pick_ref[256 * tap : 256 * tap + 256, :])
        picks = term if picks is None else picks + term
    for other in range(4):
        w_send[other] = picks[:, 128 * other : 128 * other + 128].astype(BF16)
    w_all[chip] = w_send[chip]
    dw_copies = []
    for s in range(1, 4):
        to = (chip + s) % 4
        dw_copies.append(send(2, s, w_send.at[to], w_all.at[chip], to * 2 + core))

    loads["cw"].wait()
    from_row = lax.broadcasted_iota(jnp.int32, (WIDE, 128), 0)
    to_lane = lax.broadcasted_iota(jnp.int32, (WIDE, 128), 1)
    chosen = from_row == (to_lane >> 5) * 64 + OWN * core + (to_lane & 31)
    chosen = chosen.astype(F32).astype(BF16)
    for ab in range(9):
        at = [(3 * ab + tap) * WIDE for tap in range(3)]
        rows = jnp.concatenate([cw_ref[:, low : low + WIDE] for low in at], axis=0)
        low = 128 * (ab // 3)
        rows_back[ab % 3, 0:192, low : low + 128] = dot(rows, chosen).astype(BF16)
        rows_back[ab % 3, 192:256, low : low + 128] = jnp.zeros((64, 128), BF16)

    mine = pl.ds(pl.multiple_of(core * OWN, OWN), OWN)
    blank = jnp.zeros((32, WIDE), BF16)

    def turned(ref, block):
        rows = [ref[mine, (3 * block + c) * WIDE : (3 * block + c + 1) * WIDE] for c in range(3)]
        return jnp.concatenate(rows + [blank], axis=0).T

    for ab in range(9):
        low = 128 * (ab // 3)
        rows_fwd[ab % 3, :, low : low + 128] = turned(cw_ref, ab)
    for b in range(3):
        rows_down[b] = turned(dw_ref, b)

    sums[...] = jnp.zeros((10, 256, 128), F32)
    edge = jnp.zeros((10, 32, WIDE), BF16)
    for t in range(2):
        h_full[t] = edge
        g_full[8 + t] = edge
    for t in range(8):
        for full, off in ((h_full, 2), (g_full, 0)):
            full[t + off, 0] = jnp.zeros((32, WIDE), BF16)
            full[t + off, 9] = jnp.zeros((32, WIDE), BF16)
        r_full[t, 4, 0] = jnp.zeros((32, WIDE), BF16)

    arrived(meta_copies)
    place1 = lax.broadcasted_iota(jnp.int32, (1, 128), 1) >> 5
    start = jnp.zeros((1, 128), F32)
    high = jnp.zeros((1, 128), F32)
    width = jnp.zeros((1, 128), F32)
    for clip in range(4):
        start = jnp.where(place1 == clip, meta_all[clip, 0:1, :], start)
        high = jnp.where(place1 == clip, meta_all[clip, 1:2, :], high)
        width = jnp.where(place1 == clip, meta_all[clip, 2:3, :], width)
    count = (8.0 - start) * high * width * 8.0
    row_id = lax.broadcasted_iota(jnp.int32, (512, 128), 0)
    in_time = (row_id >> 6).astype(F32) >= start
    in_rows = ((row_id >> 3) & 7).astype(F32) < high
    in_cols = (row_id & 7).astype(F32) < width
    mask_ref[...] = jnp.where(in_time & in_rows & in_cols, 1.0, 0.0)

    arrived(v_copies)
    relay(1, og_all, og_copies)
    stacked = jnp.concatenate(
        [
            jnp.concatenate([v_all[2 * other + c] for other in range(4)], axis=1)
            for c in range(2)
        ],
        axis=0,
    )
    unpacked = dot(stacked, swap_ref[...])
    for t in range(8):
        c, q = t // 4, t % 4
        cells[64 * t : 64 * t + 64, :] = unpacked[64 * c : 64 * c + 64, 128 * q : 128 * q + 128]
    mask = mask_ref[...]
    centre = group_total(jnp.sum(mask * cells[...], axis=0, keepdims=True)) / count
    offset = cells[...] - centre
    spread = group_total(jnp.sum(mask * offset * offset, axis=0, keepdims=True)) / count
    inverse = lax.rsqrt(spread + EPSILON)
    normed = offset * inverse
    normed_ref[...] = normed
    h_all[me] = (mask * (normed / (1.0 + jnp.exp(-normed)))).astype(BF16)
    h_copies = spread_out(4, h_all)

    complete(og_copies)
    up_row = lax.broadcasted_iota(jnp.int32, (128, 64), 0)
    up_col = lax.broadcasted_iota(jnp.int32, (128, 64), 1)
    lift = ((up_row >> 3 == up_col >> 2) & ((up_row & 7) == 2 * (up_col & 3))).astype(F32).astype(BF16)
    for c in range(2):
        raised = [dot(lift, og_all[2 * clip + c]).reshape(16, 8, WIDE) for clip in range(4)]
        og_up[4 * c : 4 * c + 4] = (
            jnp.concatenate(raised, axis=1).astype(BF16).reshape(4, 4, 32, WIDE)
        )
    arrived(dw_copies)

    def res_grad_frame(t, carry):
        lhs = og_up[t].reshape(128, WIDE)
        layers = []
        for b in range(3):
            panel = w_all[:, 64 * b : 64 * b + 64, :].reshape(256, 128)
            layers.append(fold_taps(dot(lhs, panel), 4, (0, -1, -2)).reshape(4, 8, 128))
        even = layers[0] + jnp.concatenate([jnp.zeros((1, 8, 128), F32), layers[2][:3]], axis=0)
        both = jnp.stack([even, layers[1]], axis=1).reshape(64, 128)
        at = pl.ds(pl.multiple_of(64 * t, 64), 64)
        value = (mask_ref[at, :] * both).astype(BF16)
        g_all[me, at, :] = value
        wide = value.astype(F32)
        res_ref[at, :] = wide
        return carry

    lax.fori_loop(0, 8, res_grad_frame, 0)
    g_copies = [send(5, 0, g_all.at[me], g_all.at[me], sibling)]

    def keep(index, source, target):
        copy = pltpu.make_async_copy(source, target, load_sems.at[index])
        copy.start()
        return copy

    kept = []

    from_row = lax.broadcasted_iota(jnp.int32, (WIDE, WIDE), 0)
    to_lane = lax.broadcasted_iota(jnp.int32, (WIDE, WIDE), 1)
    own_rows = (from_row == (to_lane & 63) + 64 * chip).astype(F32).astype(BF16)

    def og_frame(t, carry):
        rows = dot(og_up[t].reshape(128, WIDE), own_rows)
        tap = lax.broadcasted_iota(jnp.int32, (128, WIDE), 1) >> 6
        once, twice = move_cols(rows, -1), move_cols(rows, -2)
        rows = jnp.where(tap == 0, rows, jnp.where(tap == 1, once, twice))
        og_stack_t[t] = rows.T.astype(BF16)
        return carry

    lax.fori_loop(0, 8, og_frame, 0)

    kept.append(keep(4, og_stack_t, og_stack_out))
    arrived(g_copies)
    place = lax.broadcasted_iota(jnp.int32, (64, 128), 1) >> 5

    def stack_frame(t, carry):
        at = pl.ds(pl.multiple_of(64 * t, 64), 64)
        moved = []
        for c in range(2):
            block = g_all[2 * chip + c, at, :].astype(F32)
            moved.append([move_cols(block, 1 - tap) for tap in range(3)])
        split = []
        for clip in range(4):
            sides = [jnp.zeros((64, 128), F32)] * 2
            for tap in range(3):
                for c in range(2):
                    spot = 2 * (tap % 2) + c
                    turn = (OWN * (spot - clip)) % 128
                    block = moved[c][tap]
                    if turn:
                        block = pltpu.roll(block, turn, 1)
                    sides[tap // 2] = jnp.where(place == spot, block, sides[tap // 2])
            split.append(jnp.concatenate(sides, axis=1).reshape(8, 8, WIDE))
        rows = jnp.concatenate(split, axis=1).reshape(256, WIDE)
        g_full[t, 1:9] = rows.astype(BF16).reshape(8, 32, WIDE)
        return carry

    lax.fori_loop(0, 8, stack_frame, 0)

    def three_taps(u, full, weights, shift, row_of):
        total = None
        for b in range(3):
            low = row_of(b)
            window = full[pl.ds(2 * u + shift, 2), low : low + 8].reshape(512, WIDE)
            term = dot(window, weights[b])
            total = term if total is None else total + term
        return [
            total[:, 128 * a : 128 * a + 128].reshape(2, 256, 128) for a in range(3)
        ]

    def back_pair(u, carry):
        parts = three_taps(u, g_full, rows_back, 0, lambda b: 2 - b)
        for a in range(3):
            at = pl.ds(2 * u + a, 2)
            sums[at] = sums[at] + parts[a]
        return carry

    def back_frame(t, carry):
        total = sums[t + 2]
        parts = total.reshape(8, 4, 8, 128)
        at = pl.ds(pl.multiple_of(64 * t, 64), 64)
        own = jnp.zeros((64, 128), F32)
        for other in range(4):
            piece = jnp.zeros((64, 128), F32)
            for clip in range(4):
                block = parts[:, clip].reshape(64, 128)
                turn = (OWN * (clip - other)) % 128
                if turn:
                    block = pltpu.roll(block, turn, 1)
                piece = jnp.where(place == clip, block, piece)
            p_send[other, at, :] = piece.astype(BF16)
            own = jnp.where(chip == other, piece, own)
        back_ref[at, :] = own
        return carry

    lax.fori_loop(0, 4, back_pair, 0)
    relay(4, h_all, h_copies)
    lax.fori_loop(0, 8, back_frame, 0)
    p_copies = []
    for s in range(1, 4):
        to = (chip + s) % 4
        p_copies.append(send(10, s, p_send.at[to], p_all.at[s], to * 2 + core))

    def assemble(source, t):
        at = pl.ds(pl.multiple_of(256 * t, 256), 256)
        clips = gathered_lanes([source[d, at, :] for d in range(8)], swap_ref[...])
        blocks = [clip.reshape(32, 8, WIDE) for clip in clips]
        return jnp.concatenate(blocks, axis=1).astype(BF16).reshape(4, 8, 32, WIDE)

    complete(h_copies)

    def fill_hidden(t, carry):
        h_full[pl.ds(4 * t + 2, 4), 1:9] = assemble(h_all, t)
        return carry

    lax.fori_loop(0, 2, fill_hidden, 0)
    kept.append(keep(5, h_full, h_out))

    def conv_pair(u, carry):
        parts = three_taps(u, h_full, rows_fwd, 2, lambda b: b)
        for a in range(3):
            at = pl.ds(2 * u + 2 - a, 2)
            sums[at] = sums[at] + parts[a]
        return carry

    def conv_frame(t, carry):
        total = sums[t]
        folded = fold_taps(total, 8, (-1, 0, 1))
        at = pl.ds(pl.multiple_of(64 * t, 64), 64)
        r_all[me, at, :] = (mask_ref[at, :] * (cells[at, :] + folded)).astype(BF16)
        return carry

    sums[...] = jnp.zeros((10, 256, 128), F32)
    lax.fori_loop(0, 4, conv_pair, 0)
    lax.fori_loop(0, 8, conv_frame, 0)
    r_copies = spread_out(6, r_all)

    arrived(p_copies)
    mask = mask_ref[...]
    normed = normed_ref[...]
    gate = 1.0 / (1.0 + jnp.exp(-normed))
    back = back_ref[...]
    for s in range(1, 4):
        back = back + p_all[s].astype(F32)
    pushed = mask * back * gate * (1.0 + normed * (1.0 - gate))
    mean_push = group_total(jnp.sum(pushed, axis=0, keepdims=True)) / count
    mean_pair = group_total(jnp.sum(pushed * normed, axis=0, keepdims=True)) / count
    through = inverse * (pushed - mean_push - normed * mean_pair)
    back_ref[...] = mask * through + res_ref[...]
    for c in range(2):
        quarter = [back_ref[64 * (4 * c + q) : 64 * (4 * c + q) + 64, :] for q in range(4)]
        swapped = dot(jnp.concatenate(quarter, axis=1).astype(BF16), swap_ref[...]).astype(BF16)
        for other in range(4):
            x_send[2 * other + c] = swapped[:, 128 * other : 128 * other + 128]
    x_all[me] = x_send[me]
    x_copies = send_all(8, lambda to: x_send.at[to], x_all.at[me])

    relay(6, r_all, r_copies)

    def turn_frame(t, carry):
        stack_t[t] = g_full[t, 1:9].reshape(256, WIDE).T
        return carry

    lax.fori_loop(0, 4, turn_frame, 0)

    complete(r_copies)

    def fill_residual(t, carry):
        r_full[pl.ds(4 * t, 4), 0:4] = assemble(r_all, t).reshape(4, 4, 2, 32, WIDE)
        return carry

    lax.fori_loop(0, 2, fill_residual, 0)
    kept.append(keep(7, r_full, r_out))

    def down_frame(t, carry):
        total = None
        for b in range(3):
            window = r_full[t, b // 2 : b // 2 + 4, b % 2].reshape(128, WIDE)
            term = dot(window, rows_down[b])
            total = term if total is None else total + term
        folded = fold_taps(total, 4, (0, 1, 2)).astype(BF16)
        to_row = lax.broadcasted_iota(jnp.int32, (16, 32), 0)
        from_row = lax.broadcasted_iota(jnp.int32, (16, 32), 1)
        even = (from_row == to_row * 2).astype(F32).astype(BF16)
        d_send[t] = dot(even, folded).astype(BF16)
        return carry

    lax.fori_loop(0, 8, down_frame, 0)

    def frames_of(to):
        return pl.ds(4 * (to % 2), 4)

    d_all[me] = d_send[frames_of(me)]
    d_copies = send_all(7, lambda to: d_send.at[frames_of(to)], d_all.at[me])
    lax.fori_loop(4, 8, turn_frame, 0)
    kept.append(keep(6, stack_t, stack_out))

    arrived(x_copies)
    arrived(d_copies)
    for copy in kept:
        copy.wait()
    for copies in (
        meta_copies, v_copies, og_copies, dw_copies, p_copies, h_copies, g_copies, r_copies, x_copies,
        d_copies,
    ):
        for copy in copies:
            copy.wait_send()


def finish_kernel(
    x_hbm, d_hbm, h_hbm, r_hbm, stack_hbm, og_stack_hbm, swap_hbm,
    down_ref, vgrad_ref, cgrad_hbm, dgrad_hbm,
    x_all, d_all, h_full, r_full, stack_t, og_stack_t, swap_ref, cgrad_ref, dgrad_ref,
    load_sems, store_sems,
):
    chip = lax.axis_index("fsdp")
    loads = []
    for index, (source, target) in enumerate(
        (
            (swap_hbm, swap_ref),
            (x_hbm, x_all),
            (d_hbm, d_all),
            (stack_hbm, stack_t),
            (h_hbm, h_full),
            (og_stack_hbm, og_stack_t),
            (r_hbm, r_full),
        )
    ):
        loads.append(pltpu.make_async_copy(source, target, load_sems.at[index]))
        loads[-1].start()
    for copy in loads[:3]:
        copy.wait()
    frames = gathered_lanes([x_all[d] for d in range(8)], swap_ref[...])
    for t, block in enumerate(frames):
        vgrad_ref[64 * t : 64 * t + 64, :] = block.astype(BF16)
    clips = gathered_lanes([d_all[d].reshape(64, 128) for d in range(8)], swap_ref[...])
    own = clips[0]
    for clip in range(1, 4):
        own = jnp.where(chip == clip, clips[clip], own)
    down_ref[0] = own.reshape(4, 4, 4, WIDE).astype(BF16)

    stores = []

    def put(grad, ref, hbm, block, index):
        for tap in range(3):
            at = (3 * block + tap) * WIDE
            ref[:, at : at + WIDE] = grad[64 * tap : 64 * tap + 64]
        part = pl.ds(3 * block * WIDE, 3 * WIDE)
        stores.append(pltpu.make_async_copy(ref.at[:, part], hbm.at[:, part], store_sems.at[index]))
        stores[-1].start()

    loads[3].wait()
    loads[4].wait()
    lhs = jnp.concatenate([stack_t[t, 0:192] for t in range(8)], axis=1)
    for a in range(3):
        for b in range(3):
            rhs = h_full[a : a + 8, b : b + 8].reshape(2048, WIDE)
            put(dot(lhs, rhs), cgrad_ref, cgrad_hbm, 3 * a + b, 3 * a + b)
    loads[5].wait()
    loads[6].wait()
    lhs = jnp.concatenate([og_stack_t[t, 0:192] for t in range(8)], axis=1)
    for b in range(3):
        rhs = r_full[:, b // 2 : b // 2 + 4, b % 2].reshape(1024, WIDE)
        put(dot(lhs, rhs), dgrad_ref, dgrad_hbm, b, 9 + b)
    for copy in stores:
        copy.wait()


def fused(video, conv_weight, down_weight, out_grad, clip_bucket, start_frame, bucket_res):
    vmem = pl.BlockSpec(memory_space=pltpu.VMEM)
    smem = pl.BlockSpec(memory_space=pltpu.SMEM)
    anywhere = pl.BlockSpec(memory_space=pl.ANY)
    full = pltpu.VMEM((10, 10, 32, WIDE), BF16)
    gathered = pltpu.VMEM((8, 512, 128), BF16)
    wide = pltpu.VMEM((512, 128), F32)
    piece = pltpu.VMEM((8, 64, 128), BF16)
    sent = jax.ShapeDtypeStruct((8, 64, 128), BF16)
    sent_down = jax.ShapeDtypeStruct((8, 4, 16, 128), BF16)
    full_cells = jax.ShapeDtypeStruct((10, 10, 32, WIDE), BF16)
    even_cells = jax.ShapeDtypeStruct((8, 5, 2, 32, WIDE), BF16)
    stack = jax.ShapeDtypeStruct((8, 256, 256), BF16)
    og_stack = jax.ShapeDtypeStruct((8, 256, 128), BF16)
    swap = lane_swap()
    parts = pl.pallas_call(
        block_kernel,
        out_shape=(sent, sent_down, full_cells, even_cells, stack, og_stack),
        in_specs=[smem] * 3 + [vmem, anywhere, anywhere, vmem] + [anywhere] * 2,
        out_specs=(vmem,) * 2 + (anywhere,) * 4,
        scratch_shapes=[
            pltpu.VMEM((8, 128), F32),
            pltpu.VMEM(conv_weight.shape, BF16),
            pltpu.VMEM(down_weight.shape, BF16),
            pltpu.VMEM((512, 512), BF16),
            pltpu.VMEM((768, 512), BF16),
            pltpu.VMEM((4, 8, 128), F32),
            piece,
            piece,
            pltpu.VMEM((4, 192, 128), BF16),
            pltpu.VMEM((4, 192, 128), BF16),
            pltpu.VMEM((8, 64, WIDE), BF16),
            gathered,
            gathered,
            gathered,
            pltpu.VMEM((8, 16, 128), BF16),
            piece,
            pltpu.VMEM((4, 512, 128), BF16),
            pltpu.VMEM((4, 512, 128), BF16),
            full,
            full,
            pltpu.VMEM((8, 5, 2, 32, WIDE), BF16),
            pltpu.VMEM((3, 256, 384), BF16),
            pltpu.VMEM((3, 256, 128), BF16),
            pltpu.VMEM((10, 256, 128), F32),
            pltpu.VMEM((8, 4, 32, WIDE), BF16),
            pltpu.VMEM((3, 256, 384), BF16),
            wide,
            wide,
            wide,
            wide,
            pltpu.VMEM((8, 256, 256), BF16),
            pltpu.VMEM((8, 256, 128), BF16),
            wide,
            pltpu.SemaphoreType.DMA((8,)),
            pltpu.SemaphoreType.DMA((11, 8)),
            pltpu.SemaphoreType.DMA((11, 8)),
        ],
        compiler_params=pltpu.CompilerParams(
            collective_id=0, has_side_effects=True, vmem_limit_bytes=60 * 2**20
        ),
    )(
        clip_bucket,
        start_frame,
        bucket_res.T,
        video.reshape(256, WIDE),
        conv_weight,
        down_weight,
        out_grad,
        swap,
        column_pick(),
    )
    kinds = (sent, sent_down, full_cells, even_cells, stack, og_stack, swap)
    down, video_grad, conv_grad, down_grad = pl.pallas_call(
        finish_kernel,
        out_shape=(
            jax.ShapeDtypeStruct(out_grad.shape, BF16),
            jax.ShapeDtypeStruct((256, WIDE), BF16),
            jax.ShapeDtypeStruct(conv_weight.shape, F32),
            jax.ShapeDtypeStruct(down_weight.shape, F32),
        ),
        in_specs=[anywhere] * 7,
        out_specs=(vmem, vmem, anywhere, anywhere),
        scratch_shapes=[pltpu.VMEM(kind.shape, BF16) for kind in kinds]
        + [
            pltpu.VMEM(conv_weight.shape, F32),
            pltpu.VMEM(down_weight.shape, F32),
            pltpu.SemaphoreType.DMA((7,)),
            pltpu.SemaphoreType.DMA((12,)),
        ],
        compiler_params=pltpu.CompilerParams(vmem_limit_bytes=60 * 2**20),
    )(*parts, swap)
    return (down, video_grad.reshape(video.shape), conv_grad, down_grad)


def solution(mesh):
    placed = (
        P(("mix", "fsdp"), "tile", None, None, None),
        P(("mix", "fsdp"), None),
        P(("mix", "fsdp"), None),
        P(("mix", "fsdp"), "tile", None, None, None),
        P(("mix", "fsdp")),
        P(("mix", "fsdp")),
        P(),
    )
    return jax.shard_map(
        fused if mesh.shape["tile"] == 2 and mesh.shape["fsdp"] == 4 else shards,
        mesh=mesh,
        in_specs=placed,
        out_specs=(
            P(("mix", "fsdp"), "tile", None, None, None),
            P(("mix", "fsdp"), "tile", None, None, None),
            P(("mix", "fsdp"), None),
            P(("mix", "fsdp"), None),
        ),
        check_vma=False,
    )
```

```python
import functools

import jax
import jax.numpy as jnp
import numpy as np
from jax import lax
from jax.experimental import pallas as pl
from jax.experimental.pallas import tpu as pltpu
from jax.sharding import PartitionSpec as P

GROUPS = 32


EPSILON = 1e-06


def shifted(block, axis, distance):
    devices = range(lax.axis_size(axis))
    route = [(i - distance, i) for i in devices if i - distance in devices]
    return lax.ppermute(block, axis, route)


def valid_mask(clip_bucket, start_frame, bucket_res, first_frame, frame_count, side_cells):
    bucket_ids = jnp.arange(bucket_res.shape[0], dtype=jnp.int32)
    picked = (clip_bucket[:, None] == bucket_ids[None, :]).astype(jnp.int32)
    limits = jnp.sum(picked[:, :, None] * bucket_res[None, :, :], axis=1)
    frame_ids = first_frame + jnp.arange(frame_count, dtype=jnp.int32)
    positions = jnp.arange(side_cells, dtype=jnp.int32)
    in_time = frame_ids[None, :] >= start_frame[:, None]
    in_rows = positions[None, :] < limits[:, 0:1]
    in_cols = positions[None, :] < limits[:, 1:2]
    inside = in_time[:, :, None, None] & in_rows[:, None, :, None] & in_cols[:, None, None, :]
    return (inside.astype(jnp.float32)[..., None], limits)


def time_group(padded, tap_time, out_frames, side_cells, flipped):
    channel_count = padded.shape[-1]
    time_start = 2 - tap_time if flipped else tap_time
    layers = []
    for tap_row in range(3):
        for tap_col in range(3):
            row_start = 2 - tap_row if flipped else tap_row
            col_start = 2 - tap_col if flipped else tap_col
            window = padded[
                :,
                time_start : time_start + out_frames,
                row_start : row_start + side_cells,
                col_start : col_start + side_cells,
                :,
            ]
            layers.append(window.reshape(-1, channel_count))
    return jnp.stack(layers)


def stride_taps(padded, side_cells):
    channel_count = padded.shape[-1]
    layers = []
    for tap_row in range(3):
        for tap_col in range(3):
            window = padded[
                :, :, tap_row : tap_row + side_cells : 2, tap_col : tap_col + side_cells : 2, :
            ]
            layers.append(window.reshape(-1, channel_count))
    return jnp.stack(layers)


def weight_terms(grad_rows, slabs, cot_rows, hidden_padded, frame_count, side_cells):
    out_rows = grad_rows.shape[1]
    down_term = lax.dot_general(
        grad_rows, slabs, (((0,), (1,)), ((), ())), preferred_element_type=jnp.float32
    ).reshape(out_rows, -1)
    conv_parts = []
    for tap_time in range(3):
        group = time_group(hidden_padded, tap_time, frame_count, side_cells, False)
        conv_parts.append(
            lax.dot_general(
                cot_rows, group, (((0,), (1,)), ((), ())), preferred_element_type=jnp.float32
            )
        )
    conv_term = jnp.concatenate(conv_parts, axis=1).reshape(out_rows, -1)
    return (conv_term, down_term)


def transpose_conv(grad_padded, conv_weight, out_frames, side_cells):
    channel_count = grad_padded.shape[-1]
    row_total = grad_padded.shape[0] * out_frames * side_cells * side_cells
    initial = jnp.zeros((row_total, channel_count), jnp.float32)
    running = initial
    weight_panel = lax.all_gather(conv_weight, "fsdp", axis=0, tiled=True)
    panel_rows = weight_panel.shape[0]
    panel = weight_panel.reshape(panel_rows, 27, channel_count)
    for tap_time in range(3):
        group = time_group(grad_padded, tap_time, out_frames, side_cells, True)
        running = running + lax.dot_general(
            group,
            panel[:, 9 * tap_time : 9 * tap_time + 9, :],
            (((0, 2), (1, 0)), ((), ())),
            preferred_element_type=jnp.float32,
        )
    return running


def shards(video, conv_weight, down_weight, out_grad, clip_bucket, start_frame, bucket_res):
    clip_count, frame_count, side_cells, side_again, channel_count = video.shape
    half_side = side_cells // 2
    group_width = channel_count // GROUPS
    tiles = lax.axis_size("tile")
    mask, limits = valid_mask(
        clip_bucket,
        start_frame,
        bucket_res,
        lax.axis_index("tile") * frame_count,
        frame_count,
        side_cells,
    )
    valid_count = (
        (frame_count * tiles - start_frame) * limits[:, 0] * limits[:, 1] * group_width
    ).astype(jnp.float32)
    grouped_shape = (clip_count, frame_count, side_cells, side_cells, GROUPS, group_width)
    summed_axes = (1, 2, 3, 5)
    cell_weight = mask[..., None]
    grouped = video.astype(jnp.float32).reshape(grouped_shape)
    first_sum = lax.psum(jnp.sum(grouped * cell_weight, axis=summed_axes), "tile")
    centre = first_sum / valid_count[:, None]
    offset = grouped - centre[:, None, None, None, :, None]
    second_sum = lax.psum(jnp.sum(cell_weight * offset * offset, axis=summed_axes), "tile")
    spread = second_sum / valid_count[:, None]
    inverse = lax.rsqrt(spread + EPSILON)
    normed_grouped = offset * inverse[:, None, None, None, :, None]
    normed = normed_grouped.reshape(video.shape)
    hidden = (mask * jax.nn.silu(normed)).astype(jnp.bfloat16)
    past = shifted(hidden[:, frame_count - 2 :], "tile", 1)
    hidden_padded = jnp.pad(
        jnp.concatenate([past, hidden], axis=1), ((0, 0), (0, 0), (1, 1), (1, 1), (0, 0))
    )

    def conv_columns(weight_panel):
        panel = weight_panel.reshape(weight_panel.shape[0], 27, channel_count)
        summed = None
        for tap_time in range(3):
            group = time_group(hidden_padded, tap_time, frame_count, side_cells, False)
            term = lax.dot_general(
                group,
                panel[:, 9 * tap_time : 9 * tap_time + 9, :],
                (((0, 2), (1, 2)), ((), ())),
                preferred_element_type=jnp.float32,
            )
            summed = term if summed is None else summed + term
        return summed

    conv_out = conv_columns(lax.all_gather(conv_weight, "fsdp", axis=0, tiled=True))
    residual = (mask * (video.astype(jnp.float32) + conv_out.reshape(video.shape))).astype(
        jnp.bfloat16
    )
    down_slabs = stride_taps(
        jnp.pad(residual, ((0, 0), (0, 0), (0, 1), (0, 1), (0, 0))), side_cells
    )
    weight_panel = lax.all_gather(down_weight, "fsdp", axis=0, tiled=True)
    panel = weight_panel.reshape(weight_panel.shape[0], 9, channel_count)
    down_out = lax.dot_general(
        down_slabs, panel, (((0, 2), (1, 2)), ((), ())), preferred_element_type=jnp.float32
    )
    down = down_out.astype(jnp.bfloat16).reshape(
        clip_count, frame_count, half_side, half_side, channel_count
    )
    grad_flat = out_grad.reshape(-1, channel_count)
    weight_panel = lax.all_gather(down_weight, "fsdp", axis=0, tiled=True)
    panel_rows = weight_panel.shape[0]
    panel = weight_panel.reshape(panel_rows, 9, channel_count)
    tap_grads = lax.dot_general(
        grad_flat, panel, (((1,), (0,)), ((), ())), preferred_element_type=jnp.float32
    )
    spread_back = jnp.zeros(
        (clip_count, frame_count, side_cells + 1, side_cells + 1, channel_count), jnp.float32
    )
    for tap_row in range(3):
        for tap_col in range(3):
            term = tap_grads[:, tap_row * 3 + tap_col, :].reshape(
                clip_count, frame_count, half_side, half_side, channel_count
            )
            spread_back = spread_back.at[
                :, :, tap_row : tap_row + side_cells : 2, tap_col : tap_col + side_cells : 2, :
            ].add(term)
    res_grad = (mask * spread_back[:, :, :side_cells, :side_cells, :]).astype(jnp.bfloat16)
    res_flat = res_grad.reshape(-1, channel_count)
    later = shifted(res_grad[:, :2], "tile", -1)
    grad_padded = jnp.pad(
        jnp.concatenate([res_grad, later], axis=1), ((0, 0), (0, 0), (1, 1), (1, 1), (0, 0))
    )
    back_hidden = transpose_conv(grad_padded, conv_weight, frame_count, side_cells).reshape(
        video.shape
    )
    gate_value = jax.nn.sigmoid(normed)
    pushed = mask * back_hidden * gate_value * (1.0 + normed * (1.0 - gate_value))
    pushed_grouped = pushed.reshape(grouped_shape)
    push_sum, pair_sum = lax.psum(
        (
            jnp.sum(pushed_grouped, axis=summed_axes),
            jnp.sum(pushed_grouped * normed_grouped, axis=summed_axes),
        ),
        "tile",
    )
    mean_push = push_sum / valid_count[:, None]
    mean_pair = pair_sum / valid_count[:, None]
    through_norm = inverse[:, None, None, None, :, None] * (
        pushed_grouped
        - mean_push[:, None, None, None, :, None]
        - normed_grouped * mean_pair[:, None, None, None, :, None]
    )
    video_grad = (mask * through_norm.reshape(video.shape) + res_grad.astype(jnp.float32)).astype(
        jnp.bfloat16
    )
    conv_term, down_term = weight_terms(
        grad_flat, down_slabs, res_flat, hidden_padded, frame_count, side_cells
    )
    conv_share, down_share = (
        lax.psum_scatter(conv_term, ("fsdp", "tile"), scatter_dimension=0, tiled=True),
        lax.psum_scatter(down_term, ("fsdp", "tile"), scatter_dimension=0, tiled=True),
    )
    conv_weight_grad, down_weight_grad = (
        lax.all_gather(conv_share, "tile", axis=0, tiled=True),
        lax.all_gather(down_share, "tile", axis=0, tiled=True),
    )
    return (down, video_grad, conv_weight_grad, down_weight_grad)


F32 = jnp.float32
BF16 = jnp.bfloat16
MESH = pl.DeviceIdType.MESH
WIDE = 256
OWN = 32


def lane_swap():
    lane = np.arange(512)
    outer, inner, channel = lane // 128, lane // 32 % 4, lane % 32
    table = np.zeros((512, 512), np.float32)
    table[lane, inner * 128 + outer * 32 + channel] = 1.0
    return jnp.asarray(table, BF16)


def column_pick():
    table = np.zeros((2, 3, 256, 4, 4, 32), np.float32)
    for core in range(2):
        for tap in range(3):
            for chip in range(4):
                for channel in range(32):
                    table[core, tap, 64 * chip + 32 * core + channel, chip, tap, channel] = 1.0
    return jnp.asarray(table.reshape(2, 768, 512), BF16)


def dot(lhs, rhs):
    return jnp.dot(lhs, rhs, preferred_element_type=F32)


def move_cols(block, distance):
    if distance == 0:
        return block
    rows = block.shape[0]
    col = (lax.broadcasted_iota(jnp.int32, block.shape, 0) & 7) + distance
    turned = pltpu.roll(block, (-distance) % rows, 0)
    return jnp.where((col >= 0) & (col < 8), turned, 0.0)


def fold_taps(result, outer, distances):
    parts = result.reshape(outer, 4, 8, 128)
    place = lax.broadcasted_iota(jnp.int32, (outer * 8, 128), 1) >> 5
    total = None
    for tap in range(3):
        layer = jnp.zeros((outer * 8, 128), F32)
        for clip in range(4):
            block = parts[:, clip].reshape(outer * 8, 128)
            turn = (OWN * (clip - tap)) % 128
            if turn:
                block = pltpu.roll(block, turn, 1)
            layer = jnp.where(place == clip, block, layer)
        layer = move_cols(layer, distances[tap])
        total = layer if total is None else total + layer
    return total


def group_total(row):
    first = lax.broadcasted_iota(jnp.int32, (128, 128), 0) >> 3
    second = lax.broadcasted_iota(jnp.int32, (128, 128), 1) >> 3
    same = (first == second).astype(F32)
    wide = jnp.broadcast_to(row, (8, 128))
    return jnp.dot(wide, same, preferred_element_type=F32, precision=lax.Precision.HIGHEST)[0:1]


def gathered_lanes(pieces, swap):
    halves = [
        dot(jnp.concatenate(pieces[4 * half : 4 * half + 4], axis=1), swap) for half in range(2)
    ]
    return [
        jnp.concatenate([half[:, 128 * p : 128 * p + 128] for half in halves], axis=1)
        for p in range(4)
    ]


def block_kernel(
    bucket_ref, start_ref, res_table_ref, video_ref, cw_hbm, dw_hbm, og_ref, swap_hbm,
    pick_hbm,
    x_all, d_all, h_out, r_out, stack_out, og_stack_out,
    meta_ref, cw_ref, dw_ref, swap_ref, pick_ref,
    meta_all, v_send, v_all, w_send, w_all, og_all, h_all, g_all, r_all, d_send,
    x_send, p_send, p_all, h_full, g_full, r_full, rows_back, rows_down, sums, og_up, rows_fwd, cells, normed_ref, mask_ref,
    res_ref, stack_t, og_stack_t, back_ref, load_sems, send_sems, recv_sems,
):
    chip = lax.axis_index("fsdp")
    core = lax.axis_index("tile")
    me = chip * 2 + core
    sibling = chip * 2 + (1 - core)

    def peer(index):
        return {"fsdp": index // 2, "tile": index % 2}

    loads = {}
    for index, (name, source, target) in enumerate(
        (
            ("swap", swap_hbm, swap_ref),
            ("dw", dw_hbm, dw_ref),
            ("pick", pick_hbm.at[core], pick_ref),
            ("cw", cw_hbm, cw_ref),
        )
    ):
        loads[name] = pltpu.make_async_copy(source, target, load_sems.at[index])
        loads[name].start()

    barrier = pltpu.get_barrier_semaphore()
    for step in range(1, 8):
        pl.semaphore_signal(barrier, inc=1, device_id=peer((me + step) % 8), device_id_type=MESH)
    pl.semaphore_wait(barrier, 7)

    def send(phase, step, src, dst, to):
        copy = pltpu.make_async_remote_copy(
            src_ref=src, dst_ref=dst, send_sem=send_sems.at[phase, step],
            recv_sem=recv_sems.at[phase, step], device_id=peer(to), device_id_type=MESH,
        )
        copy.start()
        return copy

    def send_all(phase, source, target):
        return [send(phase, s, source((me + s) % 8), target, (me + s) % 8) for s in range(1, 8)]

    def spread_out(phase, target, part):
        block = target.at[me, part]
        copies = [send(phase, 4, block, block, sibling)]
        for s in range(1, 4):
            copies.append(send(phase, s, block, block, ((chip + s) % 4) * 2 + core))
        return copies

    def relay(phase, target, part, copies):
        passed = []
        for s in range(1, 4):
            copies[s].wait_recv()
            block = target.at[((chip + 4 - s) % 4) * 2 + core, part]
            passed.append(send(phase, 4 + s, block, block, sibling))
        copies.extend(passed)

    early, late = pl.ds(0, 256), pl.ds(256, 256)

    def complete(copies):
        copies[0].wait_recv()
        for copy in copies[4:]:
            copy.wait_recv()

    def arrived(copies):
        for copy in copies:
            copy.wait_recv()

    bucket = bucket_ref[0]
    high, width = jnp.int32(0), jnp.int32(0)
    for index in range(res_table_ref.shape[1]):
        high = high + jnp.where(bucket == index, res_table_ref[0, index], 0)
        width = width + jnp.where(bucket == index, res_table_ref[1, index], 0)
    line = lax.broadcasted_iota(jnp.int32, (8, 128), 0)
    facts = jnp.where(line == 0, start_ref[0], jnp.where(line == 1, high, width)).astype(F32)
    meta_ref[...] = facts
    meta_all[chip] = facts
    meta_copies = [
        send(3, s, meta_ref, meta_all.at[chip], ((chip + s) % 4) * 2 + core) for s in range(1, 4)
    ]
    loads["swap"].wait()
    halves = []
    for half in range(2):
        halves.append(
            jnp.concatenate(
                [video_ref[64 * t : 64 * t + 64, 128 * half : 128 * half + 128] for t in range(4)],
                axis=1,
            )
        )
    packed = dot(jnp.concatenate(halves, axis=0), swap_ref[...]).astype(BF16)
    for index in range(8):
        half, quarter = index // 4, index % 4
        v_send[index] = packed[64 * half : 64 * half + 64, 128 * quarter : 128 * quarter + 128]
    v_copies = send_all(0, lambda to: v_send.at[to], v_all.at[me])
    v_all[me] = v_send[me]
    og_all[me] = og_ref[0].astype(F32).reshape(64, WIDE).astype(BF16)
    og_copies = spread_out(1, og_all, pl.ds(0, 64))

    loads["dw"].wait()
    loads["pick"].wait()

    picks = None
    for tap in range(3):
        at = [(3 * b + tap) * WIDE for b in range(3)]
        rows = jnp.concatenate([dw_ref[:, low : low + WIDE] for low in at], axis=0)
        term = dot(rows, pick_ref[256 * tap : 256 * tap + 256, :])
        picks = term if picks is None else picks + term
    for other in range(4):
        w_send[other] = picks[:, 128 * other : 128 * other + 128].astype(BF16)
    w_all[chip] = w_send[chip]
    dw_copies = []
    for s in range(1, 4):
        to = (chip + s) % 4
        dw_copies.append(send(2, s, w_send.at[to], w_all.at[chip], to * 2 + core))

    loads["cw"].wait()
    from_row = lax.broadcasted_iota(jnp.int32, (WIDE, 128), 0)
    to_lane = lax.broadcasted_iota(jnp.int32, (WIDE, 128), 1)
    chosen = from_row == (to_lane >> 5) * 64 + OWN * core + (to_lane & 31)
    chosen = chosen.astype(F32).astype(BF16)
    for ab in range(9):
        at = [(3 * ab + tap) * WIDE for tap in range(3)]
        rows = jnp.concatenate([cw_ref[:, low : low + WIDE] for low in at], axis=0)
        low = 128 * (ab // 3)
        rows_back[ab % 3, 0:192, low : low + 128] = dot(rows, chosen).astype(BF16)
        rows_back[ab % 3, 192:256, low : low + 128] = jnp.zeros((64, 128), BF16)

    mine = pl.ds(pl.multiple_of(core * OWN, OWN), OWN)
    blank = jnp.zeros((32, WIDE), BF16)

    def turned(ref, block):
        rows = [ref[mine, (3 * block + c) * WIDE : (3 * block + c + 1) * WIDE] for c in range(3)]
        return jnp.concatenate(rows + [blank], axis=0).T

    for ab in range(9):
        low = 128 * (ab // 3)
        rows_fwd[ab % 3, :, low : low + 128] = turned(cw_ref, ab)
    for b in range(3):
        rows_down[b] = turned(dw_ref, b)

    sums[...] = jnp.zeros((10, 256, 128), F32)
    edge = jnp.zeros((10, 32, WIDE), BF16)
    for t in range(2):
        h_full[t] = edge
        g_full[8 + t] = edge
    for t in range(8):
        for full, off in ((h_full, 2), (g_full, 0)):
            full[t + off, 0] = jnp.zeros((32, WIDE), BF16)
            full[t + off, 9] = jnp.zeros((32, WIDE), BF16)
        r_full[t, 4, 0] = jnp.zeros((32, WIDE), BF16)

    arrived(meta_copies)
    place1 = lax.broadcasted_iota(jnp.int32, (1, 128), 1) >> 5
    start = jnp.zeros((1, 128), F32)
    high = jnp.zeros((1, 128), F32)
    width = jnp.zeros((1, 128), F32)
    for clip in range(4):
        start = jnp.where(place1 == clip, meta_all[clip, 0:1, :], start)
        high = jnp.where(place1 == clip, meta_all[clip, 1:2, :], high)
        width = jnp.where(place1 == clip, meta_all[clip, 2:3, :], width)
    count = (8.0 - start) * high * width * 8.0
    row_id = lax.broadcasted_iota(jnp.int32, (512, 128), 0)
    in_time = (row_id >> 6).astype(F32) >= start
    in_rows = ((row_id >> 3) & 7).astype(F32) < high
    in_cols = (row_id & 7).astype(F32) < width
    mask_ref[...] = jnp.where(in_time & in_rows & in_cols, 1.0, 0.0)

    arrived(v_copies)
    relay(1, og_all, pl.ds(0, 64), og_copies)
    stacked = jnp.concatenate(
        [
            jnp.concatenate([v_all[2 * other + c] for other in range(4)], axis=1)
            for c in range(2)
        ],
        axis=0,
    )
    unpacked = dot(stacked, swap_ref[...])
    for t in range(8):
        c, q = t // 4, t % 4
        cells[64 * t : 64 * t + 64, :] = unpacked[64 * c : 64 * c + 64, 128 * q : 128 * q + 128]
    mask = mask_ref[...]
    centre = group_total(jnp.sum(mask * cells[...], axis=0, keepdims=True)) / count
    offset = cells[...] - centre
    spread = group_total(jnp.sum(mask * offset * offset, axis=0, keepdims=True)) / count
    inverse = lax.rsqrt(spread + EPSILON)
    normed = offset * inverse
    normed_ref[...] = normed
    h_all[me] = (mask * (normed / (1.0 + jnp.exp(-normed)))).astype(BF16)
    h_copies = spread_out(4, h_all, early)
    h_late = spread_out(11, h_all, late)

    complete(og_copies)
    up_row = lax.broadcasted_iota(jnp.int32, (128, 64), 0)
    up_col = lax.broadcasted_iota(jnp.int32, (128, 64), 1)
    lift = ((up_row >> 3 == up_col >> 2) & ((up_row & 7) == 2 * (up_col & 3))).astype(F32).astype(BF16)
    for c in range(2):
        raised = [dot(lift, og_all[2 * clip + c]).reshape(16, 8, WIDE) for clip in range(4)]
        og_up[4 * c : 4 * c + 4] = (
            jnp.concatenate(raised, axis=1).astype(BF16).reshape(4, 4, 32, WIDE)
        )
    arrived(dw_copies)

    def res_grad_frame(t, carry):
        lhs = og_up[t].reshape(128, WIDE)
        layers = []
        for b in range(3):
            panel = w_all[:, 64 * b : 64 * b + 64, :].reshape(256, 128)
            layers.append(fold_taps(dot(lhs, panel), 4, (0, -1, -2)).reshape(4, 8, 128))
        even = layers[0] + jnp.concatenate([jnp.zeros((1, 8, 128), F32), layers[2][:3]], axis=0)
        both = jnp.stack([even, layers[1]], axis=1).reshape(64, 128)
        at = pl.ds(pl.multiple_of(64 * t, 64), 64)
        value = (mask_ref[at, :] * both).astype(BF16)
        g_all[me, at, :] = value
        wide = value.astype(F32)
        res_ref[at, :] = wide
        return carry

    lax.fori_loop(0, 8, res_grad_frame, 0)
    g_copies = [send(5, 0, g_all.at[me], g_all.at[me], sibling)]

    def keep(index, source, target):
        copy = pltpu.make_async_copy(source, target, load_sems.at[index])
        copy.start()
        return copy

    kept = []

    from_row = lax.broadcasted_iota(jnp.int32, (WIDE, WIDE), 0)
    to_lane = lax.broadcasted_iota(jnp.int32, (WIDE, WIDE), 1)
    own_rows = (from_row == (to_lane & 63) + 64 * chip).astype(F32).astype(BF16)

    def og_frame(t, carry):
        rows = dot(og_up[t].reshape(128, WIDE), own_rows)
        tap = lax.broadcasted_iota(jnp.int32, (128, WIDE), 1) >> 6
        once, twice = move_cols(rows, -1), move_cols(rows, -2)
        rows = jnp.where(tap == 0, rows, jnp.where(tap == 1, once, twice))
        og_stack_t[t] = rows.T.astype(BF16)
        return carry

    lax.fori_loop(0, 8, og_frame, 0)

    kept.append(keep(4, og_stack_t, og_stack_out))
    arrived(g_copies)
    place = lax.broadcasted_iota(jnp.int32, (64, 128), 1) >> 5

    def stack_frame(t, carry):
        at = pl.ds(pl.multiple_of(64 * t, 64), 64)
        moved = []
        for c in range(2):
            block = g_all[2 * chip + c, at, :].astype(F32)
            moved.append([move_cols(block, 1 - tap) for tap in range(3)])
        split = []
        for clip in range(4):
            sides = [jnp.zeros((64, 128), F32)] * 2
            for tap in range(3):
                for c in range(2):
                    spot = 2 * (tap % 2) + c
                    turn = (OWN * (spot - clip)) % 128
                    block = moved[c][tap]
                    if turn:
                        block = pltpu.roll(block, turn, 1)
                    sides[tap // 2] = jnp.where(place == spot, block, sides[tap // 2])
            split.append(jnp.concatenate(sides, axis=1).reshape(8, 8, WIDE))
        rows = jnp.concatenate(split, axis=1).reshape(256, WIDE)
        g_full[t, 1:9] = rows.astype(BF16).reshape(8, 32, WIDE)
        return carry

    lax.fori_loop(0, 8, stack_frame, 0)

    def three_taps(u, full, weights, shift, row_of):
        total = None
        for b in range(3):
            low = row_of(b)
            window = full[pl.ds(2 * u + shift, 2), low : low + 8].reshape(512, WIDE)
            term = dot(window, weights[b])
            total = term if total is None else total + term
        return [
            total[:, 128 * a : 128 * a + 128].reshape(2, 256, 128) for a in range(3)
        ]

    def back_pair(u, carry):
        parts = three_taps(u, g_full, rows_back, 0, lambda b: 2 - b)
        for a in range(3):
            at = pl.ds(2 * u + a, 2)
            sums[at] = sums[at] + parts[a]
        return carry

    def back_frame(t, carry):
        total = sums[t + 2]
        parts = total.reshape(8, 4, 8, 128)
        at = pl.ds(pl.multiple_of(64 * t, 64), 64)
        own = jnp.zeros((64, 128), F32)
        for other in range(4):
            piece = jnp.zeros((64, 128), F32)
            for clip in range(4):
                block = parts[:, clip].reshape(64, 128)
                turn = (OWN * (clip - other)) % 128
                if turn:
                    block = pltpu.roll(block, turn, 1)
                piece = jnp.where(place == clip, block, piece)
            p_send[other, at, :] = piece.astype(BF16)
            own = jnp.where(chip == other, piece, own)
        back_ref[at, :] = own
        return carry

    lax.fori_loop(0, 4, back_pair, 0)
    relay(4, h_all, early, h_copies)
    lax.fori_loop(0, 8, back_frame, 0)
    relay(11, h_all, late, h_late)
    p_copies = []
    for s in range(1, 4):
        to = (chip + s) % 4
        p_copies.append(send(10, s, p_send.at[to], p_all.at[s], to * 2 + core))

    def assemble(source, t):
        at = pl.ds(pl.multiple_of(256 * t, 256), 256)
        clips = gathered_lanes([source[d, at, :] for d in range(8)], swap_ref[...])
        blocks = [clip.reshape(32, 8, WIDE) for clip in clips]
        return jnp.concatenate(blocks, axis=1).astype(BF16).reshape(4, 8, 32, WIDE)


    def fill_hidden(t, carry):
        h_full[pl.ds(4 * t + 2, 4), 1:9] = assemble(h_all, t)
        return carry


    def conv_pair(u, carry):
        parts = three_taps(u, h_full, rows_fwd, 2, lambda b: b)
        for a in range(3):
            at = pl.ds(2 * u + 2 - a, 2)
            sums[at] = sums[at] + parts[a]
        return carry

    def conv_frame(t, carry):
        total = sums[t]
        folded = fold_taps(total, 8, (-1, 0, 1))
        at = pl.ds(pl.multiple_of(64 * t, 64), 64)
        r_all[me, at, :] = (mask_ref[at, :] * (cells[at, :] + folded)).astype(BF16)
        return carry

    sums[...] = jnp.zeros((10, 256, 128), F32)
    complete(h_copies)
    fill_hidden(0, 0)
    lax.fori_loop(0, 2, conv_pair, 0)
    lax.fori_loop(0, 4, conv_frame, 0)
    r_copies = spread_out(6, r_all, early)
    complete(h_late)
    fill_hidden(1, 0)
    kept.append(keep(5, h_full, h_out))
    lax.fori_loop(2, 4, conv_pair, 0)
    lax.fori_loop(4, 8, conv_frame, 0)
    r_late = spread_out(12, r_all, late)

    arrived(p_copies)
    relay(6, r_all, early, r_copies)
    mask = mask_ref[...]
    normed = normed_ref[...]
    gate = 1.0 / (1.0 + jnp.exp(-normed))
    back = back_ref[...]
    for s in range(1, 4):
        back = back + p_all[s].astype(F32)
    pushed = mask * back * gate * (1.0 + normed * (1.0 - gate))
    mean_push = group_total(jnp.sum(pushed, axis=0, keepdims=True)) / count
    mean_pair = group_total(jnp.sum(pushed * normed, axis=0, keepdims=True)) / count
    through = inverse * (pushed - mean_push - normed * mean_pair)
    back_ref[...] = mask * through + res_ref[...]
    for c in range(2):
        quarter = [back_ref[64 * (4 * c + q) : 64 * (4 * c + q) + 64, :] for q in range(4)]
        swapped = dot(jnp.concatenate(quarter, axis=1).astype(BF16), swap_ref[...]).astype(BF16)
        for other in range(4):
            x_send[2 * other + c] = swapped[:, 128 * other : 128 * other + 128]
    x_all[me] = x_send[me]
    x_copies = send_all(8, lambda to: x_send.at[to], x_all.at[me])

    relay(12, r_all, late, r_late)

    def turn_frame(t, carry):
        stack_t[t] = g_full[t, 1:9].reshape(256, WIDE).T
        return carry

    lax.fori_loop(0, 4, turn_frame, 0)

    def fill_residual(t, carry):
        r_full[pl.ds(4 * t, 4), 0:4] = assemble(r_all, t).reshape(4, 4, 2, 32, WIDE)
        return carry

    def down_frame(t, carry):
        total = None
        for b in range(3):
            window = r_full[t, b // 2 : b // 2 + 4, b % 2].reshape(128, WIDE)
            term = dot(window, rows_down[b])
            total = term if total is None else total + term
        folded = fold_taps(total, 4, (0, 1, 2)).astype(BF16)
        to_row = lax.broadcasted_iota(jnp.int32, (16, 32), 0)
        from_row = lax.broadcasted_iota(jnp.int32, (16, 32), 1)
        even = (from_row == to_row * 2).astype(F32).astype(BF16)
        d_send[t] = dot(even, folded).astype(BF16)
        return carry


    def frames_of(to):
        return pl.ds(4 * (to % 2), 4)

    complete(r_copies)
    fill_residual(0, 0)
    lax.fori_loop(0, 4, down_frame, 0)
    complete(r_late)
    fill_residual(1, 0)
    kept.append(keep(7, r_full, r_out))
    lax.fori_loop(4, 8, down_frame, 0)
    d_all[me] = d_send[frames_of(me)]
    d_copies = send_all(7, lambda to: d_send.at[frames_of(to)], d_all.at[me])
    lax.fori_loop(4, 8, turn_frame, 0)
    kept.append(keep(6, stack_t, stack_out))

    arrived(x_copies)
    arrived(d_copies)
    for copy in kept:
        copy.wait()
    for copies in (
        meta_copies, v_copies, og_copies, dw_copies, p_copies, h_copies, h_late, g_copies, r_copies, r_late, x_copies,
        d_copies,
    ):
        for copy in copies:
            copy.wait_send()


def finish_kernel(
    x_hbm, d_hbm, h_hbm, r_hbm, stack_hbm, og_stack_hbm, swap_hbm,
    down_ref, vgrad_ref, cgrad_hbm, dgrad_hbm,
    x_all, d_all, h_full, r_full, stack_t, og_stack_t, swap_ref, cgrad_ref, dgrad_ref,
    load_sems, store_sems,
):
    chip = lax.axis_index("fsdp")
    loads = []
    for index, (source, target) in enumerate(
        (
            (swap_hbm, swap_ref),
            (x_hbm, x_all),
            (d_hbm, d_all),
            (stack_hbm, stack_t),
            (h_hbm, h_full),
            (og_stack_hbm, og_stack_t),
            (r_hbm, r_full),
        )
    ):
        loads.append(pltpu.make_async_copy(source, target, load_sems.at[index]))
        loads[-1].start()
    for copy in loads[:3]:
        copy.wait()
    frames = gathered_lanes([x_all[d] for d in range(8)], swap_ref[...])
    for t, block in enumerate(frames):
        vgrad_ref[64 * t : 64 * t + 64, :] = block.astype(BF16)
    clips = gathered_lanes([d_all[d].reshape(64, 128) for d in range(8)], swap_ref[...])
    own = clips[0]
    for clip in range(1, 4):
        own = jnp.where(chip == clip, clips[clip], own)
    down_ref[0] = own.reshape(4, 4, 4, WIDE).astype(BF16)

    stores = []

    def put(grad, ref, hbm, block, index):
        for tap in range(3):
            at = (3 * block + tap) * WIDE
            ref[:, at : at + WIDE] = grad[64 * tap : 64 * tap + 64]
        part = pl.ds(3 * block * WIDE, 3 * WIDE)
        stores.append(pltpu.make_async_copy(ref.at[:, part], hbm.at[:, part], store_sems.at[index]))
        stores[-1].start()

    loads[3].wait()
    loads[4].wait()
    lhs = jnp.concatenate([stack_t[t, 0:192] for t in range(8)], axis=1)
    for a in range(3):
        for b in range(3):
            rhs = h_full[a : a + 8, b : b + 8].reshape(2048, WIDE)
            put(dot(lhs, rhs), cgrad_ref, cgrad_hbm, 3 * a + b, 3 * a + b)
    loads[5].wait()
    loads[6].wait()
    lhs = jnp.concatenate([og_stack_t[t, 0:192] for t in range(8)], axis=1)
    for b in range(3):
        rhs = r_full[:, b // 2 : b // 2 + 4, b % 2].reshape(1024, WIDE)
        put(dot(lhs, rhs), dgrad_ref, dgrad_hbm, b, 9 + b)
    for copy in stores:
        copy.wait()


def fused(video, conv_weight, down_weight, out_grad, clip_bucket, start_frame, bucket_res):
    vmem = pl.BlockSpec(memory_space=pltpu.VMEM)
    smem = pl.BlockSpec(memory_space=pltpu.SMEM)
    anywhere = pl.BlockSpec(memory_space=pl.ANY)
    full = pltpu.VMEM((10, 10, 32, WIDE), BF16)
    gathered = pltpu.VMEM((8, 512, 128), BF16)
    wide = pltpu.VMEM((512, 128), F32)
    piece = pltpu.VMEM((8, 64, 128), BF16)
    sent = jax.ShapeDtypeStruct((8, 64, 128), BF16)
    sent_down = jax.ShapeDtypeStruct((8, 4, 16, 128), BF16)
    full_cells = jax.ShapeDtypeStruct((10, 10, 32, WIDE), BF16)
    even_cells = jax.ShapeDtypeStruct((8, 5, 2, 32, WIDE), BF16)
    stack = jax.ShapeDtypeStruct((8, 256, 256), BF16)
    og_stack = jax.ShapeDtypeStruct((8, 256, 128), BF16)
    swap = lane_swap()
    parts = pl.pallas_call(
        block_kernel,
        out_shape=(sent, sent_down, full_cells, even_cells, stack, og_stack),
        in_specs=[smem] * 3 + [vmem, anywhere, anywhere, vmem] + [anywhere] * 2,
        out_specs=(vmem,) * 2 + (anywhere,) * 4,
        scratch_shapes=[
            pltpu.VMEM((8, 128), F32),
            pltpu.VMEM(conv_weight.shape, BF16),
            pltpu.VMEM(down_weight.shape, BF16),
            pltpu.VMEM((512, 512), BF16),
            pltpu.VMEM((768, 512), BF16),
            pltpu.VMEM((4, 8, 128), F32),
            piece,
            piece,
            pltpu.VMEM((4, 192, 128), BF16),
            pltpu.VMEM((4, 192, 128), BF16),
            pltpu.VMEM((8, 64, WIDE), BF16),
            gathered,
            gathered,
            gathered,
            pltpu.VMEM((8, 16, 128), BF16),
            piece,
            pltpu.VMEM((4, 512, 128), BF16),
            pltpu.VMEM((4, 512, 128), BF16),
            full,
            full,
            pltpu.VMEM((8, 5, 2, 32, WIDE), BF16),
            pltpu.VMEM((3, 256, 384), BF16),
            pltpu.VMEM((3, 256, 128), BF16),
            pltpu.VMEM((10, 256, 128), F32),
            pltpu.VMEM((8, 4, 32, WIDE), BF16),
            pltpu.VMEM((3, 256, 384), BF16),
            wide,
            wide,
            wide,
            wide,
            pltpu.VMEM((8, 256, 256), BF16),
            pltpu.VMEM((8, 256, 128), BF16),
            wide,
            pltpu.SemaphoreType.DMA((8,)),
            pltpu.SemaphoreType.DMA((13, 8)),
            pltpu.SemaphoreType.DMA((13, 8)),
        ],
        compiler_params=pltpu.CompilerParams(
            collective_id=0, has_side_effects=True, vmem_limit_bytes=60 * 2**20
        ),
    )(
        clip_bucket,
        start_frame,
        bucket_res.T,
        video.reshape(256, WIDE),
        conv_weight,
        down_weight,
        out_grad,
        swap,
        column_pick(),
    )
    kinds = (sent, sent_down, full_cells, even_cells, stack, og_stack, swap)
    down, video_grad, conv_grad, down_grad = pl.pallas_call(
        finish_kernel,
        out_shape=(
            jax.ShapeDtypeStruct(out_grad.shape, BF16),
            jax.ShapeDtypeStruct((256, WIDE), BF16),
            jax.ShapeDtypeStruct(conv_weight.shape, F32),
            jax.ShapeDtypeStruct(down_weight.shape, F32),
        ),
        in_specs=[anywhere] * 7,
        out_specs=(vmem, vmem, anywhere, anywhere),
        scratch_shapes=[pltpu.VMEM(kind.shape, BF16) for kind in kinds]
        + [
            pltpu.VMEM(conv_weight.shape, F32),
            pltpu.VMEM(down_weight.shape, F32),
            pltpu.SemaphoreType.DMA((7,)),
            pltpu.SemaphoreType.DMA((12,)),
        ],
        compiler_params=pltpu.CompilerParams(vmem_limit_bytes=60 * 2**20),
    )(*parts, swap)
    return (down, video_grad.reshape(video.shape), conv_grad, down_grad)


def solution(mesh):
    placed = (
        P(("mix", "fsdp"), "tile", None, None, None),
        P(("mix", "fsdp"), None),
        P(("mix", "fsdp"), None),
        P(("mix", "fsdp"), "tile", None, None, None),
        P(("mix", "fsdp")),
        P(("mix", "fsdp")),
        P(),
    )
    return jax.shard_map(
        fused if mesh.shape["tile"] == 2 and mesh.shape["fsdp"] == 4 else shards,
        mesh=mesh,
        in_specs=placed,
        out_specs=(
            P(("mix", "fsdp"), "tile", None, None, None),
            P(("mix", "fsdp"), "tile", None, None, None),
            P(("mix", "fsdp"), None),
            P(("mix", "fsdp"), None),
        ),
        check_vma=False,
    )
```
